32 devices in a mesh: owner: 8 (over z, x), view: 4 (over y, core).
Axes of the slice: x: 2, y: 2, z: 4, core: 2. Of those that a mesh axis runs over, the one named last changes fastest.
Arguments:
- estimate: float32 [128, 128, 128], P('owner'), may hold values from 0.5 to 2
- axial_views: float32 [4, 128, 128, 128], P('view', 'owner'), may hold values from 0.3 to 3
- lateral_views: float32 [4, 128, 128, 128], P('view', 'owner'), may hold values from 0.3 to 3
- psf_axial: float32 [4, 3, 33], P('view'), may hold values from 0.05 to 1
- psf_lateral: float32 [4, 3, 33], P('view'), may hold values from 0.05 to 1
- coverage: int32 [8, 4, 8], P('owner'), may hold values from 0 to 1, as said below
Outputs:
- deconvolved: float32 [128, 128, 128], P('owner')
The draws below stay inside these ranges and needn't reach their ends.
Inputs may be any that keep to these rules, and one draw needn't show every extreme that they name: `coverage`: each block is covered by 2 to 6 views; some block by exactly 6 and some by exactly 2.
All inputs are finite; a program needn't handle non-finite values.
Results may differ from the reference program's by a relative error of at most 0.0001.
Values sent between devices are 32-bit elements; how exact they have to be, the bound alone decides.
A program may use at most 128 MiB of HBM per device.

```python
import math
import jax
import jax.numpy as jnp
from jax import lax

BZ = 16
Y = 128
VA = 4
VL = 4
NBX = 4
ITERS = 2
Z = 128
X = 128
VIEWS = 8
KW = 33
N_OWNER = 8


def draw_coverage(key, part):
    count_key, score_key = jax.random.split(jax.random.fold_in(key, 7))
    counts = jax.random.randint(count_key, (N_OWNER, NBX), 2, 7)
    counts = counts.at[0, 0].set(6).at[0, 1].set(2)
    scores = jax.random.randint(score_key, (N_OWNER, NBX, VIEWS), 0, 4096) * VIEWS + jnp.arange(VIEWS)
    ordering = jnp.argsort(scores, axis=-1)
    ranking = jnp.argsort(ordering, axis=-1)
    return (ranking < counts[:, :, None]).astype(jnp.int32)


def levels(stream_key, shape, cuts, low, high):
    level, own = 1.0, jax.random.fold_in(stream_key, 6)
    for dim, shards_of in cuts:
        draws = jnp.exp(jax.random.uniform(jax.random.fold_in(own, dim), (shards_of,), jnp.float32, low / len(cuts), high / len(cuts)))
        level = level * jnp.repeat(draws, shape[dim] // shards_of).reshape([-1 if axis == dim else 1 for axis in range(len(shape))])
    return level


def setup_inputs(seed: int = 0) -> dict:
    splits = jax.random.split(jax.random.key(seed), 7)
    estimate = jnp.clip(jnp.exp(math.log(2.0) - 1.3862944 * jax.random.uniform(splits[0], (Z, Y, X), jnp.float32) ** levels(splits[0], (Z, Y, X), ((0, 8),), -0.2, 0.2)), 0.5, 2.0)
    axial_views = jnp.clip(jnp.exp(math.log(3.0) - 2.3025851 * jax.random.uniform(splits[1], (VA, Z, Y, X), jnp.float32) ** levels(splits[1], (VA, Z, Y, X), ((0, 4), (1, 8)), -0.2, 0.2)), 0.3, 3.0)
    lateral_views = jnp.clip(jnp.exp(math.log(3.0) - 2.3025851 * jax.random.uniform(splits[2], (VL, X, Y, Z), jnp.float32) ** levels(splits[2], (VL, X, Y, Z), ((0, 4), (1, 8)), -0.2, 0.2)), 0.3, 3.0)
    psf_axial = jnp.clip(jnp.exp(math.log(1.0) - 2.9957323 * jax.random.uniform(splits[3], (VA, 3, KW), jnp.float32) ** levels(splits[3], (VA, 3, KW), ((0, 4),), -0.2, 0.2)), 0.05, 1.0)
    psf_lateral = jnp.clip(jnp.exp(math.log(1.0) - 2.9957323 * jax.random.uniform(splits[4], (VL, 3, KW), jnp.float32) ** levels(splits[4], (VL, 3, KW), ((0, 4),), -0.2, 0.2)), 0.05, 1.0)
    coverage = draw_coverage(jax.random.fold_in(splits[6], 71), 0)
    return dict(estimate=estimate, axial_views=axial_views, lateral_views=lateral_views, psf_axial=psf_axial, psf_lateral=psf_lateral, coverage=coverage)


PRECISE = lax.Precision.HIGHEST


def band_matrix(kernel, block_width):
    rim_width = (kernel.shape[0] - 1) // 2
    row_index = jnp.arange(block_width + 2 * rim_width)[:, None]
    col_index = jnp.arange(block_width)[None, :]
    matches = (row_index - col_index)[:, :, None] == jnp.arange(kernel.shape[0])[None, None, :]
    return jnp.sum(jnp.where(matches, kernel, 0.0), axis=-1)


def along_last(volume, kernel):
    rim_width = (kernel.shape[0] - 1) // 2
    length = volume.shape[-1]
    block_width = min(128, length)
    blocks = volume.reshape(volume.shape[:-1] + (length // block_width, block_width))
    zero_rim = jnp.zeros(blocks.shape[:-2] + (1, rim_width), volume.dtype)
    left_rim = jnp.concatenate([zero_rim, blocks[..., :-1, block_width - rim_width:]], axis=-2)
    right_rim = jnp.concatenate([blocks[..., 1:, :rim_width], zero_rim], axis=-2)
    windows = jnp.concatenate([left_rim, blocks, right_rim], axis=-1)
    result = jnp.einsum("...bs,si->...bi", windows, band_matrix(kernel, block_width), precision=PRECISE)
    return result.reshape(volume.shape)


def blur_volume(volume, kernels):
    for axis_number in range(3):
        moved = jnp.moveaxis(volume, axis_number, -1)
        volume = jnp.moveaxis(along_last(moved, kernels[axis_number]), -1, axis_number)
    return volume


def edge_weights(kernel, length):
    rim_width = (kernel.shape[0] - 1) // 2
    source = jnp.arange(length)[:, None] + jnp.arange(kernel.shape[0])[None, :] - rim_width
    inside = (source >= 0) & (source < length)
    return jnp.sum(jnp.where(inside, kernel, 0.0), axis=-1)


def reference(estimate, axial_views, lateral_views, psf_axial, psf_lateral, coverage):
    psf_all = jnp.concatenate([psf_axial, psf_lateral], axis=0)
    kernel = psf_all / jnp.sum(psf_all, axis=-1, keepdims=True)
    flipped = kernel[..., ::-1]
    plane_count, line_count, column_count = estimate.shape
    view_total = psf_all.shape[0]
    block_rows = jnp.arange(plane_count) // BZ
    block_cols = jnp.arange(column_count) // (column_count // NBX)
    covered = coverage[block_rows][:, block_cols, :].astype(jnp.float32)
    cover_count = jnp.sum(coverage[block_rows][:, block_cols, :], axis=-1).astype(jnp.float32)
    for iteration in range(ITERS):
        log_total = jnp.zeros(estimate.shape, jnp.float32)
        for view_number in range(view_total):
            if view_number < VA:
                observed = axial_views[view_number]
            else:
                observed = jnp.transpose(lateral_views[view_number - VA], (2, 1, 0))
            blurred = blur_volume(estimate, kernel[view_number])
            quotient = observed / blurred
            back_sum = blur_volume(quotient, flipped[view_number])
            scale_sum = (edge_weights(flipped[view_number, 0], plane_count)[:, None, None]
                         * edge_weights(flipped[view_number, 1], line_count)[None, :, None]
                         * edge_weights(flipped[view_number, 2], column_count)[None, None, :])
            log_total = log_total + covered[:, None, :, view_number] * jnp.log(back_sum / scale_sum)
        estimate = estimate * jnp.exp(log_total / cover_count[:, None, :])
    return estimate
```

```python
import functools

import jax
import jax.numpy as jnp
from jax import lax
from jax.experimental import pallas as pl
from jax.experimental.pallas import tpu as pltpu
from jax.sharding import PartitionSpec as P

VA = 4
ITERS = 2


PRECISE = lax.Precision.HIGHEST


def extended(shard, sides, width):
    for axis, dim in sides:
        peers, length = (lax.axis_size(axis), shard.shape[dim])
        up = [(i, (i + 1) % peers) for i in range(peers - 1)]
        down = [(j, i) for i, j in up]
        last = lax.slice_in_dim(shard, length - width, length, axis=dim)
        leading = lax.slice_in_dim(shard, 0, width, axis=dim)
        before = lax.ppermute(last, axis, up)
        after = lax.ppermute(leading, axis, down)
        shard = jnp.concatenate([before, shard, after], axis=dim)
    return shard


def band_matrix(kernel, block_width):
    rim_width = (kernel.shape[-1] - 1) // 2
    row_index = jnp.arange(block_width + 2 * rim_width)[:, None]
    col_index = jnp.arange(block_width)[None, :]
    matches = (row_index - col_index)[:, :, None] == jnp.arange(kernel.shape[-1])[None, None, :]
    return jnp.sum(jnp.where(matches[None], kernel[:, None, None, :], 0.0), axis=-1)


def middle_matrix(kernel, length):
    rim_width = (kernel.shape[-1] - 1) // 2
    row_index = jnp.arange(length)[:, None]
    col_index = jnp.arange(length)[None, :]
    matches = (row_index - col_index + rim_width)[:, :, None] == jnp.arange(kernel.shape[-1])[
        None, None, :
    ]
    return jnp.sum(jnp.where(matches[None], kernel[:, None, None, :], 0.0), axis=-1)


def along_last(volume, kernel):
    rim_width = (kernel.shape[-1] - 1) // 2
    length = volume.shape[-1]
    block_width = min(128, length)
    blocks = volume.reshape(volume.shape[:-1] + (length // block_width, block_width))
    zero_rim = jnp.zeros(blocks.shape[:-2] + (1, rim_width), volume.dtype)
    left_rim = jnp.concatenate([zero_rim, blocks[..., :-1, block_width - rim_width :]], axis=-2)
    right_rim = jnp.concatenate([blocks[..., 1:, :rim_width], zero_rim], axis=-2)
    windows = jnp.concatenate([left_rim, blocks, right_rim], axis=-1)
    result = jnp.einsum(
        "vabns,vsi->vabni", windows, band_matrix(kernel, block_width), precision=PRECISE
    )
    return result.reshape(volume.shape)


def forward(padded, kernel_first, kernel_mid, kernel_last):
    plane_count = padded.shape[0] - (kernel_first.shape[-1] - 1)
    result = jnp.einsum(
        "syl,vsi->viyl", padded, band_matrix(kernel_first, plane_count), precision=PRECISE
    )
    result = jnp.einsum(
        "viyl,vyk->vikl", result, middle_matrix(kernel_mid, result.shape[2]), precision=PRECISE
    )
    return along_last(result, kernel_last)


def backward(padded, kernel_first, kernel_mid, kernel_last):
    plane_count = padded.shape[1] - (kernel_first.shape[-1] - 1)
    result = jnp.einsum(
        "vsyl,vsi->viyl", padded, band_matrix(kernel_first, plane_count), precision=PRECISE
    )
    result = jnp.einsum(
        "viyl,vyk->vikl", result, middle_matrix(kernel_mid, result.shape[2]), precision=PRECISE
    )
    return along_last(result, kernel_last)


def edge_weights(kernel, positions, length):
    rim_width = (kernel.shape[-1] - 1) // 2
    source = positions[:, None] + jnp.arange(kernel.shape[-1])[None, :] - rim_width
    inside = (source >= 0) & (source < length)
    return jnp.sum(jnp.where(inside[None], kernel[:, None, :], 0.0), axis=-1)


def log_correction(padded, kernel_first, kernel_mid, kernel_last, first_start, first_total):
    back_sum = backward(padded, kernel_first, kernel_mid, kernel_last)
    plane_count, line_count, column_count = back_sum.shape[1:]
    first_weights = edge_weights(kernel_first, first_start + jnp.arange(plane_count), first_total)
    mid_weights = edge_weights(kernel_mid, jnp.arange(line_count), line_count)
    last_weights = edge_weights(kernel_last, jnp.arange(column_count), column_count)
    scale_sum = (
        first_weights[:, :, None, None]
        * mid_weights[:, None, :, None]
        * last_weights[:, None, None, :]
    )
    return jnp.log(back_sum / scale_sum)


def select_views(covered, view_ids):
    picked = (jnp.arange(covered.shape[-1])[None, :] == view_ids[:, None]).astype(jnp.float32)
    return jnp.einsum("vw,xw->vx", picked, covered, precision=PRECISE)


def slab_logs(padded_estimate, view_data, kernel, flipped, weights, first_start, first_total):
    blurred = forward(padded_estimate, kernel[:, 0], kernel[:, 1], kernel[:, 2])
    quotient = view_data / blurred
    rim_width = (kernel.shape[-1] - 1) // 2
    quotient_padded = extended(quotient, (("owner", 1),), rim_width)
    log_terms = log_correction(
        quotient_padded, flipped[:, 0], flipped[:, 1], flipped[:, 2], first_start, first_total
    )
    return jnp.sum(weights[:, None, None, :] * log_terms, axis=0)


def local(estimate, axial_views, lateral_views, psf_axial, psf_lateral, coverage):
    plane_count, line_count, column_count = estimate.shape
    owners = lax.axis_size("owner")
    slab_index = lax.axis_index("owner")
    view_index = lax.axis_index("view")
    slab_width = column_count // owners
    rim_width = (psf_axial.shape[-1] - 1) // 2
    kernel_axial = psf_axial / jnp.sum(psf_axial, axis=-1, keepdims=True)
    kernel_lateral = psf_lateral / jnp.sum(psf_lateral, axis=-1, keepdims=True)
    flipped_axial = kernel_axial[..., ::-1]
    flipped_lateral = kernel_lateral[..., ::-1]
    block_width = column_count // coverage.shape[1]
    covered = jnp.repeat(coverage[0].astype(jnp.float32), block_width, axis=0)
    cover_count = jnp.sum(covered, axis=-1)
    axial_count = psf_axial.shape[0]
    lateral_count = psf_lateral.shape[0]
    weights_axial = select_views(covered, view_index * axial_count + jnp.arange(axial_count))
    weights_lateral = select_views(
        covered, VA + view_index * lateral_count + jnp.arange(lateral_count)
    )
    plane_start = slab_index * plane_count
    plane_total = plane_count * owners
    moved_views = lateral_views.reshape(
        lateral_count, slab_width, line_count, owners, plane_count
    ).transpose(0, 4, 2, 3, 1)
    lateral_slabs = lax.all_to_all(moved_views, "owner", split_axis=3, concat_axis=4, tiled=True)
    lateral_slabs = lateral_slabs.reshape(lateral_count, plane_count, line_count, column_count)
    view_all = jnp.concatenate([axial_views, lateral_slabs], axis=0)
    kernel_all = jnp.concatenate([kernel_axial, kernel_lateral], axis=0)
    flipped_all = jnp.concatenate([flipped_axial, flipped_lateral], axis=0)
    weights_all = jnp.concatenate([weights_axial, weights_lateral], axis=0)
    for iteration in range(ITERS):
        padded_estimate = extended(estimate, (("owner", 0),), rim_width)
        log_total = slab_logs(
            padded_estimate,
            view_all,
            kernel_all,
            flipped_all,
            weights_all,
            plane_start,
            plane_total,
        )
        log_total = lax.psum(log_total, "view")
        estimate = estimate * jnp.exp(log_total / cover_count[None, None, :])
    return estimate


F32 = jnp.float32
BF16 = jnp.bfloat16
MESH = pl.DeviceIdType.MESH


def split_bf16(values):
    high = values.astype(BF16)
    low = (values - high.astype(F32)).astype(BF16)
    return high, low


def dot32(left, right):
    return jnp.dot(left, right, preferred_element_type=F32)


def joint_kernel(
    owners,
    views,
    planes,
    lines,
    columns,
    psf_ref,
    estimate_ref,
    axial_ref,
    lateral_ref,
    cover_ref,
    out_ref,
    window,
    observed,
    turned,
    mid,
    quot,
    logs,
    pair_sum,
    peer_sum,
    cover,
    x_fwd,
    x_back,
    y_fwd,
    y_back,
    z_fwd,
    z_back,
    log_xy,
    log_z,
    weight,
    cover_sem,
    axial_sem,
    lateral_sem,
    edge_sem,
    share_sem,
    pair_sem,
    peer_sem,
):
    taps = psf_ref.shape[0] // 3
    rim = (taps - 1) // 2
    groups = owners // 2
    span = 2 * planes
    block = planes // views
    slab = columns // owners

    me = lax.axis_index("owner")
    view = lax.axis_index("view")
    group = me // 2
    side = lax.rem(me, 2)
    core = lax.rem(view, 2)
    row = view // 2
    takes_lateral = lax.rem(side + core, 2)
    has_below = group > 0
    has_above = group < groups - 1

    def device(side_, view_):
        return (2 * group + side_, view_)

    sibling = device(side, 2 * row + 1 - core)

    barrier = pltpu.get_barrier_semaphore()
    for step in range(1, owners):
        pl.semaphore_signal(
            barrier, inc=1, device_id=(lax.rem(me + step, owners), view), device_id_type=MESH
        )
    for side_ in (side, 1 - side):
        for step in range(1, views):
            pl.semaphore_signal(
                barrier,
                inc=1,
                device_id=device(side_, lax.rem(view + step, views)),
                device_id_type=MESH,
            )
    own_rows = pl.ds((planes + planes * side) * lines, planes * lines)
    window[own_rows, :] = estimate_ref[...]
    cover[pl.ds(side, 1)] = cover_ref[...][None]
    pl.semaphore_wait(barrier, owners - 1 + 2 * (views - 1))

    def remote(src, dst, sems, index, target):
        return pltpu.make_async_remote_copy(
            src_ref=src,
            dst_ref=dst,
            send_sem=sems.at[0, index],
            recv_sem=sems.at[1, index],
            device_id=target,
            device_id_type=MESH,
        )

    def window_rows(e):
        return pl.ds(e * (block * lines), block * lines)

    def share(stage, first, last):
        def copy(e_src, e_dst, slot, target):
            return pltpu.make_async_remote_copy(
                src_ref=window.at[window_rows(e_src)],
                dst_ref=window.at[window_rows(e_dst)],
                send_sem=share_sem.at[0, stage, slot],
                recv_sem=share_sem.at[1, stage, e_dst],
                device_id=target,
                device_id_type=MESH,
            )

        def arrival(e):
            return copy(e, e, 0, sibling)

        def slot_of(side_, row_, core_):
            return views + views * side_ + 2 * row_ + core_

        own = slot_of(side, row, core)
        sent = []

        def start(condition, made):
            if condition is None:
                made.start()
            else:
                pl.when(condition)(made.start)
            sent.append((condition, made))

        if not first:
            start(None, copy(own, own, 0, device(side, 2 * (1 - row) + core)))
        if not last:
            start(None, copy(own, own, 1, device(1 - side, view)))
            start(None, copy(own, own, 2, device(1 - side, 2 * (1 - row) + core)))
        if not first:
            start(None, copy(own, own, 3, sibling))
        slot = 4
        kinds = [(0, 0), (0, 1)] if last else [(0, 0), (1, 0), (0, 1), (1, 1)]
        if first:
            kinds = [(0, 0), (0, 1), (1, 0), (1, 1)]
        for d_side, d_row in kinds:
            side_ = lax.rem(side + d_side, 2)
            row_ = lax.rem(row + d_row, 2)
            e = slot_of(side_, row_, core)
            is_own = (d_side, d_row) == (0, 0)
            if not is_own and not (first and d_side == 0):
                arrival(e).wait_recv()
            if not last:
                to = group + 2 * side_ - 1
                valid = (to >= 0) & (to < groups)
                e_dst = (1 - side_) * 3 * views + 2 * row_ + core
                start(valid, copy(e, e_dst, slot, (2 * to + side, view)))
                slot += 1
            if not is_own and not (first and d_side == 0):
                start(None, copy(e, e, slot, sibling))
                slot += 1
        if not last:
            for row_ in (0, 1):
                for base, condition in ((0, has_below), (3 * views, has_above)):
                    e = base + 2 * row_ + core
                    made = copy(e, e, slot, sibling)
                    pl.when(condition)(arrival(e).wait_recv)
                    start(condition, made)
                    slot += 1
        other = 1 - core
        for d_side, d_row in kinds:
            if first and d_side == 0:
                continue
            side_ = lax.rem(side + d_side, 2)
            row_ = lax.rem(row + d_row, 2)
            arrival(slot_of(side_, row_, other)).wait_recv()
        if not last:
            for row_ in (0, 1):
                pl.when(has_below)(arrival(2 * row_ + other).wait_recv)
                pl.when(has_above)(arrival(3 * views + 2 * row_ + other).wait_recv)
        for condition, made in sent:
            if condition is None:
                made.wait_send()
            else:
                pl.when(condition)(made.wait_send)

    def toeplitz(axis, shape, offset, flip):
        first = lax.broadcasted_iota(jnp.int32, shape, 0)
        second = lax.broadcasted_iota(jnp.int32, shape, 1)
        place = (second - first if flip else first - second) + (rim + offset)

        def add(t, total):
            return jnp.where(place == t, psf_ref[axis * taps + t], total)

        return lax.fori_loop(0, taps, add, jnp.zeros(shape, F32))

    def store_right(ref, matrix):
        high, low = split_bf16(matrix)
        top = jnp.concatenate([high, low], axis=1)
        ref[...] = jnp.concatenate([top, top], axis=0)

    def store_left(ref, matrix):
        high, low = split_bf16(matrix)
        ref[...] = jnp.concatenate(
            [jnp.concatenate([high, high], axis=1), jnp.concatenate([low, low], axis=1)], axis=0
        )

    def prepare():
        store_right(x_fwd, toeplitz(2, (columns, columns), 0, False))
        back_x = toeplitz(2, (columns, columns), 0, True)
        store_right(x_back, back_x)
        store_left(y_fwd, toeplitz(1, (lines, lines), 0, True))
        back_y = toeplitz(1, (lines, lines), 0, False)
        store_left(y_back, back_y)
        store_left(z_fwd, toeplitz(0, (span, 2 * span), -planes, True))
        back_z = toeplitz(0, (span, 2 * span), planes, False)
        store_left(z_back, back_z)
        log_xy[...] = jnp.log(jnp.sum(back_y, axis=1, keepdims=True)) + jnp.log(
            jnp.sum(back_x, axis=0, keepdims=True)
        )
        plane = lax.broadcasted_iota(jnp.int32, (span, 2 * span), 1) + (group * span - planes)
        inside = (plane >= 0) & (plane < owners * planes)
        sums = jnp.sum(jnp.where(inside, back_z, 0.0), axis=1, keepdims=True)
        log_z[...] = jnp.broadcast_to(jnp.log(sums), (span, columns))

    cover_copy = remote(cover.at[side], cover.at[side], cover_sem, 0, device(1 - side, view))
    cover_copy.start()
    axial_target = device(core, view)
    axial_mine = pl.ds(side * planes, planes)
    axial_copy = remote(axial_ref, observed.at[axial_mine], axial_sem, 0, axial_target)

    def lateral_copy(to):
        return pltpu.make_async_remote_copy(
            src_ref=turned.at[pl.ds(to * span, span)],
            dst_ref=observed.at[:, pl.ds(me * slab, slab), :],
            send_sem=lateral_sem.at[0, to],
            recv_sem=lateral_sem.at[1, me],
            device_id=(2 * to + 1 - core, view),
            device_id_type=MESH,
        )

    def lateral_arrival(source):
        return pltpu.make_async_remote_copy(
            src_ref=observed.at[:, pl.ds(source * slab, slab), :],
            dst_ref=observed.at[:, pl.ds(source * slab, slab), :],
            send_sem=lateral_sem.at[0, 0],
            recv_sem=lateral_sem.at[1, source],
            device_id=sibling,
            device_id_type=MESH,
        )

    def turn():
        for x in range(slab):
            turned[:, x, :] = lateral_ref[x].T

    def start_views():
        @pl.when(takes_lateral == 1)
        def _():
            axial_copy.start()

        for to in range(groups):

            @pl.when((takes_lateral == 0) | (to != group))
            def _():
                lateral_copy(to).start()

    def finish_views():
        @pl.when(takes_lateral == 1)
        def _():
            observed[:, pl.ds(pl.multiple_of(me * slab, slab), slab), :] = turned[
                pl.ds(group * span, span)
            ]
            axial_copy.wait_send()
            for step in range(1, owners):
                lateral_arrival(lax.rem(me + step, owners)).wait_recv()

            def flip(z, carry):
                observed[z] = observed[z].T
                return carry

            lax.fori_loop(0, span, flip, 0)

        @pl.when(takes_lateral == 0)
        def _():
            observed[axial_mine] = axial_ref[...]
            theirs = observed.at[pl.ds((1 - side) * planes, planes)]
            remote(theirs, theirs, axial_sem, 0, sibling).wait_recv()

        for to in range(groups):

            @pl.when((takes_lateral == 0) | (to != group))
            def _():
                lateral_copy(to).wait_send()

    def along_z(source, matrix, y):
        both = jnp.concatenate(
            [
                source[pl.ds(y, 2 * span, stride=lines), :],
                source[pl.ds(y + 1, 2 * span, stride=lines), :],
            ],
            axis=1,
        )
        high, low = split_bf16(both)
        result = dot32(matrix[...], jnp.concatenate([high, low], axis=0))
        result = result[:span] + result[span:]
        return result[:, :columns], result[:, columns:]

    def along_x(planes_two, matrix):
        high, low = split_bf16(planes_two)
        result = dot32(jnp.concatenate([high, low], axis=1), matrix[...])
        return result[:, :columns] + result[:, columns:]

    def along_y(planes_two, matrix):
        high, low = split_bf16(planes_two)
        result = dot32(matrix[...], jnp.concatenate([high, low], axis=0))
        return result[:lines] + result[lines:]

    def side_by_side(stacked):
        return jnp.concatenate([stacked[:lines], stacked[lines:]], axis=1)

    def stacked_up(beside):
        return jnp.concatenate([beside[:, :columns], beside[:, columns:]], axis=0)

    def forward_z():
        def lines_of(i, carry):
            for part in range(4):
                y = i * 8 + 2 * part
                one, two = along_z(window, z_fwd, y)
                mid[pl.ds(y, span, stride=lines), :] = one
                mid[pl.ds(y + 1, span, stride=lines), :] = two
            return carry

        lax.fori_loop(0, lines // 8, lines_of, 0)

    def plane_pair(iteration, z):
        rows = pl.ds(pl.multiple_of(z * lines, 2 * lines), 2 * lines)
        blurred = along_x(mid[rows, :], x_fwd)
        blurred = along_y(side_by_side(blurred), y_fwd)
        seen = jnp.concatenate([observed[z], observed[z + 1]], axis=1)
        back = along_y(seen / blurred, y_back)
        back = along_x(stacked_up(back), x_back)
        there = pl.ds(pl.multiple_of((planes + z) * lines, 2 * lines), 2 * lines)
        quot[iteration, there, :] = back

    def edge(iteration, s, up):
        start = (2 * planes if up else planes) + 2 * s
        end = (0 if up else 3 * planes) + 2 * s
        to = me + 2 if up else me - 2
        way = 1 if up else 0
        return pltpu.make_async_remote_copy(
            src_ref=quot.at[iteration, pl.ds(start * lines, 2 * lines)],
            dst_ref=quot.at[iteration, pl.ds(end * lines, 2 * lines)],
            send_sem=edge_sem.at[0, iteration, way, s],
            recv_sem=edge_sem.at[1, iteration, way, s],
            device_id=(to, view),
            device_id_type=MESH,
        )

    def middle(iteration):
        def step(s, carry):
            plane_pair(iteration, 2 * s)
            plane_pair(iteration, planes + 2 * s)
            pl.when(has_below)(edge(iteration, s, False).start)
            pl.when(has_above)(edge(iteration, s, True).start)
            return carry

        lax.fori_loop(0, planes // 2, step, 0)

        def finish(s, carry):
            @pl.when(has_below)
            def _():
                edge(iteration, s, False).wait_send()
                edge(iteration, s, True).wait_recv()

            @pl.when(has_above)
            def _():
                edge(iteration, s, True).wait_send()
                edge(iteration, s, False).wait_recv()

            return carry

        lax.fori_loop(0, planes // 2, finish, 0)

    def backward_z(iteration):
        source = quot.at[iteration]

        def lines_of(i, carry):
            for part in range(4):
                y = i * 8 + 2 * part
                for step, back in enumerate(along_z(source, z_back, y)):
                    value = jnp.log(back) - (log_z[...] + log_xy[pl.ds(y + step, 1), :])
                    logs[pl.ds(y + step, span, stride=lines), :] = weight[...] * value
            return carry

        lax.fori_loop(0, lines // 8, lines_of, 0)

    def block_rows(b):
        return pl.ds(pl.multiple_of(b * (block * lines), block * lines), block * lines)

    def reduce_and_update(iteration):
        kinds = [(1, 1), (1, 0), (0, 1), (0, 0)]

        def log_block(kind, core_):
            side_ = lax.rem(side + kind[0], 2)
            row_ = lax.rem(row + kind[1], 2)
            return views * side_ + 2 * row_ + core_

        def to_sibling(k):
            return pltpu.make_async_remote_copy(
                src_ref=logs.at[block_rows(log_block(kinds[k], 1 - core))],
                dst_ref=pair_sum.at[iteration, k],
                send_sem=pair_sem.at[0, iteration, k],
                recv_sem=pair_sem.at[1, iteration, k],
                device_id=sibling,
                device_id_type=MESH,
            )

        def to_peer(k):
            side_ = lax.rem(side + kinds[k][0], 2)
            row_ = lax.rem(row + kinds[k][1], 2)
            return pltpu.make_async_remote_copy(
                src_ref=logs.at[block_rows(log_block(kinds[k], core))],
                dst_ref=peer_sum.at[iteration, k],
                send_sem=peer_sem.at[0, iteration, k],
                recv_sem=peer_sem.at[1, iteration, k],
                device_id=device(side_, 2 * row_ + core),
                device_id_type=MESH,
            )

        for k in range(4):
            to_sibling(k).start()
        for k in range(4):
            to_sibling(k).wait_recv()
            mine = block_rows(log_block(kinds[k], core))
            logs[mine, :] = logs[mine, :] + pair_sum[iteration, k]
            if k < 3:
                to_peer(k).start()
        for k in (1, 2, 0):
            to_peer(k).wait_recv()
        count = jnp.sum(cover_ref[...], axis=0, keepdims=True)
        mine = block_rows(views * side + view)
        total = logs[mine, :] + peer_sum[iteration, 0] + peer_sum[iteration, 1] + peer_sum[iteration, 2]
        here = window_rows(views + views * side + view)
        window[here, :] = window[here, :] * jnp.exp(total / count)
        for k in range(4):
            to_sibling(k).wait_send()
        for k in range(3):
            to_peer(k).wait_send()

    turn()
    start_views()

    @pl.when(group == 0)
    def _():
        below = pl.ds(0, planes * lines)
        window[below, :] = jnp.zeros((planes * lines, columns), F32)
        for iteration in range(ITERS):
            quot[iteration, below, :] = jnp.zeros((planes * lines, columns), F32)

    @pl.when(group == groups - 1)
    def _():
        above = pl.ds(3 * planes * lines, planes * lines)
        window[above, :] = jnp.zeros((planes * lines, columns), F32)
        for iteration in range(ITERS):
            quot[iteration, above, :] = jnp.zeros((planes * lines, columns), F32)

    share(0, True, False)
    prepare()
    forward_z()
    cover_copy.wait_send()
    remote(cover.at[1 - side], cover.at[1 - side], cover_sem, 0, sibling).wait_recv()
    which = takes_lateral * views + view
    weight[:planes, :] = jnp.broadcast_to(cover[0, pl.ds(which, 1), :], (planes, columns))
    weight[planes:, :] = jnp.broadcast_to(cover[1, pl.ds(which, 1), :], (planes, columns))
    finish_views()
    for iteration in range(ITERS):
        if iteration > 0:
            forward_z()
        middle(iteration)
        backward_z(iteration)
        reduce_and_update(iteration)
        share(iteration + 1, False, iteration == ITERS - 1)
    out_ref[...] = window[own_rows, :]


def joint(estimate, axial_views, lateral_views, psf_axial, psf_lateral, coverage):
    planes, lines, columns = estimate.shape
    owners = lax.axis_size("owner")
    views = lax.axis_size("view")
    slab = columns // owners
    span = 2 * planes
    depth = owners * planes
    block_rows = planes // views * lines
    takes_lateral = (lax.axis_index("owner") + lax.axis_index("view")) % 2 == 1
    psf = jnp.where(takes_lateral, psf_lateral[0], psf_axial[0])
    psf = psf / jnp.sum(psf, axis=-1, keepdims=True)
    cover = jnp.repeat(coverage[0].astype(F32).T, columns // coverage.shape[1], axis=1)
    vmem = pl.BlockSpec(memory_space=pltpu.VMEM)
    dma = pltpu.SemaphoreType.DMA
    result = pl.pallas_call(
        functools.partial(joint_kernel, owners, views, planes, lines, columns),
        out_shape=jax.ShapeDtypeStruct((planes * lines, columns), F32),
        in_specs=[pl.BlockSpec(memory_space=pltpu.SMEM)] + [vmem] * 4,
        out_specs=vmem,
        scratch_shapes=[
            pltpu.VMEM((2 * span * lines, columns), F32),
            pltpu.VMEM((span, lines, columns), F32),
            pltpu.VMEM((depth, slab, lines), F32),
            pltpu.VMEM((span * lines, columns), F32),
            pltpu.VMEM((ITERS, 2 * span * lines, columns), F32),
            pltpu.VMEM((span * lines, columns), F32),
            pltpu.VMEM((ITERS, 4, block_rows, columns), F32),
            pltpu.VMEM((ITERS, 3, block_rows, columns), F32),
            pltpu.VMEM((2,) + cover.shape, F32),
            pltpu.VMEM((2 * columns, 2 * columns), BF16),
            pltpu.VMEM((2 * columns, 2 * columns), BF16),
            pltpu.VMEM((2 * lines, 2 * lines), BF16),
            pltpu.VMEM((2 * lines, 2 * lines), BF16),
            pltpu.VMEM((2 * span, 4 * span), BF16),
            pltpu.VMEM((2 * span, 4 * span), BF16),
            pltpu.VMEM((lines, columns), F32),
            pltpu.VMEM((span, columns), F32),
            pltpu.VMEM((span, columns), F32),
            dma((2, 1)),
            dma((2, 1)),
            dma((2, owners)),
            dma((2, ITERS, 2, planes // 2)),
            dma((2, ITERS + 1, 4 * views)),
            dma((2, ITERS, 4)),
            dma((2, ITERS, 4)),
        ],
        compiler_params=pltpu.CompilerParams(
            collective_id=0, has_side_effects=True, vmem_limit_bytes=48 * 1024 * 1024
        ),
    )(
        psf.reshape(-1),
        estimate.reshape(planes * lines, columns),
        axial_views[0],
        lateral_views[0],
        cover,
    )
    return result.reshape(planes, lines, columns)


def chosen(estimate, axial_views, lateral_views, psf_axial, psf_lateral, coverage):
    planes, lines, columns = estimate.shape
    owners = lax.axis_size("owner")
    views = lax.axis_size("view")
    rim = (psf_axial.shape[-1] - 1) // 2
    fits = (
        lines == columns
        and columns % 128 == 0
        and planes * lines * columns * 4 <= 1024 * 1024
        and planes * owners == columns
        and axial_views.shape[0] == 1
        and lateral_views.shape[0] == 1
        and views == 4
        and owners % 2 == 0
        and planes % views == 0
        and rim <= planes
        and columns // owners % 8 == 0
    )
    body = joint if fits else local
    return body(estimate, axial_views, lateral_views, psf_axial, psf_lateral, coverage)


def solution(mesh):
    in_specs = (
        P("owner", None, None),
        P("view", "owner", None, None),
        P("view", "owner", None, None),
        P("view", None, None),
        P("view", None, None),
        P("owner", None, None),
    )
    out_specs = P("owner", None, None)
    return jax.shard_map(chosen, mesh=mesh, in_specs=in_specs, out_specs=out_specs, check_vma=False)
```

```python
import functools

import jax
import jax.numpy as jnp
from jax import lax
from jax.experimental import pallas as pl
from jax.experimental.pallas import tpu as pltpu
from jax.sharding import PartitionSpec as P

VA = 4
ITERS = 2


PRECISE = lax.Precision.HIGHEST


def extended(shard, sides, width):
    for axis, dim in sides:
        peers, length = (lax.axis_size(axis), shard.shape[dim])
        up = [(i, (i + 1) % peers) for i in range(peers - 1)]
        down = [(j, i) for i, j in up]
        last = lax.slice_in_dim(shard, length - width, length, axis=dim)
        leading = lax.slice_in_dim(shard, 0, width, axis=dim)
        before = lax.ppermute(last, axis, up)
        after = lax.ppermute(leading, axis, down)
        shard = jnp.concatenate([before, shard, after], axis=dim)
    return shard


def band_matrix(kernel, block_width):
    rim_width = (kernel.shape[-1] - 1) // 2
    row_index = jnp.arange(block_width + 2 * rim_width)[:, None]
    col_index = jnp.arange(block_width)[None, :]
    matches = (row_index - col_index)[:, :, None] == jnp.arange(kernel.shape[-1])[None, None, :]
    return jnp.sum(jnp.where(matches[None], kernel[:, None, None, :], 0.0), axis=-1)


def middle_matrix(kernel, length):
    rim_width = (kernel.shape[-1] - 1) // 2
    row_index = jnp.arange(length)[:, None]
    col_index = jnp.arange(length)[None, :]
    matches = (row_index - col_index + rim_width)[:, :, None] == jnp.arange(kernel.shape[-1])[
        None, None, :
    ]
    return jnp.sum(jnp.where(matches[None], kernel[:, None, None, :], 0.0), axis=-1)


def along_last(volume, kernel):
    rim_width = (kernel.shape[-1] - 1) // 2
    length = volume.shape[-1]
    block_width = min(128, length)
    blocks = volume.reshape(volume.shape[:-1] + (length // block_width, block_width))
    zero_rim = jnp.zeros(blocks.shape[:-2] + (1, rim_width), volume.dtype)
    left_rim = jnp.concatenate([zero_rim, blocks[..., :-1, block_width - rim_width :]], axis=-2)
    right_rim = jnp.concatenate([blocks[..., 1:, :rim_width], zero_rim], axis=-2)
    windows = jnp.concatenate([left_rim, blocks, right_rim], axis=-1)
    result = jnp.einsum(
        "vabns,vsi->vabni", windows, band_matrix(kernel, block_width), precision=PRECISE
    )
    return result.reshape(volume.shape)


def forward(padded, kernel_first, kernel_mid, kernel_last):
    plane_count = padded.shape[0] - (kernel_first.shape[-1] - 1)
    result = jnp.einsum(
        "syl,vsi->viyl", padded, band_matrix(kernel_first, plane_count), precision=PRECISE
    )
    result = jnp.einsum(
        "viyl,vyk->vikl", result, middle_matrix(kernel_mid, result.shape[2]), precision=PRECISE
    )
    return along_last(result, kernel_last)


def backward(padded, kernel_first, kernel_mid, kernel_last):
    plane_count = padded.shape[1] - (kernel_first.shape[-1] - 1)
    result = jnp.einsum(
        "vsyl,vsi->viyl", padded, band_matrix(kernel_first, plane_count), precision=PRECISE
    )
    result = jnp.einsum(
        "viyl,vyk->vikl", result, middle_matrix(kernel_mid, result.shape[2]), precision=PRECISE
    )
    return along_last(result, kernel_last)


def edge_weights(kernel, positions, length):
    rim_width = (kernel.shape[-1] - 1) // 2
    source = positions[:, None] + jnp.arange(kernel.shape[-1])[None, :] - rim_width
    inside = (source >= 0) & (source < length)
    return jnp.sum(jnp.where(inside[None], kernel[:, None, :], 0.0), axis=-1)


def log_correction(padded, kernel_first, kernel_mid, kernel_last, first_start, first_total):
    back_sum = backward(padded, kernel_first, kernel_mid, kernel_last)
    plane_count, line_count, column_count = back_sum.shape[1:]
    first_weights = edge_weights(kernel_first, first_start + jnp.arange(plane_count), first_total)
    mid_weights = edge_weights(kernel_mid, jnp.arange(line_count), line_count)
    last_weights = edge_weights(kernel_last, jnp.arange(column_count), column_count)
    scale_sum = (
        first_weights[:, :, None, None]
        * mid_weights[:, None, :, None]
        * last_weights[:, None, None, :]
    )
    return jnp.log(back_sum / scale_sum)


def select_views(covered, view_ids):
    picked = (jnp.arange(covered.shape[-1])[None, :] == view_ids[:, None]).astype(jnp.float32)
    return jnp.einsum("vw,xw->vx", picked, covered, precision=PRECISE)


def slab_logs(padded_estimate, view_data, kernel, flipped, weights, first_start, first_total):
    blurred = forward(padded_estimate, kernel[:, 0], kernel[:, 1], kernel[:, 2])
    quotient = view_data / blurred
    rim_width = (kernel.shape[-1] - 1) // 2
    quotient_padded = extended(quotient, (("owner", 1),), rim_width)
    log_terms = log_correction(
        quotient_padded, flipped[:, 0], flipped[:, 1], flipped[:, 2], first_start, first_total
    )
    return jnp.sum(weights[:, None, None, :] * log_terms, axis=0)


def local(estimate, axial_views, lateral_views, psf_axial, psf_lateral, coverage):
    plane_count, line_count, column_count = estimate.shape
    owners = lax.axis_size("owner")
    slab_index = lax.axis_index("owner")
    view_index = lax.axis_index("view")
    slab_width = column_count // owners
    rim_width = (psf_axial.shape[-1] - 1) // 2
    kernel_axial = psf_axial / jnp.sum(psf_axial, axis=-1, keepdims=True)
    kernel_lateral = psf_lateral / jnp.sum(psf_lateral, axis=-1, keepdims=True)
    flipped_axial = kernel_axial[..., ::-1]
    flipped_lateral = kernel_lateral[..., ::-1]
    block_width = column_count // coverage.shape[1]
    covered = jnp.repeat(coverage[0].astype(jnp.float32), block_width, axis=0)
    cover_count = jnp.sum(covered, axis=-1)
    axial_count = psf_axial.shape[0]
    lateral_count = psf_lateral.shape[0]
    weights_axial = select_views(covered, view_index * axial_count + jnp.arange(axial_count))
    weights_lateral = select_views(
        covered, VA + view_index * lateral_count + jnp.arange(lateral_count)
    )
    plane_start = slab_index * plane_count
    plane_total = plane_count * owners
    moved_views = lateral_views.reshape(
        lateral_count, slab_width, line_count, owners, plane_count
    ).transpose(0, 4, 2, 3, 1)
    lateral_slabs = lax.all_to_all(moved_views, "owner", split_axis=3, concat_axis=4, tiled=True)
    lateral_slabs = lateral_slabs.reshape(lateral_count, plane_count, line_count, column_count)
    view_all = jnp.concatenate([axial_views, lateral_slabs], axis=0)
    kernel_all = jnp.concatenate([kernel_axial, kernel_lateral], axis=0)
    flipped_all = jnp.concatenate([flipped_axial, flipped_lateral], axis=0)
    weights_all = jnp.concatenate([weights_axial, weights_lateral], axis=0)
    for iteration in range(ITERS):
        padded_estimate = extended(estimate, (("owner", 0),), rim_width)
        log_total = slab_logs(
            padded_estimate,
            view_all,
            kernel_all,
            flipped_all,
            weights_all,
            plane_start,
            plane_total,
        )
        log_total = lax.psum(log_total, "view")
        estimate = estimate * jnp.exp(log_total / cover_count[None, None, :])
    return estimate


F32 = jnp.float32
BF16 = jnp.bfloat16
MESH = pl.DeviceIdType.MESH
CHUNKS = 4


def split_bf16(values):
    high = values.astype(BF16)
    low = (values - high.astype(F32)).astype(BF16)
    return high, low


def dot32(left, right):
    return jnp.dot(left, right, preferred_element_type=F32)


def joint_kernel(
    owners,
    views,
    planes,
    lines,
    columns,
    psf_ref,
    estimate_ref,
    axial_ref,
    lateral_ref,
    cover_ref,
    out_ref,
    window,
    observed,
    turned,
    mid,
    quot,
    logs,
    pair_sum,
    peer_sum,
    cover,
    x_fwd,
    x_back,
    y_fwd,
    y_back,
    z_fwd,
    z_back,
    log_xy,
    log_z,
    weight,
    cover_sem,
    axial_sem,
    lateral_sem,
    edge_sem,
    share_sem,
    pair_sem,
    peer_sem,
):
    taps = psf_ref.shape[0] // 3
    rim = (taps - 1) // 2
    groups = owners // 2
    span = 2 * planes
    block = planes // views
    chunk_lines = lines // CHUNKS
    slab = columns // owners

    me = lax.axis_index("owner")
    view = lax.axis_index("view")
    group = me // 2
    side = lax.rem(me, 2)
    core = lax.rem(view, 2)
    row = view // 2
    takes_lateral = lax.rem(side + core, 2)
    has_below = group > 0
    has_above = group < groups - 1

    def device(side_, view_):
        return (2 * group + side_, view_)

    sibling = device(side, 2 * row + 1 - core)

    barrier = pltpu.get_barrier_semaphore()
    for step in range(1, owners):
        pl.semaphore_signal(
            barrier, inc=1, device_id=(lax.rem(me + step, owners), view), device_id_type=MESH
        )
    for side_ in (side, 1 - side):
        for step in range(1, views):
            pl.semaphore_signal(
                barrier,
                inc=1,
                device_id=device(side_, lax.rem(view + step, views)),
                device_id_type=MESH,
            )
    own_planes = pl.ds(planes + planes * side, planes)
    window[own_planes] = estimate_ref[...]
    cover[pl.ds(side, 1)] = cover_ref[...][None]
    pl.semaphore_wait(barrier, owners - 1 + 2 * (views - 1))

    def remote(src, dst, sems, index, target):
        return pltpu.make_async_remote_copy(
            src_ref=src,
            dst_ref=dst,
            send_sem=sems.at[0, index],
            recv_sem=sems.at[1, index],
            device_id=target,
            device_id_type=MESH,
        )

    def chunk(c):
        return pl.ds(c * chunk_lines, chunk_lines)

    def part(e, c):
        return window.at[pl.ds(e * block, block), chunk(c)]

    def slot_of(side_, row_, core_):
        return views + views * side_ + 2 * row_ + core_

    def copy_part(stage, c, e_src, e_dst, slot, target):
        return pltpu.make_async_remote_copy(
            src_ref=part(e_src, c),
            dst_ref=part(e_dst, c),
            send_sem=share_sem.at[0, stage, c, slot],
            recv_sem=share_sem.at[1, stage, c, e_dst],
            device_id=target,
            device_id_type=MESH,
        )

    def arrival(stage, c, e):
        return copy_part(stage, c, e, e, 0, sibling)

    sent = {}

    def start(stage, c, condition, *where):
        made = copy_part(stage, c, *where)
        if condition is None:
            made.start()
        else:
            pl.when(condition)(made.start)
        sent.setdefault((stage, c), []).append((condition, where))

    own = slot_of(side, row, core)
    row_peer = device(side, 2 * (1 - row) + core)
    side_peer = device(1 - side, view)
    far_peer = device(1 - side, 2 * (1 - row) + core)

    def block_of(kind):
        side_ = lax.rem(side + kind[0], 2)
        row_ = lax.rem(row + kind[1], 2)
        return side_, row_, slot_of(side_, row_, core)

    def send_beside(stage, c, kind, slot):
        side_, row_, e = block_of(kind)
        to = group + 2 * side_ - 1
        valid = (to >= 0) & (to < groups)
        e_dst = (1 - side_) * 3 * views + 2 * row_ + core
        start(stage, c, valid, e, e_dst, slot, (2 * to + side, view))

    def spread_own(stage, c):
        first, last = stage == 0, stage == ITERS
        if not last:
            start(stage, c, None, own, own, 0, side_peer)
        if not first:
            start(stage, c, None, own, own, 1, row_peer)
            start(stage, c, None, own, own, 2, sibling)
        if not first and not last:
            start(stage, c, None, own, own, 3, far_peer)
        if not last:
            send_beside(stage, c, (0, 0), 4)
        if first:
            send_beside(stage, c, (0, 1), 5)

    def spread_group(stage, c):
        first, last = stage == 0, stage == ITERS
        kinds = [(0, 1), (1, 0), (1, 1)]
        if first:
            kinds = kinds[1:]
        if last:
            kinds = kinds[:1]
        for kind in kinds:
            e = block_of(kind)[2]
            arrival(stage, c, e).wait_recv()
            if first and kind == (1, 0):
                start(stage, c, None, e, e, 3, row_peer)
            if not last:
                send_beside(stage, c, kind, 4 + 2 * kind[0] + kind[1])
            start(stage, c, None, e, e, 8 + 2 * kind[0] + kind[1], sibling)

    def spread_beside(stage, c):
        if stage == ITERS:
            return
        for row_ in (0, 1):
            for k, base, condition in ((0, 0, has_below), (1, 3 * views, has_above)):
                e = base + 2 * row_ + core
                pl.when(condition)(arrival(stage, c, e).wait_recv)
                start(stage, c, condition, e, e, 12 + 2 * row_ + k, sibling)

    def spread_done(stage, c):
        first, last = stage == 0, stage == ITERS
        other = 1 - core
        for row_ in (0, 1):
            if not first:
                arrival(stage, c, slot_of(side, row_, other)).wait_recv()
            if not last:
                arrival(stage, c, slot_of(1 - side, row_, other)).wait_recv()
                pl.when(has_below)(arrival(stage, c, 2 * row_ + other).wait_recv)
                pl.when(has_above)(arrival(stage, c, 3 * views + 2 * row_ + other).wait_recv)
        for condition, where in sent[(stage, c)]:
            made = copy_part(stage, c, *where)
            if condition is None:
                made.wait_send()
            else:
                pl.when(condition)(made.wait_send)

    def toeplitz(axis, shape, offset, flip):
        first = lax.broadcasted_iota(jnp.int32, shape, 0)
        second = lax.broadcasted_iota(jnp.int32, shape, 1)
        place = (second - first if flip else first - second) + (rim + offset)

        def add(t, total):
            return jnp.where(place == t, psf_ref[axis * taps + t], total)

        return lax.fori_loop(0, taps, add, jnp.zeros(shape, F32))

    def store_right(ref, matrix):
        high, low = split_bf16(matrix)
        top = jnp.concatenate([high, low], axis=1)
        ref[...] = jnp.concatenate([top, top], axis=0)

    def store_left(ref, matrix):
        high, low = split_bf16(matrix)
        ref[...] = jnp.concatenate(
            [jnp.concatenate([high, high], axis=1), jnp.concatenate([low, low], axis=1)], axis=0
        )

    def prepare():
        store_right(x_fwd, toeplitz(2, (columns, columns), 0, False))
        back_x = toeplitz(2, (columns, columns), 0, True)
        store_right(x_back, back_x)
        store_left(y_fwd, toeplitz(1, (lines, lines), 0, True))
        back_y = toeplitz(1, (lines, lines), 0, False)
        store_left(y_back, back_y)
        store_left(z_fwd, toeplitz(0, (span, 2 * span), -planes, True))
        back_z = toeplitz(0, (span, 2 * span), planes, False)
        store_left(z_back, back_z)
        log_xy[...] = jnp.log(jnp.sum(back_y, axis=1, keepdims=True)) + jnp.log(
            jnp.sum(back_x, axis=0, keepdims=True)
        )
        plane = lax.broadcasted_iota(jnp.int32, (span, 2 * span), 1) + (group * span - planes)
        inside = (plane >= 0) & (plane < owners * planes)
        sums = jnp.sum(jnp.where(inside, back_z, 0.0), axis=1, keepdims=True)
        log_z[...] = jnp.broadcast_to(jnp.log(sums), (span, columns))

    cover_copy = remote(cover.at[side], cover.at[side], cover_sem, 0, device(1 - side, view))
    cover_copy.start()
    axial_target = device(core, view)
    axial_mine = pl.ds(side * planes, planes)
    axial_copy = remote(axial_ref, observed.at[axial_mine], axial_sem, 0, axial_target)

    def lateral_copy(to):
        return pltpu.make_async_remote_copy(
            src_ref=turned.at[pl.ds(to * span, span)],
            dst_ref=observed.at[:, pl.ds(me * slab, slab), :],
            send_sem=lateral_sem.at[0, to],
            recv_sem=lateral_sem.at[1, me],
            device_id=(2 * to + 1 - core, view),
            device_id_type=MESH,
        )

    def lateral_arrival(source):
        return pltpu.make_async_remote_copy(
            src_ref=observed.at[:, pl.ds(source * slab, slab), :],
            dst_ref=observed.at[:, pl.ds(source * slab, slab), :],
            send_sem=lateral_sem.at[0, 0],
            recv_sem=lateral_sem.at[1, source],
            device_id=sibling,
            device_id_type=MESH,
        )

    def turn():
        for x in range(slab):
            turned[:, x, :] = lateral_ref[x].T

    def start_views():
        @pl.when(takes_lateral == 1)
        def _():
            axial_copy.start()

        for to in range(groups):

            @pl.when((takes_lateral == 0) | (to != group))
            def _():
                lateral_copy(to).start()

    def finish_views():
        @pl.when(takes_lateral == 1)
        def _():
            observed[:, pl.ds(pl.multiple_of(me * slab, slab), slab), :] = turned[
                pl.ds(group * span, span)
            ]
            axial_copy.wait_send()
            for step in range(1, owners):
                lateral_arrival(lax.rem(me + step, owners)).wait_recv()

            def flip(z, carry):
                observed[z] = observed[z].T
                return carry

            lax.fori_loop(0, span, flip, 0)

        @pl.when(takes_lateral == 0)
        def _():
            observed[axial_mine] = axial_ref[...]
            theirs = observed.at[pl.ds((1 - side) * planes, planes)]
            remote(theirs, theirs, axial_sem, 0, sibling).wait_recv()

        for to in range(groups):

            @pl.when((takes_lateral == 0) | (to != group))
            def _():
                lateral_copy(to).wait_send()

    def along_z(source, matrix, y):
        both = jnp.concatenate(
            [
                source[pl.ds(y, 2 * span, stride=lines), :],
                source[pl.ds(y + 1, 2 * span, stride=lines), :],
            ],
            axis=1,
        )
        high, low = split_bf16(both)
        result = dot32(matrix[...], jnp.concatenate([high, low], axis=0))
        result = result[:span] + result[span:]
        return result[:, :columns], result[:, columns:]

    def along_x(planes_two, matrix):
        high, low = split_bf16(planes_two)
        result = dot32(jnp.concatenate([high, low], axis=1), matrix[...])
        return result[:, :columns] + result[:, columns:]

    def along_y(planes_two, matrix):
        high, low = split_bf16(planes_two)
        result = dot32(matrix[...], jnp.concatenate([high, low], axis=0))
        return result[:lines] + result[lines:]

    def side_by_side(stacked):
        return jnp.concatenate([stacked[:lines], stacked[lines:]], axis=1)

    def stacked_up(beside):
        return jnp.concatenate([beside[:, :columns], beside[:, columns:]], axis=0)

    window_lines = window.reshape(2 * span * lines, columns)
    mid_lines = mid.reshape(span * lines, columns)
    logs_lines = logs.reshape(span * lines, columns)

    def forward_z(c):
        def lines_of(i, carry):
            for step in range(4):
                y = c * chunk_lines + i * 8 + 2 * step
                one, two = along_z(window_lines, z_fwd, y)
                mid_lines[pl.ds(y, span, stride=lines), :] = one
                mid_lines[pl.ds(y + 1, span, stride=lines), :] = two
            return carry

        lax.fori_loop(0, chunk_lines // 8, lines_of, 0)

    def plane_pair(iteration, z):
        blurred = along_x(mid[pl.ds(z, 2)].reshape(2 * lines, columns), x_fwd)
        blurred = along_y(side_by_side(blurred), y_fwd)
        seen = jnp.concatenate([observed[z], observed[z + 1]], axis=1)
        back = along_y(seen / blurred, y_back)
        back = along_x(stacked_up(back), x_back)
        quot[iteration, pl.ds(planes + z, 2)] = back.reshape(2, lines, columns)

    early = CHUNKS // 2
    steps = planes // 2

    def edge(iteration, index, up, plane, count, lines_at):
        start_plane = (2 * planes if up else planes) + plane
        end_plane = (0 if up else 3 * planes) + plane
        way = 1 if up else 0
        return pltpu.make_async_remote_copy(
            src_ref=quot.at[iteration, pl.ds(start_plane, count), lines_at],
            dst_ref=quot.at[iteration, pl.ds(end_plane, count), lines_at],
            send_sem=edge_sem.at[0, iteration, way, index],
            recv_sem=edge_sem.at[1, iteration, way, index],
            device_id=(me + 2 if up else me - 2, view),
            device_id_type=MESH,
        )

    def early_edge(iteration, s, up):
        return edge(iteration, s, up, 2 * s, 2, pl.ds(0, early * chunk_lines))

    def late_edge(iteration, c, up):
        return edge(iteration, steps + c - early, up, 0, planes, chunk(c))

    def middle(iteration):
        def step(s, carry):
            plane_pair(iteration, 2 * s)
            plane_pair(iteration, planes + 2 * s)
            pl.when(has_below)(early_edge(iteration, s, False).start)
            pl.when(has_above)(early_edge(iteration, s, True).start)
            return carry

        lax.fori_loop(0, steps, step, 0)
        for c in range(early, CHUNKS):
            pl.when(has_below)(late_edge(iteration, c, False).start)
            pl.when(has_above)(late_edge(iteration, c, True).start)

    def edges_arrived(iteration, c):
        def finish(s, carry):
            pl.when(has_above)(early_edge(iteration, s, False).wait_recv)
            pl.when(has_below)(early_edge(iteration, s, True).wait_recv)
            return carry

        if c == 0:
            lax.fori_loop(0, steps, finish, 0)
        if c >= early:
            pl.when(has_above)(late_edge(iteration, c, False).wait_recv)
            pl.when(has_below)(late_edge(iteration, c, True).wait_recv)

    def edges_sent(iteration):
        def finish(s, carry):
            pl.when(has_below)(early_edge(iteration, s, False).wait_send)
            pl.when(has_above)(early_edge(iteration, s, True).wait_send)
            return carry

        lax.fori_loop(0, steps, finish, 0)
        for c in range(early, CHUNKS):
            pl.when(has_below)(late_edge(iteration, c, False).wait_send)
            pl.when(has_above)(late_edge(iteration, c, True).wait_send)

    def backward_z(iteration, c):
        source = quot.at[iteration].reshape(2 * span * lines, columns)

        def lines_of(i, carry):
            for part_ in range(4):
                y = c * chunk_lines + i * 8 + 2 * part_
                for step, back in enumerate(along_z(source, z_back, y)):
                    value = jnp.log(back) - (log_z[...] + log_xy[pl.ds(y + step, 1), :])
                    logs_lines[pl.ds(y + step, span, stride=lines), :] = weight[...] * value
            return carry

        lax.fori_loop(0, chunk_lines // 8, lines_of, 0)

    kinds = [(1, 1), (1, 0), (0, 1), (0, 0)]

    def log_block(kind, core_):
        side_ = lax.rem(side + kind[0], 2)
        row_ = lax.rem(row + kind[1], 2)
        return pl.ds((views * side_ + 2 * row_ + core_) * block, block)

    def to_sibling(iteration, c, k):
        return pltpu.make_async_remote_copy(
            src_ref=logs.at[log_block(kinds[k], 1 - core), chunk(c)],
            dst_ref=pair_sum.at[iteration, k, :, chunk(c)],
            send_sem=pair_sem.at[0, iteration, c, k],
            recv_sem=pair_sem.at[1, iteration, c, k],
            device_id=sibling,
            device_id_type=MESH,
        )

    def to_peer(iteration, c, k):
        side_ = lax.rem(side + kinds[k][0], 2)
        row_ = lax.rem(row + kinds[k][1], 2)
        return pltpu.make_async_remote_copy(
            src_ref=logs.at[log_block(kinds[k], core), chunk(c)],
            dst_ref=peer_sum.at[iteration, k, :, chunk(c)],
            send_sem=peer_sem.at[0, iteration, c, k],
            recv_sem=peer_sem.at[1, iteration, c, k],
            device_id=device(side_, 2 * row_ + core),
            device_id_type=MESH,
        )

    def correct(iteration, c):
        edges_arrived(iteration, c)
        backward_z(iteration, c)
        for k in range(4):
            to_sibling(iteration, c, k).start()

    def reduce_pair(iteration, c):
        for k in range(4):
            to_sibling(iteration, c, k).wait_recv()
            mine = log_block(kinds[k], core)
            logs[mine, chunk(c)] = logs[mine, chunk(c)] + pair_sum[iteration, k, :, chunk(c)]
            if k < 3:
                to_peer(iteration, c, k).start()

    def update(iteration, c):
        for k in (1, 2, 0):
            to_peer(iteration, c, k).wait_recv()
        count = jnp.sum(cover_ref[...], axis=0, keepdims=True)
        total = logs[log_block((0, 0), core), chunk(c)]
        for k in range(3):
            total = total + peer_sum[iteration, k, :, chunk(c)]
        here = pl.ds(own * block, block)
        window[here, chunk(c)] = window[here, chunk(c)] * jnp.exp(total / count[None])
        spread_own(iteration + 1, c)

    def sums_sent(iteration, c):
        for k in range(4):
            to_sibling(iteration, c, k).wait_send()
        for k in range(3):
            to_peer(iteration, c, k).wait_send()

    def settle(stage, c):
        spread_done(stage, c)
        if stage < ITERS:
            forward_z(c)
        else:
            out_ref[:, chunk(c)] = window[own_planes, chunk(c)]

    def pipeline(stages):
        for t in range(CHUNKS + len(stages) - 1):
            for lag, stage in enumerate(stages):
                if 0 <= t - lag < CHUNKS:
                    stage(t - lag)

    zero = jnp.zeros((planes, lines, columns), F32)

    @pl.when(group == 0)
    def _():
        window[:planes] = zero
        for iteration in range(ITERS):
            quot[iteration, :planes] = zero

    @pl.when(group == groups - 1)
    def _():
        window[3 * planes :] = zero
        for iteration in range(ITERS):
            quot[iteration, 3 * planes :] = zero

    for c in range(CHUNKS):
        spread_own(0, c)
    turn()
    start_views()
    prepare()
    pipeline(
        [
            functools.partial(spread_group, 0),
            functools.partial(spread_beside, 0),
            functools.partial(settle, 0),
        ]
    )
    cover_copy.wait_send()
    remote(cover.at[1 - side], cover.at[1 - side], cover_sem, 0, sibling).wait_recv()
    which = takes_lateral * views + view
    weight[:planes, :] = jnp.broadcast_to(cover[0, pl.ds(which, 1), :], (planes, columns))
    weight[planes:, :] = jnp.broadcast_to(cover[1, pl.ds(which, 1), :], (planes, columns))
    finish_views()
    for iteration in range(ITERS):
        middle(iteration)
        pipeline(
            [
                functools.partial(correct, iteration),
                functools.partial(reduce_pair, iteration),
                functools.partial(update, iteration),
                functools.partial(spread_group, iteration + 1),
                functools.partial(spread_beside, iteration + 1),
                functools.partial(settle, iteration + 1),
            ]
        )
        edges_sent(iteration)
        for c in range(CHUNKS):
            sums_sent(iteration, c)


def joint(estimate, axial_views, lateral_views, psf_axial, psf_lateral, coverage):
    planes, lines, columns = estimate.shape
    owners = lax.axis_size("owner")
    views = lax.axis_size("view")
    slab = columns // owners
    span = 2 * planes
    depth = owners * planes
    block = planes // views
    takes_lateral = (lax.axis_index("owner") + lax.axis_index("view")) % 2 == 1
    psf = jnp.where(takes_lateral, psf_lateral[0], psf_axial[0])
    psf = psf / jnp.sum(psf, axis=-1, keepdims=True)
    cover = jnp.repeat(coverage[0].astype(F32).T, columns // coverage.shape[1], axis=1)
    vmem = pl.BlockSpec(memory_space=pltpu.VMEM)
    dma = pltpu.SemaphoreType.DMA
    result = pl.pallas_call(
        functools.partial(joint_kernel, owners, views, planes, lines, columns),
        out_shape=jax.ShapeDtypeStruct((planes, lines, columns), F32),
        in_specs=[pl.BlockSpec(memory_space=pltpu.SMEM)] + [vmem] * 4,
        out_specs=vmem,
        scratch_shapes=[
            pltpu.VMEM((2 * span, lines, columns), F32),
            pltpu.VMEM((span, lines, columns), F32),
            pltpu.VMEM((depth, slab, lines), F32),
            pltpu.VMEM((span, lines, columns), F32),
            pltpu.VMEM((ITERS, 2 * span, lines, columns), F32),
            pltpu.VMEM((span, lines, columns), F32),
            pltpu.VMEM((ITERS, 4, block, lines, columns), F32),
            pltpu.VMEM((ITERS, 3, block, lines, columns), F32),
            pltpu.VMEM((2,) + cover.shape, F32),
            pltpu.VMEM((2 * columns, 2 * columns), BF16),
            pltpu.VMEM((2 * columns, 2 * columns), BF16),
            pltpu.VMEM((2 * lines, 2 * lines), BF16),
            pltpu.VMEM((2 * lines, 2 * lines), BF16),
            pltpu.VMEM((2 * span, 4 * span), BF16),
            pltpu.VMEM((2 * span, 4 * span), BF16),
            pltpu.VMEM((lines, columns), F32),
            pltpu.VMEM((span, columns), F32),
            pltpu.VMEM((span, columns), F32),
            dma((2, 1)),
            dma((2, 1)),
            dma((2, owners)),
            dma((2, ITERS, 2, planes // 2 + CHUNKS)),
            dma((2, ITERS + 1, CHUNKS, 4 * views)),
            dma((2, ITERS, CHUNKS, 4)),
            dma((2, ITERS, CHUNKS, 4)),
        ],
        compiler_params=pltpu.CompilerParams(
            collective_id=0, has_side_effects=True, vmem_limit_bytes=48 * 1024 * 1024
        ),
    )(
        psf.reshape(-1),
        estimate,
        axial_views[0],
        lateral_views[0],
        cover,
    )
    return result


def chosen(estimate, axial_views, lateral_views, psf_axial, psf_lateral, coverage):
    planes, lines, columns = estimate.shape
    owners = lax.axis_size("owner")
    views = lax.axis_size("view")
    rim = (psf_axial.shape[-1] - 1) // 2
    fits = (
        lines == columns
        and columns % 128 == 0
        and planes * lines * columns * 4 <= 1024 * 1024
        and planes * owners == columns
        and axial_views.shape[0] == 1
        and lateral_views.shape[0] == 1
        and views == 4
        and owners % 2 == 0
        and planes % views == 0
        and rim <= planes
        and columns // owners % 8 == 0
        and lines % (8 * CHUNKS) == 0
    )
    body = joint if fits else local
    return body(estimate, axial_views, lateral_views, psf_axial, psf_lateral, coverage)


def solution(mesh):
    in_specs = (
        P("owner", None, None),
        P("view", "owner", None, None),
        P("view", "owner", None, None),
        P("view", None, None),
        P("view", None, None),
        P("owner", None, None),
    )
    out_specs = P("owner", None, None)
    return jax.shard_map(chosen, mesh=mesh, in_specs=in_specs, out_specs=out_specs, check_vma=False)
```

```python
import functools

import jax
import jax.numpy as jnp
from jax import lax
from jax.experimental import pallas as pl
from jax.experimental.pallas import tpu as pltpu
from jax.sharding import PartitionSpec as P

VA = 4
ITERS = 2


PRECISE = lax.Precision.HIGHEST


def extended(shard, sides, width):
    for axis, dim in sides:
        peers, length = (lax.axis_size(axis), shard.shape[dim])
        up = [(i, (i + 1) % peers) for i in range(peers - 1)]
        down = [(j, i) for i, j in up]
        last = lax.slice_in_dim(shard, length - width, length, axis=dim)
        leading = lax.slice_in_dim(shard, 0, width, axis=dim)
        before = lax.ppermute(last, axis, up)
        after = lax.ppermute(leading, axis, down)
        shard = jnp.concatenate([before, shard, after], axis=dim)
    return shard


def band_matrix(kernel, block_width):
    rim_width = (kernel.shape[-1] - 1) // 2
    row_index = jnp.arange(block_width + 2 * rim_width)[:, None]
    col_index = jnp.arange(block_width)[None, :]
    matches = (row_index - col_index)[:, :, None] == jnp.arange(kernel.shape[-1])[None, None, :]
    return jnp.sum(jnp.where(matches[None], kernel[:, None, None, :], 0.0), axis=-1)


def middle_matrix(kernel, length):
    rim_width = (kernel.shape[-1] - 1) // 2
    row_index = jnp.arange(length)[:, None]
    col_index = jnp.arange(length)[None, :]
    matches = (row_index - col_index + rim_width)[:, :, None] == jnp.arange(kernel.shape[-1])[
        None, None, :
    ]
    return jnp.sum(jnp.where(matches[None], kernel[:, None, None, :], 0.0), axis=-1)


def along_last(volume, kernel):
    rim_width = (kernel.shape[-1] - 1) // 2
    length = volume.shape[-1]
    block_width = min(128, length)
    blocks = volume.reshape(volume.shape[:-1] + (length // block_width, block_width))
    zero_rim = jnp.zeros(blocks.shape[:-2] + (1, rim_width), volume.dtype)
    left_rim = jnp.concatenate([zero_rim, blocks[..., :-1, block_width - rim_width :]], axis=-2)
    right_rim = jnp.concatenate([blocks[..., 1:, :rim_width], zero_rim], axis=-2)
    windows = jnp.concatenate([left_rim, blocks, right_rim], axis=-1)
    result = jnp.einsum(
        "vabns,vsi->vabni", windows, band_matrix(kernel, block_width), precision=PRECISE
    )
    return result.reshape(volume.shape)


def forward(padded, kernel_first, kernel_mid, kernel_last):
    plane_count = padded.shape[0] - (kernel_first.shape[-1] - 1)
    result = jnp.einsum(
        "syl,vsi->viyl", padded, band_matrix(kernel_first, plane_count), precision=PRECISE
    )
    result = jnp.einsum(
        "viyl,vyk->vikl", result, middle_matrix(kernel_mid, result.shape[2]), precision=PRECISE
    )
    return along_last(result, kernel_last)


def backward(padded, kernel_first, kernel_mid, kernel_last):
    plane_count = padded.shape[1] - (kernel_first.shape[-1] - 1)
    result = jnp.einsum(
        "vsyl,vsi->viyl", padded, band_matrix(kernel_first, plane_count), precision=PRECISE
    )
    result = jnp.einsum(
        "viyl,vyk->vikl", result, middle_matrix(kernel_mid, result.shape[2]), precision=PRECISE
    )
    return along_last(result, kernel_last)


def edge_weights(kernel, positions, length):
    rim_width = (kernel.shape[-1] - 1) // 2
    source = positions[:, None] + jnp.arange(kernel.shape[-1])[None, :] - rim_width
    inside = (source >= 0) & (source < length)
    return jnp.sum(jnp.where(inside[None], kernel[:, None, :], 0.0), axis=-1)


def log_correction(padded, kernel_first, kernel_mid, kernel_last, first_start, first_total):
    back_sum = backward(padded, kernel_first, kernel_mid, kernel_last)
    plane_count, line_count, column_count = back_sum.shape[1:]
    first_weights = edge_weights(kernel_first, first_start + jnp.arange(plane_count), first_total)
    mid_weights = edge_weights(kernel_mid, jnp.arange(line_count), line_count)
    last_weights = edge_weights(kernel_last, jnp.arange(column_count), column_count)
    scale_sum = (
        first_weights[:, :, None, None]
        * mid_weights[:, None, :, None]
        * last_weights[:, None, None, :]
    )
    return jnp.log(back_sum / scale_sum)


def select_views(covered, view_ids):
    picked = (jnp.arange(covered.shape[-1])[None, :] == view_ids[:, None]).astype(jnp.float32)
    return jnp.einsum("vw,xw->vx", picked, covered, precision=PRECISE)


def slab_logs(padded_estimate, view_data, kernel, flipped, weights, first_start, first_total):
    blurred = forward(padded_estimate, kernel[:, 0], kernel[:, 1], kernel[:, 2])
    quotient = view_data / blurred
    rim_width = (kernel.shape[-1] - 1) // 2
    quotient_padded = extended(quotient, (("owner", 1),), rim_width)
    log_terms = log_correction(
        quotient_padded, flipped[:, 0], flipped[:, 1], flipped[:, 2], first_start, first_total
    )
    return jnp.sum(weights[:, None, None, :] * log_terms, axis=0)


def local(estimate, axial_views, lateral_views, psf_axial, psf_lateral, coverage):
    plane_count, line_count, column_count = estimate.shape
    owners = lax.axis_size("owner")
    slab_index = lax.axis_index("owner")
    view_index = lax.axis_index("view")
    slab_width = column_count // owners
    rim_width = (psf_axial.shape[-1] - 1) // 2
    kernel_axial = psf_axial / jnp.sum(psf_axial, axis=-1, keepdims=True)
    kernel_lateral = psf_lateral / jnp.sum(psf_lateral, axis=-1, keepdims=True)
    flipped_axial = kernel_axial[..., ::-1]
    flipped_lateral = kernel_lateral[..., ::-1]
    block_width = column_count // coverage.shape[1]
    covered = jnp.repeat(coverage[0].astype(jnp.float32), block_width, axis=0)
    cover_count = jnp.sum(covered, axis=-1)
    axial_count = psf_axial.shape[0]
    lateral_count = psf_lateral.shape[0]
    weights_axial = select_views(covered, view_index * axial_count + jnp.arange(axial_count))
    weights_lateral = select_views(
        covered, VA + view_index * lateral_count + jnp.arange(lateral_count)
    )
    plane_start = slab_index * plane_count
    plane_total = plane_count * owners
    moved_views = lateral_views.reshape(
        lateral_count, slab_width, line_count, owners, plane_count
    ).transpose(0, 4, 2, 3, 1)
    lateral_slabs = lax.all_to_all(moved_views, "owner", split_axis=3, concat_axis=4, tiled=True)
    lateral_slabs = lateral_slabs.reshape(lateral_count, plane_count, line_count, column_count)
    view_all = jnp.concatenate([axial_views, lateral_slabs], axis=0)
    kernel_all = jnp.concatenate([kernel_axial, kernel_lateral], axis=0)
    flipped_all = jnp.concatenate([flipped_axial, flipped_lateral], axis=0)
    weights_all = jnp.concatenate([weights_axial, weights_lateral], axis=0)
    for iteration in range(ITERS):
        padded_estimate = extended(estimate, (("owner", 0),), rim_width)
        log_total = slab_logs(
            padded_estimate,
            view_all,
            kernel_all,
            flipped_all,
            weights_all,
            plane_start,
            plane_total,
        )
        log_total = lax.psum(log_total, "view")
        estimate = estimate * jnp.exp(log_total / cover_count[None, None, :])
    return estimate


F32 = jnp.float32
BF16 = jnp.bfloat16
MESH = pl.DeviceIdType.MESH
CHUNKS = 8
PARTS = 4


def split_bf16(values):
    high = values.astype(BF16)
    low = (values - high.astype(F32)).astype(BF16)
    return high, low


def dot32(left, right):
    return jnp.dot(left, right, preferred_element_type=F32)


def joint_kernel(
    owners,
    views,
    planes,
    lines,
    columns,
    psf_ref,
    estimate_ref,
    axial_ref,
    lateral_ref,
    cover_ref,
    out_ref,
    window,
    observed,
    lateral,
    turned,
    mid,
    quot,
    logs,
    pair_sum,
    peer_sum,
    cover,
    x_fwd,
    x_back,
    y_fwd,
    y_back,
    z_fwd,
    z_back,
    log_xy,
    log_z,
    weight,
    cover_sem,
    axial_sem,
    lateral_sem,
    edge_sem,
    share_sem,
    pair_sem,
    peer_sem,
    local_sem,
):
    taps = psf_ref.shape[0] // 3
    rim = (taps - 1) // 2
    groups = owners // 2
    span = 2 * planes
    block = planes // views
    chunk_lines = lines // CHUNKS
    slab = columns // owners

    me = lax.axis_index("owner")
    view = lax.axis_index("view")
    group = me // 2
    side = lax.rem(me, 2)
    core = lax.rem(view, 2)
    row = view // 2
    takes_lateral = lax.rem(side + core, 2)
    has_below = group > 0
    has_above = group < groups - 1

    def device(side_, view_):
        return (2 * group + side_, view_)

    sibling = device(side, 2 * row + 1 - core)

    barrier = pltpu.get_barrier_semaphore()
    for step in range(1, owners):
        pl.semaphore_signal(
            barrier, inc=1, device_id=(lax.rem(me + step, owners), view), device_id_type=MESH
        )
    for side_ in (side, 1 - side):
        for step in range(1, views):
            pl.semaphore_signal(
                barrier,
                inc=1,
                device_id=device(side_, lax.rem(view + step, views)),
                device_id_type=MESH,
            )
    own_planes = pl.ds(planes + planes * side, planes)
    estimate_in = pltpu.make_async_copy(estimate_ref, window.at[own_planes], local_sem.at[0])
    lateral_in = pltpu.make_async_copy(lateral_ref, lateral, local_sem.at[1])
    estimate_in.start()
    lateral_in.start()
    cover[pl.ds(side, 1)] = cover_ref[...][None]

    def clear(base):
        def plane(z, carry):
            zero = jnp.zeros((lines, columns), F32)
            window[base + z] = zero
            for iteration in range(ITERS):
                quot[iteration, base + z] = zero
            return carry

        lax.fori_loop(0, planes, plane, 0)

    pl.when(group == 0)(lambda: clear(0))
    pl.when(group == groups - 1)(lambda: clear(3 * planes))

    estimate_in.wait()
    pl.semaphore_wait(barrier, owners - 1 + 2 * (views - 1))

    def remote(src, dst, sems, index, target):
        return pltpu.make_async_remote_copy(
            src_ref=src,
            dst_ref=dst,
            send_sem=sems.at[0, index],
            recv_sem=sems.at[1, index],
            device_id=target,
            device_id_type=MESH,
        )

    def chunk(c):
        return pl.ds(c * chunk_lines, chunk_lines)

    def part(e, c):
        return window.at[pl.ds(e * block, block), chunk(c)]

    def slot_of(side_, row_, core_):
        return views + views * side_ + 2 * row_ + core_

    def copy_part(stage, c, e_src, e_dst, slot, target):
        return pltpu.make_async_remote_copy(
            src_ref=part(e_src, c),
            dst_ref=part(e_dst, c),
            send_sem=share_sem.at[0, stage, c, slot],
            recv_sem=share_sem.at[1, stage, c, e_dst],
            device_id=target,
            device_id_type=MESH,
        )

    def arrival(stage, c, e):
        return copy_part(stage, c, e, e, 0, sibling)

    sent = {}

    def start(stage, c, condition, *where):
        made = copy_part(stage, c, *where)
        if condition is None:
            made.start()
        else:
            pl.when(condition)(made.start)
        sent.setdefault((stage, c), []).append((condition, where))

    own = slot_of(side, row, core)
    row_peer = device(side, 2 * (1 - row) + core)
    side_peer = device(1 - side, view)
    far_peer = device(1 - side, 2 * (1 - row) + core)

    def block_of(kind):
        side_ = lax.rem(side + kind[0], 2)
        row_ = lax.rem(row + kind[1], 2)
        return side_, row_, slot_of(side_, row_, core)

    def send_beside(stage, c, kind, slot):
        side_, row_, e = block_of(kind)
        to = group + 2 * side_ - 1
        valid = (to >= 0) & (to < groups)
        e_dst = (1 - side_) * 3 * views + 2 * row_ + core
        start(stage, c, valid, e, e_dst, slot, (2 * to + side, view))

    def spread_own(stage, c):
        first, last = stage == 0, stage == ITERS
        if not last:
            start(stage, c, None, own, own, 0, side_peer)
        if not first:
            start(stage, c, None, own, own, 1, row_peer)
            start(stage, c, None, own, own, 2, sibling)
        if not first and not last:
            start(stage, c, None, own, own, 3, far_peer)
        if not last:
            send_beside(stage, c, (0, 0), 4)
        if first:
            send_beside(stage, c, (0, 1), 5)

    def spread_group(stage, c):
        first, last = stage == 0, stage == ITERS
        kinds = [(0, 1), (1, 0), (1, 1)]
        if first:
            kinds = kinds[1:]
        if last:
            kinds = kinds[:1]
        for kind in kinds:
            e = block_of(kind)[2]
            arrival(stage, c, e).wait_recv()
            if first and kind == (1, 0):
                start(stage, c, None, e, e, 3, row_peer)
            if not last:
                send_beside(stage, c, kind, 4 + 2 * kind[0] + kind[1])
            start(stage, c, None, e, e, 8 + 2 * kind[0] + kind[1], sibling)

    def spread_beside(stage, c):
        if stage == ITERS:
            return
        for row_ in (0, 1):
            for k, base, condition in ((0, 0, has_below), (1, 3 * views, has_above)):
                e = base + 2 * row_ + core
                pl.when(condition)(arrival(stage, c, e).wait_recv)
                start(stage, c, condition, e, e, 12 + 2 * row_ + k, sibling)

    def spread_done(stage, c):
        first, last = stage == 0, stage == ITERS
        other = 1 - core
        for row_ in (0, 1):
            if not first:
                arrival(stage, c, slot_of(side, row_, other)).wait_recv()
            if not last:
                arrival(stage, c, slot_of(1 - side, row_, other)).wait_recv()
                pl.when(has_below)(arrival(stage, c, 2 * row_ + other).wait_recv)
                pl.when(has_above)(arrival(stage, c, 3 * views + 2 * row_ + other).wait_recv)
        for condition, where in sent[(stage, c)]:
            made = copy_part(stage, c, *where)
            if condition is None:
                made.wait_send()
            else:
                pl.when(condition)(made.wait_send)

    def toeplitz(axis, shape, offset, flip):
        first = lax.broadcasted_iota(jnp.int32, shape, 0)
        second = lax.broadcasted_iota(jnp.int32, shape, 1)
        place = (second - first if flip else first - second) + (rim + offset)

        def add(t, total):
            return jnp.where(place == t, psf_ref[axis * taps + t], total)

        return lax.fori_loop(0, taps, add, jnp.zeros(shape, F32))

    def store_right(ref, matrix):
        high, low = split_bf16(matrix)
        top = jnp.concatenate([high, low], axis=1)
        ref[...] = jnp.concatenate([top, top], axis=0)

    def store_left(ref, matrix):
        high, low = split_bf16(matrix)
        ref[...] = jnp.concatenate(
            [jnp.concatenate([high, high], axis=1), jnp.concatenate([low, low], axis=1)], axis=0
        )

    def prepare():
        store_right(x_fwd, toeplitz(2, (columns, columns), 0, False))
        back_x = toeplitz(2, (columns, columns), 0, True)
        store_right(x_back, back_x)
        store_left(y_fwd, toeplitz(1, (lines, lines), 0, True))
        back_y = toeplitz(1, (lines, lines), 0, False)
        store_left(y_back, back_y)
        store_left(z_fwd, toeplitz(0, (span, 2 * span), -planes, True))
        back_z = toeplitz(0, (span, 2 * span), planes, False)
        store_left(z_back, back_z)
        log_xy[...] = jnp.log(jnp.sum(back_y, axis=1, keepdims=True)) + jnp.log(
            jnp.sum(back_x, axis=0, keepdims=True)
        )
        plane = lax.broadcasted_iota(jnp.int32, (span, 2 * span), 1) + (group * span - planes)
        inside = (plane >= 0) & (plane < owners * planes)
        sums = jnp.sum(jnp.where(inside, back_z, 0.0), axis=1, keepdims=True)
        log_z[...] = jnp.broadcast_to(jnp.log(sums), (span, columns))

    cover_copy = remote(cover.at[side], cover.at[side], cover_sem, 0, device(1 - side, view))
    cover_copy.start()
    axial_target = device(core, view)
    axial_mine = pl.ds(side * planes, planes)
    depth = planes // PARTS
    axial_in = pltpu.make_async_copy(axial_ref, observed.at[axial_mine], local_sem.at[2])

    def axial_copy(q):
        return remote(
            axial_ref.at[pl.ds(q * depth, depth)],
            observed.at[pl.ds(side * planes + q * depth, depth)],
            axial_sem,
            q,
            axial_target,
        )

    def axial_arrival(q):
        theirs = observed.at[pl.ds((1 - side) * planes + q * depth, depth)]
        return remote(theirs, theirs, axial_sem, q, sibling)

    def lateral_copy(to, q, half):
        plane = half * planes + q * depth
        return pltpu.make_async_remote_copy(
            src_ref=turned.at[pl.ds(to * span + plane, depth)],
            dst_ref=observed.at[pl.ds(plane, depth), pl.ds(me * slab, slab), :],
            send_sem=lateral_sem.at[0, to, q, half],
            recv_sem=lateral_sem.at[1, me, q, half],
            device_id=(2 * to + 1 - core, view),
            device_id_type=MESH,
        )

    def lateral_arrival(source, q, half):
        there = observed.at[pl.ds(half * planes + q * depth, depth), pl.ds(source * slab, slab), :]
        return pltpu.make_async_remote_copy(
            src_ref=there,
            dst_ref=there,
            send_sem=lateral_sem.at[0, 0, q, half],
            recv_sem=lateral_sem.at[1, source, q, half],
            device_id=sibling,
            device_id_type=MESH,
        )

    def turn():
        lateral_in.wait()
        for x in range(slab):
            turned[:, x, :] = lateral[x].T

    def each_lateral(act):
        for q in range(PARTS):
            for to in range(groups):

                @pl.when((takes_lateral == 0) | (to != group))
                def _():
                    act(lateral_copy(to, q, 0))
                    act(lateral_copy(to, q, 1))

    def start_axial():
        @pl.when(takes_lateral == 1)
        def _():
            for q in range(PARTS):
                axial_copy(q).start()

        @pl.when(takes_lateral == 0)
        def _():
            axial_in.start()

    def start_lateral():
        each_lateral(lambda copy: copy.start())

        @pl.when(takes_lateral == 1)
        def _():
            observed[:, pl.ds(pl.multiple_of(me * slab, slab), slab), :] = turned[
                pl.ds(group * span, span)
            ]

    def views_arrived(q):
        @pl.when(takes_lateral == 1)
        def _():
            for half in (0, 1):
                for step in range(1, owners):
                    lateral_arrival(lax.rem(me + step, owners), q, half).wait_recv()

                def flip(z, carry):
                    observed[z] = observed[z].T
                    return carry

                first_plane = half * planes + q * depth
                lax.fori_loop(first_plane, first_plane + depth, flip, 0)

        @pl.when(takes_lateral == 0)
        def _():
            if q == 0:
                axial_in.wait()
            axial_arrival(q).wait_recv()

    def views_sent():
        each_lateral(lambda copy: copy.wait_send())

        @pl.when(takes_lateral == 1)
        def _():
            for q in range(PARTS):
                axial_copy(q).wait_send()

    def along_z(source, matrix, y):
        both = jnp.concatenate(
            [
                source[pl.ds(y, 2 * span, stride=lines), :],
                source[pl.ds(y + 1, 2 * span, stride=lines), :],
            ],
            axis=1,
        )
        high, low = split_bf16(both)
        result = dot32(matrix[...], jnp.concatenate([high, low], axis=0))
        result = result[:span] + result[span:]
        return result[:, :columns], result[:, columns:]

    def along_x(planes_two, matrix):
        high, low = split_bf16(planes_two)
        result = dot32(jnp.concatenate([high, low], axis=1), matrix[...])
        return result[:, :columns] + result[:, columns:]

    def along_y(planes_two, matrix):
        high, low = split_bf16(planes_two)
        result = dot32(matrix[...], jnp.concatenate([high, low], axis=0))
        return result[:lines] + result[lines:]

    def side_by_side(stacked):
        return jnp.concatenate([stacked[:lines], stacked[lines:]], axis=1)

    def stacked_up(beside):
        return jnp.concatenate([beside[:, :columns], beside[:, columns:]], axis=0)

    window_lines = window.reshape(2 * span * lines, columns)
    mid_lines = mid.reshape(span * lines, columns)
    logs_lines = logs.reshape(span * lines, columns)

    def forward_z(c):
        def lines_of(i, carry):
            for step in range(4):
                y = c * chunk_lines + i * 8 + 2 * step
                one, two = along_z(window_lines, z_fwd, y)
                mid_lines[pl.ds(y, span, stride=lines), :] = one
                mid_lines[pl.ds(y + 1, span, stride=lines), :] = two
            return carry

        lax.fori_loop(0, chunk_lines // 8, lines_of, 0)

    def plane_pair(iteration, z):
        blurred = along_x(mid[pl.ds(z, 2)].reshape(2 * lines, columns), x_fwd)
        blurred = along_y(side_by_side(blurred), y_fwd)
        seen = jnp.concatenate([observed[z], observed[z + 1]], axis=1)
        back = along_y(seen / blurred, y_back)
        back = along_x(stacked_up(back), x_back)
        quot[iteration, pl.ds(planes + z, 2)] = back.reshape(2, lines, columns)

    early = CHUNKS // 2
    steps = planes // 2

    def edge(iteration, index, up, plane, count, lines_at):
        start_plane = (2 * planes if up else planes) + plane
        end_plane = (0 if up else 3 * planes) + plane
        way = 1 if up else 0
        return pltpu.make_async_remote_copy(
            src_ref=quot.at[iteration, pl.ds(start_plane, count), lines_at],
            dst_ref=quot.at[iteration, pl.ds(end_plane, count), lines_at],
            send_sem=edge_sem.at[0, iteration, way, index],
            recv_sem=edge_sem.at[1, iteration, way, index],
            device_id=(me + 2 if up else me - 2, view),
            device_id_type=MESH,
        )

    def early_edge(iteration, s, up):
        return edge(iteration, s, up, 2 * s, 2, pl.ds(0, early * chunk_lines))

    def late_edge(iteration, c, up):
        return edge(iteration, steps + c - early, up, 0, planes, chunk(c))

    def middle(iteration):
        def step(s, carry):
            plane_pair(iteration, 2 * s)
            plane_pair(iteration, planes + 2 * s)
            pl.when(has_below)(early_edge(iteration, s, False).start)
            pl.when(has_above)(early_edge(iteration, s, True).start)
            return carry

        if iteration == 0:
            for q in range(PARTS):
                views_arrived(q)
                lax.fori_loop(q * (steps // PARTS), (q + 1) * (steps // PARTS), step, 0)
        else:
            lax.fori_loop(0, steps, step, 0)
        for c in range(early, CHUNKS):
            pl.when(has_below)(late_edge(iteration, c, False).start)
            pl.when(has_above)(late_edge(iteration, c, True).start)

    def edges_arrived(iteration, c):
        def finish(s, carry):
            pl.when(has_above)(early_edge(iteration, s, False).wait_recv)
            pl.when(has_below)(early_edge(iteration, s, True).wait_recv)
            return carry

        if c == 0:
            lax.fori_loop(0, steps, finish, 0)
        if c >= early:
            pl.when(has_above)(late_edge(iteration, c, False).wait_recv)
            pl.when(has_below)(late_edge(iteration, c, True).wait_recv)

    def edges_sent(iteration):
        def finish(s, carry):
            pl.when(has_below)(early_edge(iteration, s, False).wait_send)
            pl.when(has_above)(early_edge(iteration, s, True).wait_send)
            return carry

        lax.fori_loop(0, steps, finish, 0)
        for c in range(early, CHUNKS):
            pl.when(has_below)(late_edge(iteration, c, False).wait_send)
            pl.when(has_above)(late_edge(iteration, c, True).wait_send)

    def backward_z(iteration, c):
        source = quot.at[iteration].reshape(2 * span * lines, columns)

        def lines_of(i, carry):
            for part_ in range(4):
                y = c * chunk_lines + i * 8 + 2 * part_
                for step, back in enumerate(along_z(source, z_back, y)):
                    value = jnp.log(back) - (log_z[...] + log_xy[pl.ds(y + step, 1), :])
                    logs_lines[pl.ds(y + step, span, stride=lines), :] = weight[...] * value
            return carry

        lax.fori_loop(0, chunk_lines // 8, lines_of, 0)

    kinds = [(1, 1), (1, 0), (0, 1), (0, 0)]

    def log_block(kind, core_):
        side_ = lax.rem(side + kind[0], 2)
        row_ = lax.rem(row + kind[1], 2)
        return pl.ds((views * side_ + 2 * row_ + core_) * block, block)

    def to_sibling(iteration, c, k):
        return pltpu.make_async_remote_copy(
            src_ref=logs.at[log_block(kinds[k], 1 - core), chunk(c)],
            dst_ref=pair_sum.at[iteration, k, :, chunk(c)],
            send_sem=pair_sem.at[0, iteration, c, k],
            recv_sem=pair_sem.at[1, iteration, c, k],
            device_id=sibling,
            device_id_type=MESH,
        )

    def to_peer(iteration, c, k):
        side_ = lax.rem(side + kinds[k][0], 2)
        row_ = lax.rem(row + kinds[k][1], 2)
        return pltpu.make_async_remote_copy(
            src_ref=logs.at[log_block(kinds[k], core), chunk(c)],
            dst_ref=peer_sum.at[iteration, k, :, chunk(c)],
            send_sem=peer_sem.at[0, iteration, c, k],
            recv_sem=peer_sem.at[1, iteration, c, k],
            device_id=device(side_, 2 * row_ + core),
            device_id_type=MESH,
        )

    def correct(iteration, c):
        edges_arrived(iteration, c)
        backward_z(iteration, c)
        for k in range(4):
            to_sibling(iteration, c, k).start()

    def reduce_pair(iteration, c):
        for k in range(4):
            to_sibling(iteration, c, k).wait_recv()
            mine = log_block(kinds[k], core)
            logs[mine, chunk(c)] = logs[mine, chunk(c)] + pair_sum[iteration, k, :, chunk(c)]
            if k < 3:
                to_peer(iteration, c, k).start()

    def update(iteration, c):
        for k in (1, 2, 0):
            to_peer(iteration, c, k).wait_recv()
        count = jnp.sum(cover_ref[...], axis=0, keepdims=True)
        total = logs[log_block((0, 0), core), chunk(c)]
        for k in range(3):
            total = total + peer_sum[iteration, k, :, chunk(c)]
        here = pl.ds(own * block, block)
        window[here, chunk(c)] = window[here, chunk(c)] * jnp.exp(total / count[None])
        spread_own(iteration + 1, c)

    def sums_sent(iteration, c):
        for k in range(4):
            to_sibling(iteration, c, k).wait_send()
        for k in range(3):
            to_peer(iteration, c, k).wait_send()

    def settle(stage, c):
        spread_done(stage, c)
        if stage < ITERS:
            forward_z(c)
        else:
            out_ref[:, chunk(c)] = window[own_planes, chunk(c)]

    def pipeline(stages):
        for t in range(CHUNKS + len(stages) - 1):
            for lag, stage in enumerate(stages):
                if 0 <= t - lag < CHUNKS:
                    stage(t - lag)

    for c in range(CHUNKS):
        spread_own(0, c)
    start_axial()
    turn()
    start_lateral()
    prepare()
    pipeline(
        [
            functools.partial(spread_group, 0),
            functools.partial(spread_beside, 0),
            functools.partial(settle, 0),
        ]
    )
    cover_copy.wait_send()
    remote(cover.at[1 - side], cover.at[1 - side], cover_sem, 0, sibling).wait_recv()
    which = takes_lateral * views + view
    weight[:planes, :] = jnp.broadcast_to(cover[0, pl.ds(which, 1), :], (planes, columns))
    weight[planes:, :] = jnp.broadcast_to(cover[1, pl.ds(which, 1), :], (planes, columns))
    for iteration in range(ITERS):
        middle(iteration)
        pipeline(
            [
                functools.partial(correct, iteration),
                functools.partial(reduce_pair, iteration),
                functools.partial(update, iteration),
                functools.partial(spread_group, iteration + 1),
                functools.partial(spread_beside, iteration + 1),
                functools.partial(settle, iteration + 1),
            ]
        )
        edges_sent(iteration)
        for c in range(CHUNKS):
            sums_sent(iteration, c)
    views_sent()


def joint(estimate, axial_views, lateral_views, psf_axial, psf_lateral, coverage):
    planes, lines, columns = estimate.shape
    owners = lax.axis_size("owner")
    views = lax.axis_size("view")
    slab = columns // owners
    span = 2 * planes
    depth = owners * planes
    block = planes // views
    takes_lateral = (lax.axis_index("owner") + lax.axis_index("view")) % 2 == 1
    psf = jnp.where(takes_lateral, psf_lateral[0], psf_axial[0])
    psf = psf / jnp.sum(psf, axis=-1, keepdims=True)
    cover = jnp.repeat(coverage[0].astype(F32).T, columns // coverage.shape[1], axis=1)
    vmem = pl.BlockSpec(memory_space=pltpu.VMEM)
    hbm = pl.BlockSpec(memory_space=pl.ANY)
    dma = pltpu.SemaphoreType.DMA
    result = pl.pallas_call(
        functools.partial(joint_kernel, owners, views, planes, lines, columns),
        out_shape=jax.ShapeDtypeStruct((planes, lines, columns), F32),
        in_specs=[pl.BlockSpec(memory_space=pltpu.SMEM)] + [hbm] * 3 + [vmem],
        out_specs=vmem,
        scratch_shapes=[
            pltpu.VMEM((2 * span, lines, columns), F32),
            pltpu.VMEM((span, lines, columns), F32),
            pltpu.VMEM((slab, lines, depth), F32),
            pltpu.VMEM((depth, slab, lines), F32),
            pltpu.VMEM((span, lines, columns), F32),
            pltpu.VMEM((ITERS, 2 * span, lines, columns), F32),
            pltpu.VMEM((span, lines, columns), F32),
            pltpu.VMEM((ITERS, 4, block, lines, columns), F32),
            pltpu.VMEM((ITERS, 3, block, lines, columns), F32),
            pltpu.VMEM((2,) + cover.shape, F32),
            pltpu.VMEM((2 * columns, 2 * columns), BF16),
            pltpu.VMEM((2 * columns, 2 * columns), BF16),
            pltpu.VMEM((2 * lines, 2 * lines), BF16),
            pltpu.VMEM((2 * lines, 2 * lines), BF16),
            pltpu.VMEM((2 * span, 4 * span), BF16),
            pltpu.VMEM((2 * span, 4 * span), BF16),
            pltpu.VMEM((lines, columns), F32),
            pltpu.VMEM((span, columns), F32),
            pltpu.VMEM((span, columns), F32),
            dma((2, 1)),
            dma((2, PARTS)),
            dma((2, owners, PARTS, 2)),
            dma((2, ITERS, 2, planes // 2 + CHUNKS)),
            dma((2, ITERS + 1, CHUNKS, 4 * views)),
            dma((2, ITERS, CHUNKS, 4)),
            dma((2, ITERS, CHUNKS, 4)),
            dma((3,)),
        ],
        compiler_params=pltpu.CompilerParams(
            collective_id=0, has_side_effects=True, vmem_limit_bytes=48 * 1024 * 1024
        ),
    )(
        psf.reshape(-1),
        estimate,
        axial_views[0],
        lateral_views[0],
        cover,
    )
    return result


def chosen(estimate, axial_views, lateral_views, psf_axial, psf_lateral, coverage):
    planes, lines, columns = estimate.shape
    owners = lax.axis_size("owner")
    views = lax.axis_size("view")
    rim = (psf_axial.shape[-1] - 1) // 2
    fits = (
        lines == columns
        and columns % 128 == 0
        and planes * lines * columns * 4 <= 1024 * 1024
        and planes * owners == columns
        and axial_views.shape[0] == 1
        and lateral_views.shape[0] == 1
        and views == 4
        and owners % 2 == 0
        and planes % views == 0
        and planes % (2 * PARTS) == 0
        and rim <= planes
        and columns // owners % 8 == 0
        and lines % (8 * CHUNKS) == 0
    )
    body = joint if fits else local
    return body(estimate, axial_views, lateral_views, psf_axial, psf_lateral, coverage)


def solution(mesh):
    in_specs = (
        P("owner", None, None),
        P("view", "owner", None, None),
        P("view", "owner", None, None),
        P("view", None, None),
        P("view", None, None),
        P("owner", None, None),
    )
    out_specs = P("owner", None, None)
    return jax.shard_map(chosen, mesh=mesh, in_specs=in_specs, out_specs=out_specs, check_vma=False)
```

```python
import functools

import jax
import jax.numpy as jnp
from jax import lax
from jax.experimental import pallas as pl
from jax.experimental.pallas import tpu as pltpu
from jax.sharding import PartitionSpec as P

VA = 4
ITERS = 2


PRECISE = lax.Precision.HIGHEST


def extended(shard, sides, width):
    for axis, dim in sides:
        peers, length = (lax.axis_size(axis), shard.shape[dim])
        up = [(i, (i + 1) % peers) for i in range(peers - 1)]
        down = [(j, i) for i, j in up]
        last = lax.slice_in_dim(shard, length - width, length, axis=dim)
        leading = lax.slice_in_dim(shard, 0, width, axis=dim)
        before = lax.ppermute(last, axis, up)
        after = lax.ppermute(leading, axis, down)
        shard = jnp.concatenate([before, shard, after], axis=dim)
    return shard


def band_matrix(kernel, block_width):
    rim_width = (kernel.shape[-1] - 1) // 2
    row_index = jnp.arange(block_width + 2 * rim_width)[:, None]
    col_index = jnp.arange(block_width)[None, :]
    matches = (row_index - col_index)[:, :, None] == jnp.arange(kernel.shape[-1])[None, None, :]
    return jnp.sum(jnp.where(matches[None], kernel[:, None, None, :], 0.0), axis=-1)


def middle_matrix(kernel, length):
    rim_width = (kernel.shape[-1] - 1) // 2
    row_index = jnp.arange(length)[:, None]
    col_index = jnp.arange(length)[None, :]
    matches = (row_index - col_index + rim_width)[:, :, None] == jnp.arange(kernel.shape[-1])[
        None, None, :
    ]
    return jnp.sum(jnp.where(matches[None], kernel[:, None, None, :], 0.0), axis=-1)


def along_last(volume, kernel):
    rim_width = (kernel.shape[-1] - 1) // 2
    length = volume.shape[-1]
    block_width = min(128, length)
    blocks = volume.reshape(volume.shape[:-1] + (length // block_width, block_width))
    zero_rim = jnp.zeros(blocks.shape[:-2] + (1, rim_width), volume.dtype)
    left_rim = jnp.concatenate([zero_rim, blocks[..., :-1, block_width - rim_width :]], axis=-2)
    right_rim = jnp.concatenate([blocks[..., 1:, :rim_width], zero_rim], axis=-2)
    windows = jnp.concatenate([left_rim, blocks, right_rim], axis=-1)
    result = jnp.einsum(
        "vabns,vsi->vabni", windows, band_matrix(kernel, block_width), precision=PRECISE
    )
    return result.reshape(volume.shape)


def forward(padded, kernel_first, kernel_mid, kernel_last):
    plane_count = padded.shape[0] - (kernel_first.shape[-1] - 1)
    result = jnp.einsum(
        "syl,vsi->viyl", padded, band_matrix(kernel_first, plane_count), precision=PRECISE
    )
    result = jnp.einsum(
        "viyl,vyk->vikl", result, middle_matrix(kernel_mid, result.shape[2]), precision=PRECISE
    )
    return along_last(result, kernel_last)


def backward(padded, kernel_first, kernel_mid, kernel_last):
    plane_count = padded.shape[1] - (kernel_first.shape[-1] - 1)
    result = jnp.einsum(
        "vsyl,vsi->viyl", padded, band_matrix(kernel_first, plane_count), precision=PRECISE
    )
    result = jnp.einsum(
        "viyl,vyk->vikl", result, middle_matrix(kernel_mid, result.shape[2]), precision=PRECISE
    )
    return along_last(result, kernel_last)


def edge_weights(kernel, positions, length):
    rim_width = (kernel.shape[-1] - 1) // 2
    source = positions[:, None] + jnp.arange(kernel.shape[-1])[None, :] - rim_width
    inside = (source >= 0) & (source < length)
    return jnp.sum(jnp.where(inside[None], kernel[:, None, :], 0.0), axis=-1)


def log_correction(padded, kernel_first, kernel_mid, kernel_last, first_start, first_total):
    back_sum = backward(padded, kernel_first, kernel_mid, kernel_last)
    plane_count, line_count, column_count = back_sum.shape[1:]
    first_weights = edge_weights(kernel_first, first_start + jnp.arange(plane_count), first_total)
    mid_weights = edge_weights(kernel_mid, jnp.arange(line_count), line_count)
    last_weights = edge_weights(kernel_last, jnp.arange(column_count), column_count)
    scale_sum = (
        first_weights[:, :, None, None]
        * mid_weights[:, None, :, None]
        * last_weights[:, None, None, :]
    )
    return jnp.log(back_sum / scale_sum)


def select_views(covered, view_ids):
    picked = (jnp.arange(covered.shape[-1])[None, :] == view_ids[:, None]).astype(jnp.float32)
    return jnp.einsum("vw,xw->vx", picked, covered, precision=PRECISE)


def slab_logs(padded_estimate, view_data, kernel, flipped, weights, first_start, first_total):
    blurred = forward(padded_estimate, kernel[:, 0], kernel[:, 1], kernel[:, 2])
    quotient = view_data / blurred
    rim_width = (kernel.shape[-1] - 1) // 2
    quotient_padded = extended(quotient, (("owner", 1),), rim_width)
    log_terms = log_correction(
        quotient_padded, flipped[:, 0], flipped[:, 1], flipped[:, 2], first_start, first_total
    )
    return jnp.sum(weights[:, None, None, :] * log_terms, axis=0)


def local(estimate, axial_views, lateral_views, psf_axial, psf_lateral, coverage):
    plane_count, line_count, column_count = estimate.shape
    owners = lax.axis_size("owner")
    slab_index = lax.axis_index("owner")
    view_index = lax.axis_index("view")
    slab_width = column_count // owners
    rim_width = (psf_axial.shape[-1] - 1) // 2
    kernel_axial = psf_axial / jnp.sum(psf_axial, axis=-1, keepdims=True)
    kernel_lateral = psf_lateral / jnp.sum(psf_lateral, axis=-1, keepdims=True)
    flipped_axial = kernel_axial[..., ::-1]
    flipped_lateral = kernel_lateral[..., ::-1]
    block_width = column_count // coverage.shape[1]
    covered = jnp.repeat(coverage[0].astype(jnp.float32), block_width, axis=0)
    cover_count = jnp.sum(covered, axis=-1)
    axial_count = psf_axial.shape[0]
    lateral_count = psf_lateral.shape[0]
    weights_axial = select_views(covered, view_index * axial_count + jnp.arange(axial_count))
    weights_lateral = select_views(
        covered, VA + view_index * lateral_count + jnp.arange(lateral_count)
    )
    plane_start = slab_index * plane_count
    plane_total = plane_count * owners
    moved_views = lateral_views.reshape(
        lateral_count, slab_width, line_count, owners, plane_count
    ).transpose(0, 4, 2, 3, 1)
    lateral_slabs = lax.all_to_all(moved_views, "owner", split_axis=3, concat_axis=4, tiled=True)
    lateral_slabs = lateral_slabs.reshape(lateral_count, plane_count, line_count, column_count)
    view_all = jnp.concatenate([axial_views, lateral_slabs], axis=0)
    kernel_all = jnp.concatenate([kernel_axial, kernel_lateral], axis=0)
    flipped_all = jnp.concatenate([flipped_axial, flipped_lateral], axis=0)
    weights_all = jnp.concatenate([weights_axial, weights_lateral], axis=0)
    for iteration in range(ITERS):
        padded_estimate = extended(estimate, (("owner", 0),), rim_width)
        log_total = slab_logs(
            padded_estimate,
            view_all,
            kernel_all,
            flipped_all,
            weights_all,
            plane_start,
            plane_total,
        )
        log_total = lax.psum(log_total, "view")
        estimate = estimate * jnp.exp(log_total / cover_count[None, None, :])
    return estimate


F32 = jnp.float32
BF16 = jnp.bfloat16
MESH = pl.DeviceIdType.MESH
CHUNKS = 4
PARTS = 2


def split_bf16(values):
    high = values.astype(BF16)
    low = (values - high.astype(F32)).astype(BF16)
    return high, low


def dot32(left, right):
    return jnp.dot(left, right, preferred_element_type=F32)


def joint_kernel(
    owners,
    views,
    planes,
    lines,
    columns,
    psf_ref,
    estimate_ref,
    axial_ref,
    lateral_ref,
    cover_ref,
    out_ref,
    window,
    observed,
    lateral,
    turned,
    mid,
    quot,
    logs,
    pair_sum,
    peer_sum,
    cover,
    x_fwd,
    x_back,
    y_fwd,
    y_back,
    z_fwd,
    z_back,
    log_xy,
    log_z,
    weight,
    cover_sem,
    axial_sem,
    lateral_sem,
    edge_sem,
    share_sem,
    pair_sem,
    peer_sem,
    local_sem,
):
    taps = psf_ref.shape[0] // 3
    rim = (taps - 1) // 2
    groups = owners // 2
    span = 2 * planes
    block = planes // views
    chunk_lines = lines // CHUNKS
    slab = columns // owners

    me = lax.axis_index("owner")
    view = lax.axis_index("view")
    group = me // 2
    side = lax.rem(me, 2)
    core = lax.rem(view, 2)
    row = view // 2
    takes_lateral = lax.rem(side + core, 2)
    has_below = group > 0
    has_above = group < groups - 1

    def device(side_, view_):
        return (2 * group + side_, view_)

    sibling = device(side, 2 * row + 1 - core)

    barrier = pltpu.get_barrier_semaphore()
    for step in range(1, owners):
        pl.semaphore_signal(
            barrier, inc=1, device_id=(lax.rem(me + step, owners), view), device_id_type=MESH
        )
    for side_ in (side, 1 - side):
        for step in range(1, views):
            pl.semaphore_signal(
                barrier,
                inc=1,
                device_id=device(side_, lax.rem(view + step, views)),
                device_id_type=MESH,
            )
    own_planes = pl.ds(planes + planes * side, planes)
    estimate_in = pltpu.make_async_copy(estimate_ref, window.at[own_planes], local_sem.at[0])
    lateral_in = pltpu.make_async_copy(lateral_ref, lateral, local_sem.at[1])
    estimate_in.start()
    lateral_in.start()
    cover[pl.ds(side, 1)] = cover_ref[...][None]

    def clear(base):
        def plane(z, carry):
            zero = jnp.zeros((lines, columns), F32)
            window[base + z] = zero
            for iteration in range(ITERS):
                quot[iteration * 2 * span + base + z] = zero
            return carry

        lax.fori_loop(0, planes, plane, 0)

    pl.when(group == 0)(lambda: clear(0))
    pl.when(group == groups - 1)(lambda: clear(3 * planes))

    estimate_in.wait()
    pl.semaphore_wait(barrier, owners - 1 + 2 * (views - 1))

    def remote(src, dst, sems, index, target):
        return pltpu.make_async_remote_copy(
            src_ref=src,
            dst_ref=dst,
            send_sem=sems.at[0, index],
            recv_sem=sems.at[1, index],
            device_id=target,
            device_id_type=MESH,
        )

    def chunk(c):
        return pl.ds(pl.multiple_of(c * chunk_lines, chunk_lines), chunk_lines)

    def part(e, c):
        return window.at[pl.ds(e * block, block), chunk(c)]

    def slot_of(side_, row_, core_):
        return views + views * side_ + 2 * row_ + core_

    def copy_part(stage, c, e_src, e_dst, slot, target):
        return pltpu.make_async_remote_copy(
            src_ref=part(e_src, c),
            dst_ref=part(e_dst, c),
            send_sem=share_sem.at[0, stage, c, slot],
            recv_sem=share_sem.at[1, stage, c, e_dst],
            device_id=target,
            device_id_type=MESH,
        )

    def arrival(stage, c, e):
        return copy_part(stage, c, e, e, 0, sibling)

    own = slot_of(side, row, core)
    row_peer = device(side, 2 * (1 - row) + core)
    side_peer = device(1 - side, view)
    far_peer = device(1 - side, 2 * (1 - row) + core)
    other = 1 - core
    yes = group >= 0

    def block_of(kind):
        side_ = lax.rem(side + kind[0], 2)
        row_ = lax.rem(row + kind[1], 2)
        return side_, slot_of(side_, row_, core)

    def beside(more, kind):
        side_, e = block_of(kind)
        to = group + 2 * side_ - 1
        valid = (to >= 0) & (to < groups) & more
        e_dst = e + (1 - 3 * side_) * views + (1 - side_) * views
        return valid, e, e_dst, 4 + 2 * kind[0] + kind[1], (2 * to + side, view)

    def plan(first, more):
        if first:
            at_once = [(yes, own, own, 0, side_peer), beside(yes, (0, 0)), beside(yes, (0, 1))]
        else:
            at_once = [
                (more, own, own, 0, side_peer),
                (yes, own, own, 1, row_peer),
                (yes, own, own, 2, sibling),
                (more, own, own, 3, far_peer),
                beside(more, (0, 0)),
            ]
        group_steps = []
        for kind in [(1, 0), (1, 1)] if first else [(0, 1), (1, 0), (1, 1)]:
            e = block_of(kind)[1]
            when = yes if kind == (0, 1) else more
            onward = [beside(more, kind), (when, e, e, 8 + 2 * kind[0] + kind[1], sibling)]
            if first and kind == (1, 0):
                onward.append((yes, e, e, 3, row_peer))
            group_steps.append((when, e, onward))
        beside_steps = []
        rest = []
        for row_ in (0, 1):
            for k, base, condition in ((0, 0, has_below), (1, 3 * views, has_above)):
                e = base + 2 * row_ + core
                onward = [(condition & more, e, e, 12 + 2 * row_ + k, sibling)]
                beside_steps.append((condition & more, e, onward))
                rest.append((condition & more, base + 2 * row_ + other))
            if not first:
                rest.append((yes, slot_of(side, row_, other)))
            rest.append((more, slot_of(1 - side, row_, other)))
        return at_once, group_steps, beside_steps, rest

    def start_all(stage, c, sends):
        for condition, *where in sends:
            pl.when(condition)(copy_part(stage, c, *where).start)

    def send_on(stage, c, steps_):
        for condition, e, onward in steps_:
            pl.when(condition)(arrival(stage, c, e).wait_recv)
            start_all(stage, c, onward)

    def spread_done(stage, c, made):
        at_once, group_steps, beside_steps, rest = made
        for condition, e in rest:
            pl.when(condition)(arrival(stage, c, e).wait_recv)
        onwards = [onward for _, _, onward in group_steps + beside_steps]
        for condition, *where in sum(onwards, at_once):
            pl.when(condition)(copy_part(stage, c, *where).wait_send)

    def toeplitz(axis, shape, offset, flip):
        first = lax.broadcasted_iota(jnp.int32, shape, 0)
        second = lax.broadcasted_iota(jnp.int32, shape, 1)
        place = (second - first if flip else first - second) + (rim + offset)

        def add(t, total):
            return jnp.where(place == t, psf_ref[axis * taps + t], total)

        return lax.fori_loop(0, taps, add, jnp.zeros(shape, F32))

    def store_right(ref, matrix):
        high, low = split_bf16(matrix)
        top = jnp.concatenate([high, low], axis=1)
        ref[...] = jnp.concatenate([top, top], axis=0)

    def store_left(ref, matrix):
        high, low = split_bf16(matrix)
        ref[...] = jnp.concatenate(
            [jnp.concatenate([high, high], axis=1), jnp.concatenate([low, low], axis=1)], axis=0
        )

    def prepare():
        store_right(x_fwd, toeplitz(2, (columns, columns), 0, False))
        back_x = toeplitz(2, (columns, columns), 0, True)
        store_right(x_back, back_x)
        store_left(y_fwd, toeplitz(1, (lines, lines), 0, True))
        back_y = toeplitz(1, (lines, lines), 0, False)
        store_left(y_back, back_y)
        store_left(z_fwd, toeplitz(0, (span, 2 * span), -planes, True))
        back_z = toeplitz(0, (span, 2 * span), planes, False)
        store_left(z_back, back_z)
        log_xy[...] = jnp.log(jnp.sum(back_y, axis=1, keepdims=True)) + jnp.log(
            jnp.sum(back_x, axis=0, keepdims=True)
        )
        plane = lax.broadcasted_iota(jnp.int32, (span, 2 * span), 1) + (group * span - planes)
        inside = (plane >= 0) & (plane < owners * planes)
        sums = jnp.sum(jnp.where(inside, back_z, 0.0), axis=1, keepdims=True)
        log_z[...] = jnp.broadcast_to(jnp.log(sums), (span, columns))

    cover_copy = remote(cover.at[side], cover.at[side], cover_sem, 0, device(1 - side, view))
    cover_copy.start()
    axial_target = device(core, view)
    axial_mine = pl.ds(side * planes, planes)
    depth = planes // PARTS
    axial_in = pltpu.make_async_copy(axial_ref, observed.at[axial_mine], local_sem.at[2])

    def axial_copy(q):
        return remote(
            axial_ref.at[pl.ds(q * depth, depth)],
            observed.at[pl.ds(side * planes + q * depth, depth)],
            axial_sem,
            q,
            axial_target,
        )

    def axial_arrival(q):
        theirs = observed.at[pl.ds((1 - side) * planes + q * depth, depth)]
        return remote(theirs, theirs, axial_sem, q, sibling)

    def lateral_copy(to, q, half):
        plane = half * planes + q * depth
        return pltpu.make_async_remote_copy(
            src_ref=turned.at[pl.ds(to * span + plane, depth)],
            dst_ref=observed.at[pl.ds(plane, depth), pl.ds(me * slab, slab), :],
            send_sem=lateral_sem.at[0, to, q, half],
            recv_sem=lateral_sem.at[1, me, q, half],
            device_id=(2 * to + 1 - core, view),
            device_id_type=MESH,
        )

    def lateral_arrival(source, q, half):
        there = observed.at[pl.ds(half * planes + q * depth, depth), pl.ds(source * slab, slab), :]
        return pltpu.make_async_remote_copy(
            src_ref=there,
            dst_ref=there,
            send_sem=lateral_sem.at[0, 0, q, half],
            recv_sem=lateral_sem.at[1, source, q, half],
            device_id=sibling,
            device_id_type=MESH,
        )

    def turn():
        lateral_in.wait()
        for x in range(slab):
            turned[:, x, :] = lateral[x].T

    def each_lateral(act):
        def one(i, carry):
            q, to = i // groups, lax.rem(i, groups)

            @pl.when((takes_lateral == 0) | (to != group))
            def _():
                act(lateral_copy(to, q, 0))
                act(lateral_copy(to, q, 1))

            return carry

        lax.fori_loop(0, PARTS * groups, one, 0)

    def start_axial():
        @pl.when(takes_lateral == 1)
        def _():
            for q in range(PARTS):
                axial_copy(q).start()

        @pl.when(takes_lateral == 0)
        def _():
            axial_in.start()

    def start_lateral():
        each_lateral(lambda copy: copy.start())

        @pl.when(takes_lateral == 1)
        def _():
            observed[:, pl.ds(pl.multiple_of(me * slab, slab), slab), :] = turned[
                pl.ds(group * span, span)
            ]

    def views_arrived(q):
        @pl.when(takes_lateral == 1)
        def _():
            def from_owner(step, carry):
                source = lax.rem(me + step, owners)
                lateral_arrival(source, q, 0).wait_recv()
                lateral_arrival(source, q, 1).wait_recv()
                return carry

            lax.fori_loop(1, owners, from_owner, 0)

            def flip(k, carry):
                z = q * depth + k
                observed[z] = observed[z].T
                observed[planes + z] = observed[planes + z].T
                return carry

            lax.fori_loop(0, depth, flip, 0)

        @pl.when(takes_lateral == 0)
        def _():
            pl.when(q == 0)(axial_in.wait)
            axial_arrival(q).wait_recv()

    def views_sent():
        each_lateral(lambda copy: copy.wait_send())

        @pl.when(takes_lateral == 1)
        def _():
            for q in range(PARTS):
                axial_copy(q).wait_send()

    def along_z(source, matrix, y, first_row=0):
        both = jnp.concatenate(
            [
                source[pl.ds(first_row + y, 2 * span, stride=lines), :],
                source[pl.ds(first_row + y + 1, 2 * span, stride=lines), :],
            ],
            axis=1,
        )
        high, low = split_bf16(both)
        result = dot32(matrix[...], jnp.concatenate([high, low], axis=0))
        result = result[:span] + result[span:]
        return result[:, :columns], result[:, columns:]

    def along_x(planes_two, matrix):
        high, low = split_bf16(planes_two)
        result = dot32(jnp.concatenate([high, low], axis=1), matrix[...])
        return result[:, :columns] + result[:, columns:]

    def along_y(planes_two, matrix):
        high, low = split_bf16(planes_two)
        result = dot32(matrix[...], jnp.concatenate([high, low], axis=0))
        return result[:lines] + result[lines:]

    def side_by_side(stacked):
        return jnp.concatenate([stacked[:lines], stacked[lines:]], axis=1)

    def stacked_up(beside):
        return jnp.concatenate([beside[:, :columns], beside[:, columns:]], axis=0)

    window_lines = window.reshape(2 * span * lines, columns)
    mid_lines = mid.reshape(span * lines, columns)
    logs_lines = logs.reshape(span * lines, columns)
    quot_lines = quot.reshape(ITERS * 2 * span * lines, columns)

    def forward_z(c):
        def lines_of(i, carry):
            for step in range(4):
                y = c * chunk_lines + i * 8 + 2 * step
                one, two = along_z(window_lines, z_fwd, y)
                mid_lines[pl.ds(y, span, stride=lines), :] = one
                mid_lines[pl.ds(y + 1, span, stride=lines), :] = two
            return carry

        lax.fori_loop(0, chunk_lines // 8, lines_of, 0)

    def plane_pair(iteration, z):
        blurred = along_x(mid[pl.ds(z, 2)].reshape(2 * lines, columns), x_fwd)
        blurred = along_y(side_by_side(blurred), y_fwd)
        seen = jnp.concatenate([observed[z], observed[z + 1]], axis=1)
        back = along_y(seen / blurred, y_back)
        back = along_x(stacked_up(back), x_back)
        quot[pl.ds(iteration * 2 * span + planes + z, 2)] = back.reshape(2, lines, columns)

    early = CHUNKS // 2
    steps = planes // 2

    def edge(iteration, index, up, plane, count, lines_at):
        start_plane = (2 * planes if up else planes) + plane
        end_plane = (0 if up else 3 * planes) + plane
        way = 1 if up else 0
        return pltpu.make_async_remote_copy(
            src_ref=quot.at[pl.ds(iteration * 2 * span + start_plane, count), lines_at],
            dst_ref=quot.at[pl.ds(iteration * 2 * span + end_plane, count), lines_at],
            send_sem=edge_sem.at[0, iteration, way, index],
            recv_sem=edge_sem.at[1, iteration, way, index],
            device_id=(me + 2 if up else me - 2, view),
            device_id_type=MESH,
        )

    def early_edge(iteration, s, up):
        return edge(iteration, s, up, 2 * s, 2, pl.ds(0, early * chunk_lines))

    def late_edge(iteration, c, up):
        return edge(iteration, steps + c - early, up, 0, planes, chunk(c))

    def middle(iteration):
        def step(s, carry):
            plane_pair(iteration, 2 * s)
            plane_pair(iteration, planes + 2 * s)
            pl.when(has_below)(early_edge(iteration, s, False).start)
            pl.when(has_above)(early_edge(iteration, s, True).start)
            return carry

        def part_of(q, carry):
            pl.when(iteration == 0)(lambda: views_arrived(q))
            return lax.fori_loop(q * (steps // PARTS), (q + 1) * (steps // PARTS), step, carry)

        lax.fori_loop(0, PARTS, part_of, 0)
        for c in range(early, CHUNKS):
            pl.when(has_below)(late_edge(iteration, c, False).start)
            pl.when(has_above)(late_edge(iteration, c, True).start)

    def run(body):
        lax.fori_loop(0, steps, body, 0)

    def edges_arrived(iteration, c):
        def finish(s, carry):
            pl.when(has_above)(early_edge(iteration, s, False).wait_recv)
            pl.when(has_below)(early_edge(iteration, s, True).wait_recv)
            return carry

        pl.when(c == 0)(lambda: run(finish))
        pl.when((c >= early) & has_above)(lambda: late_edge(iteration, c, False).wait_recv())
        pl.when((c >= early) & has_below)(lambda: late_edge(iteration, c, True).wait_recv())

    def edges_sent(iteration):
        def finish(s, carry):
            pl.when(has_below)(early_edge(iteration, s, False).wait_send)
            pl.when(has_above)(early_edge(iteration, s, True).wait_send)
            return carry

        lax.fori_loop(0, steps, finish, 0)
        for c in range(early, CHUNKS):
            pl.when(has_below)(late_edge(iteration, c, False).wait_send)
            pl.when(has_above)(late_edge(iteration, c, True).wait_send)

    def backward_z(iteration, c):
        first_row = iteration * 2 * span * lines

        def lines_of(i, carry):
            for part_ in range(4):
                y = c * chunk_lines + i * 8 + 2 * part_
                for step, back in enumerate(along_z(quot_lines, z_back, y, first_row)):
                    value = jnp.log(back) - (log_z[...] + log_xy[pl.ds(y + step, 1), :])
                    logs_lines[pl.ds(y + step, span, stride=lines), :] = weight[...] * value
            return carry

        lax.fori_loop(0, chunk_lines // 8, lines_of, 0)

    kinds = [(1, 1), (1, 0), (0, 1), (0, 0)]

    def log_block(kind, core_):
        side_ = lax.rem(side + kind[0], 2)
        row_ = lax.rem(row + kind[1], 2)
        return pl.ds((views * side_ + 2 * row_ + core_) * block, block)

    def to_sibling(iteration, c, k):
        return pltpu.make_async_remote_copy(
            src_ref=logs.at[log_block(kinds[k], 1 - core), chunk(c)],
            dst_ref=pair_sum.at[iteration, k, :, chunk(c)],
            send_sem=pair_sem.at[0, iteration, c, k],
            recv_sem=pair_sem.at[1, iteration, c, k],
            device_id=sibling,
            device_id_type=MESH,
        )

    def to_peer(iteration, c, k):
        side_ = lax.rem(side + kinds[k][0], 2)
        row_ = lax.rem(row + kinds[k][1], 2)
        return pltpu.make_async_remote_copy(
            src_ref=logs.at[log_block(kinds[k], core), chunk(c)],
            dst_ref=peer_sum.at[iteration, k, :, chunk(c)],
            send_sem=peer_sem.at[0, iteration, c, k],
            recv_sem=peer_sem.at[1, iteration, c, k],
            device_id=device(side_, 2 * row_ + core),
            device_id_type=MESH,
        )

    def correct(iteration, c):
        edges_arrived(iteration, c)
        backward_z(iteration, c)
        for k in range(4):
            to_sibling(iteration, c, k).start()

    def reduce_pair(iteration, c):
        for k in range(4):
            to_sibling(iteration, c, k).wait_recv()
            mine = log_block(kinds[k], core)
            logs[mine, chunk(c)] = logs[mine, chunk(c)] + pair_sum[iteration, k, :, chunk(c)]
            if k < 3:
                to_peer(iteration, c, k).start()

    def update(iteration, made, c):
        for k in (1, 2, 0):
            to_peer(iteration, c, k).wait_recv()
        count = jnp.sum(cover_ref[...], axis=0, keepdims=True)
        total = logs[log_block((0, 0), core), chunk(c)]
        for k in range(3):
            total = total + peer_sum[iteration, k, :, chunk(c)]
        here = pl.ds(own * block, block)
        window[here, chunk(c)] = window[here, chunk(c)] * jnp.exp(total / count[None])
        start_all(iteration + 1, c, made[0])

    def sums_sent(iteration, c):
        for k in range(4):
            to_sibling(iteration, c, k).wait_send()
        for k in range(3):
            to_peer(iteration, c, k).wait_send()

    def pipeline(stages):
        def turn_of(t, carry):
            for lag, stage in enumerate(stages):
                c = t - lag
                pl.when((c >= 0) & (c < CHUNKS))(functools.partial(stage, c))
            return carry

        lax.fori_loop(0, CHUNKS + len(stages) - 1, turn_of, 0)

    def initial():
        made = plan(True, yes)

        def begin(c, carry):
            start_all(0, c, made[0])
            return carry

        lax.fori_loop(0, CHUNKS, begin, 0)
        start_axial()
        turn()
        start_lateral()
        prepare()

        def settle(c):
            spread_done(0, c, made)
            forward_z(c)

        pipeline(
            [lambda c: send_on(0, c, made[1]), lambda c: send_on(0, c, made[2]), settle]
        )

    def one_pass(iteration, carry):
        more = iteration < ITERS - 1
        made = plan(False, more)
        stage = iteration + 1
        middle(iteration)

        def settle(c):
            spread_done(stage, c, made)

            @pl.when(more)
            def _():
                forward_z(c)

            @pl.when(iteration == ITERS - 1)
            def _():
                out_ref[:, chunk(c)] = window[own_planes, chunk(c)]

        pipeline(
            [
                lambda c: correct(iteration, c),
                lambda c: reduce_pair(iteration, c),
                lambda c: update(iteration, made, c),
                lambda c: send_on(stage, c, made[1]),
                lambda c: send_on(stage, c, made[2]),
                settle,
            ]
        )
        edges_sent(iteration)

        def finish(c, carry_):
            sums_sent(iteration, c)
            return carry_

        return lax.fori_loop(0, CHUNKS, finish, carry)

    initial()
    cover_copy.wait_send()
    remote(cover.at[1 - side], cover.at[1 - side], cover_sem, 0, sibling).wait_recv()
    which = takes_lateral * views + view
    weight[:planes, :] = jnp.broadcast_to(cover[0, pl.ds(which, 1), :], (planes, columns))
    weight[planes:, :] = jnp.broadcast_to(cover[1, pl.ds(which, 1), :], (planes, columns))
    lax.fori_loop(0, ITERS, one_pass, 0)
    views_sent()


def joint(estimate, axial_views, lateral_views, psf_axial, psf_lateral, coverage):
    planes, lines, columns = estimate.shape
    owners = lax.axis_size("owner")
    views = lax.axis_size("view")
    slab = columns // owners
    span = 2 * planes
    depth = owners * planes
    block = planes // views
    takes_lateral = (lax.axis_index("owner") + lax.axis_index("view")) % 2 == 1
    psf = jnp.where(takes_lateral, psf_lateral[0], psf_axial[0])
    psf = psf / jnp.sum(psf, axis=-1, keepdims=True)
    cover = jnp.repeat(coverage[0].astype(F32).T, columns // coverage.shape[1], axis=1)
    vmem = pl.BlockSpec(memory_space=pltpu.VMEM)
    hbm = pl.BlockSpec(memory_space=pl.ANY)
    dma = pltpu.SemaphoreType.DMA
    result = pl.pallas_call(
        functools.partial(joint_kernel, owners, views, planes, lines, columns),
        out_shape=jax.ShapeDtypeStruct((planes, lines, columns), F32),
        in_specs=[pl.BlockSpec(memory_space=pltpu.SMEM)] + [hbm] * 3 + [vmem],
        out_specs=vmem,
        scratch_shapes=[
            pltpu.VMEM((2 * span, lines, columns), F32),
            pltpu.VMEM((span, lines, columns), F32),
            pltpu.VMEM((slab, lines, depth), F32),
            pltpu.VMEM((depth, slab, lines), F32),
            pltpu.VMEM((span, lines, columns), F32),
            pltpu.VMEM((ITERS * 2 * span, lines, columns), F32),
            pltpu.VMEM((span, lines, columns), F32),
            pltpu.VMEM((ITERS, 4, block, lines, columns), F32),
            pltpu.VMEM((ITERS, 3, block, lines, columns), F32),
            pltpu.VMEM((2,) + cover.shape, F32),
            pltpu.VMEM((2 * columns, 2 * columns), BF16),
            pltpu.VMEM((2 * columns, 2 * columns), BF16),
            pltpu.VMEM((2 * lines, 2 * lines), BF16),
            pltpu.VMEM((2 * lines, 2 * lines), BF16),
            pltpu.VMEM((2 * span, 4 * span), BF16),
            pltpu.VMEM((2 * span, 4 * span), BF16),
            pltpu.VMEM((lines, columns), F32),
            pltpu.VMEM((span, columns), F32),
            pltpu.VMEM((span, columns), F32),
            dma((2, 1)),
            dma((2, PARTS)),
            dma((2, owners, PARTS, 2)),
            dma((2, ITERS, 2, planes // 2 + CHUNKS)),
            dma((2, ITERS + 1, CHUNKS, 4 * views)),
            dma((2, ITERS, CHUNKS, 4)),
            dma((2, ITERS, CHUNKS, 4)),
            dma((3,)),
        ],
        compiler_params=pltpu.CompilerParams(
            collective_id=0, has_side_effects=True, vmem_limit_bytes=48 * 1024 * 1024
        ),
    )(
        psf.reshape(-1),
        estimate,
        axial_views[0],
        lateral_views[0],
        cover,
    )
    return result


def chosen(estimate, axial_views, lateral_views, psf_axial, psf_lateral, coverage):
    planes, lines, columns = estimate.shape
    owners = lax.axis_size("owner")
    views = lax.axis_size("view")
    rim = (psf_axial.shape[-1] - 1) // 2
    fits = (
        lines == columns
        and columns % 128 == 0
        and planes * lines * columns * 4 <= 1024 * 1024
        and planes * owners == columns
        and axial_views.shape[0] == 1
        and lateral_views.shape[0] == 1
        and views == 4
        and owners % 2 == 0
        and planes % views == 0
        and planes % (2 * PARTS) == 0
        and rim <= planes
        and columns // owners % 8 == 0
        and lines % (8 * CHUNKS) == 0
    )
    body = joint if fits else local
    return body(estimate, axial_views, lateral_views, psf_axial, psf_lateral, coverage)


def solution(mesh):
    in_specs = (
        P("owner", None, None),
        P("view", "owner", None, None),
        P("view", "owner", None, None),
        P("view", None, None),
        P("view", None, None),
        P("owner", None, None),
    )
    out_specs = P("owner", None, None)
    return jax.shard_map(chosen, mesh=mesh, in_specs=in_specs, out_specs=out_specs, check_vma=False)
```

```python
import functools

import jax
import jax.numpy as jnp
from jax import lax
from jax.experimental import pallas as pl
from jax.experimental.pallas import tpu as pltpu
from jax.sharding import PartitionSpec as P

VA = 4
ITERS = 2


PRECISE = lax.Precision.HIGHEST


def extended(shard, sides, width):
    for axis, dim in sides:
        peers, length = (lax.axis_size(axis), shard.shape[dim])
        up = [(i, (i + 1) % peers) for i in range(peers - 1)]
        down = [(j, i) for i, j in up]
        last = lax.slice_in_dim(shard, length - width, length, axis=dim)
        leading = lax.slice_in_dim(shard, 0, width, axis=dim)
        before = lax.ppermute(last, axis, up)
        after = lax.ppermute(leading, axis, down)
        shard = jnp.concatenate([before, shard, after], axis=dim)
    return shard


def band_matrix(kernel, block_width):
    rim_width = (kernel.shape[-1] - 1) // 2
    row_index = jnp.arange(block_width + 2 * rim_width)[:, None]
    col_index = jnp.arange(block_width)[None, :]
    matches = (row_index - col_index)[:, :, None] == jnp.arange(kernel.shape[-1])[None, None, :]
    return jnp.sum(jnp.where(matches[None], kernel[:, None, None, :], 0.0), axis=-1)


def middle_matrix(kernel, length):
    rim_width = (kernel.shape[-1] - 1) // 2
    row_index = jnp.arange(length)[:, None]
    col_index = jnp.arange(length)[None, :]
    matches = (row_index - col_index + rim_width)[:, :, None] == jnp.arange(kernel.shape[-1])[
        None, None, :
    ]
    return jnp.sum(jnp.where(matches[None], kernel[:, None, None, :], 0.0), axis=-1)


def along_last(volume, kernel):
    rim_width = (kernel.shape[-1] - 1) // 2
    length = volume.shape[-1]
    block_width = min(128, length)
    blocks = volume.reshape(volume.shape[:-1] + (length // block_width, block_width))
    zero_rim = jnp.zeros(blocks.shape[:-2] + (1, rim_width), volume.dtype)
    left_rim = jnp.concatenate([zero_rim, blocks[..., :-1, block_width - rim_width :]], axis=-2)
    right_rim = jnp.concatenate([blocks[..., 1:, :rim_width], zero_rim], axis=-2)
    windows = jnp.concatenate([left_rim, blocks, right_rim], axis=-1)
    result = jnp.einsum(
        "vabns,vsi->vabni", windows, band_matrix(kernel, block_width), precision=PRECISE
    )
    return result.reshape(volume.shape)


def forward(padded, kernel_first, kernel_mid, kernel_last):
    plane_count = padded.shape[0] - (kernel_first.shape[-1] - 1)
    result = jnp.einsum(
        "syl,vsi->viyl", padded, band_matrix(kernel_first, plane_count), precision=PRECISE
    )
    result = jnp.einsum(
        "viyl,vyk->vikl", result, middle_matrix(kernel_mid, result.shape[2]), precision=PRECISE
    )
    return along_last(result, kernel_last)


def backward(padded, kernel_first, kernel_mid, kernel_last):
    plane_count = padded.shape[1] - (kernel_first.shape[-1] - 1)
    result = jnp.einsum(
        "vsyl,vsi->viyl", padded, band_matrix(kernel_first, plane_count), precision=PRECISE
    )
    result = jnp.einsum(
        "viyl,vyk->vikl", result, middle_matrix(kernel_mid, result.shape[2]), precision=PRECISE
    )
    return along_last(result, kernel_last)


def edge_weights(kernel, positions, length):
    rim_width = (kernel.shape[-1] - 1) // 2
    source = positions[:, None] + jnp.arange(kernel.shape[-1])[None, :] - rim_width
    inside = (source >= 0) & (source < length)
    return jnp.sum(jnp.where(inside[None], kernel[:, None, :], 0.0), axis=-1)


def log_correction(padded, kernel_first, kernel_mid, kernel_last, first_start, first_total):
    back_sum = backward(padded, kernel_first, kernel_mid, kernel_last)
    plane_count, line_count, column_count = back_sum.shape[1:]
    first_weights = edge_weights(kernel_first, first_start + jnp.arange(plane_count), first_total)
    mid_weights = edge_weights(kernel_mid, jnp.arange(line_count), line_count)
    last_weights = edge_weights(kernel_last, jnp.arange(column_count), column_count)
    scale_sum = (
        first_weights[:, :, None, None]
        * mid_weights[:, None, :, None]
        * last_weights[:, None, None, :]
    )
    return jnp.log(back_sum / scale_sum)


def select_views(covered, view_ids):
    picked = (jnp.arange(covered.shape[-1])[None, :] == view_ids[:, None]).astype(jnp.float32)
    return jnp.einsum("vw,xw->vx", picked, covered, precision=PRECISE)


def slab_logs(padded_estimate, view_data, kernel, flipped, weights, first_start, first_total):
    blurred = forward(padded_estimate, kernel[:, 0], kernel[:, 1], kernel[:, 2])
    quotient = view_data / blurred
    rim_width = (kernel.shape[-1] - 1) // 2
    quotient_padded = extended(quotient, (("owner", 1),), rim_width)
    log_terms = log_correction(
        quotient_padded, flipped[:, 0], flipped[:, 1], flipped[:, 2], first_start, first_total
    )
    return jnp.sum(weights[:, None, None, :] * log_terms, axis=0)


def local(estimate, axial_views, lateral_views, psf_axial, psf_lateral, coverage):
    plane_count, line_count, column_count = estimate.shape
    owners = lax.axis_size("owner")
    slab_index = lax.axis_index("owner")
    view_index = lax.axis_index("view")
    slab_width = column_count // owners
    rim_width = (psf_axial.shape[-1] - 1) // 2
    kernel_axial = psf_axial / jnp.sum(psf_axial, axis=-1, keepdims=True)
    kernel_lateral = psf_lateral / jnp.sum(psf_lateral, axis=-1, keepdims=True)
    flipped_axial = kernel_axial[..., ::-1]
    flipped_lateral = kernel_lateral[..., ::-1]
    block_width = column_count // coverage.shape[1]
    covered = jnp.repeat(coverage[0].astype(jnp.float32), block_width, axis=0)
    cover_count = jnp.sum(covered, axis=-1)
    axial_count = psf_axial.shape[0]
    lateral_count = psf_lateral.shape[0]
    weights_axial = select_views(covered, view_index * axial_count + jnp.arange(axial_count))
    weights_lateral = select_views(
        covered, VA + view_index * lateral_count + jnp.arange(lateral_count)
    )
    plane_start = slab_index * plane_count
    plane_total = plane_count * owners
    moved_views = lateral_views.reshape(
        lateral_count, slab_width, line_count, owners, plane_count
    ).transpose(0, 4, 2, 3, 1)
    lateral_slabs = lax.all_to_all(moved_views, "owner", split_axis=3, concat_axis=4, tiled=True)
    lateral_slabs = lateral_slabs.reshape(lateral_count, plane_count, line_count, column_count)
    view_all = jnp.concatenate([axial_views, lateral_slabs], axis=0)
    kernel_all = jnp.concatenate([kernel_axial, kernel_lateral], axis=0)
    flipped_all = jnp.concatenate([flipped_axial, flipped_lateral], axis=0)
    weights_all = jnp.concatenate([weights_axial, weights_lateral], axis=0)
    for iteration in range(ITERS):
        padded_estimate = extended(estimate, (("owner", 0),), rim_width)
        log_total = slab_logs(
            padded_estimate,
            view_all,
            kernel_all,
            flipped_all,
            weights_all,
            plane_start,
            plane_total,
        )
        log_total = lax.psum(log_total, "view")
        estimate = estimate * jnp.exp(log_total / cover_count[None, None, :])
    return estimate


F32 = jnp.float32
BF16 = jnp.bfloat16
MESH = pl.DeviceIdType.MESH
CHUNKS = 4
PARTS = 2
EDGE = 4
GROUP = 8


def split_bf16(values):
    high = values.astype(BF16)
    low = (values - high.astype(F32)).astype(BF16)
    return high, low


def dot32(left, right):
    return jnp.dot(left, right, preferred_element_type=F32)


def joint_kernel(
    owners,
    views,
    planes,
    lines,
    columns,
    psf_ref,
    estimate_ref,
    axial_ref,
    lateral_ref,
    cover_ref,
    out_ref,
    window,
    observed,
    lateral,
    turned,
    mid,
    quot,
    logs,
    pair_sum,
    peer_sum,
    cover,
    x_fwd,
    x_back,
    y_fwd,
    y_back,
    z_fwd,
    z_back,
    log_xy,
    log_z,
    weight,
    cover_sem,
    axial_sem,
    lateral_sem,
    edge_sem,
    share_sem,
    pair_sem,
    peer_sem,
    local_sem,
):
    taps = psf_ref.shape[0] // 3
    rim = (taps - 1) // 2
    groups = owners // 2
    span = 2 * planes
    block = planes // views
    chunk_lines = lines // CHUNKS
    slab = columns // owners

    me = lax.axis_index("owner")
    view = lax.axis_index("view")
    group = me // 2
    side = lax.rem(me, 2)
    core = lax.rem(view, 2)
    row = view // 2
    takes_lateral = lax.rem(side + core, 2)
    has_below = group > 0
    has_above = group < groups - 1

    def device(side_, view_):
        return (2 * group + side_, view_)

    sibling = device(side, 2 * row + 1 - core)

    barrier = pltpu.get_barrier_semaphore()
    for step in range(1, owners):
        pl.semaphore_signal(
            barrier, inc=1, device_id=(lax.rem(me + step, owners), view), device_id_type=MESH
        )
    for side_ in (side, 1 - side):
        for step in range(1, views):
            pl.semaphore_signal(
                barrier,
                inc=1,
                device_id=device(side_, lax.rem(view + step, views)),
                device_id_type=MESH,
            )
    own_planes = pl.ds(planes + planes * side, planes)
    estimate_in = pltpu.make_async_copy(estimate_ref, window.at[own_planes], local_sem.at[0])
    lateral_in = pltpu.make_async_copy(lateral_ref, lateral, local_sem.at[1])
    estimate_in.start()
    lateral_in.start()
    cover[pl.ds(side, 1)] = cover_ref[...][None]

    def clear(base):
        def plane(z, carry):
            zero = jnp.zeros((lines, columns), F32)
            window[base + z] = zero
            for iteration in range(ITERS):
                quot[iteration * 2 * span + base + z] = zero
            return carry

        lax.fori_loop(0, planes, plane, 0)

    pl.when(group == 0)(lambda: clear(0))
    pl.when(group == groups - 1)(lambda: clear(3 * planes))

    estimate_in.wait()
    pl.semaphore_wait(barrier, owners - 1 + 2 * (views - 1))

    def remote(src, dst, sems, index, target):
        return pltpu.make_async_remote_copy(
            src_ref=src,
            dst_ref=dst,
            send_sem=sems.at[0, index],
            recv_sem=sems.at[1, index],
            device_id=target,
            device_id_type=MESH,
        )

    def chunk(c):
        return pl.ds(pl.multiple_of(c * chunk_lines, chunk_lines), chunk_lines)

    def part(e, c):
        return window.at[pl.ds(e * block, block), chunk(c)]

    def slot_of(side_, row_, core_):
        return views + views * side_ + 2 * row_ + core_

    def copy_part(stage, c, e_src, e_dst, slot, target):
        return pltpu.make_async_remote_copy(
            src_ref=part(e_src, c),
            dst_ref=part(e_dst, c),
            send_sem=share_sem.at[0, stage, c, slot],
            recv_sem=share_sem.at[1, stage, c, e_dst],
            device_id=target,
            device_id_type=MESH,
        )

    def arrival(stage, c, e):
        return copy_part(stage, c, e, e, 0, sibling)

    own = slot_of(side, row, core)
    row_peer = device(side, 2 * (1 - row) + core)
    side_peer = device(1 - side, view)
    far_peer = device(1 - side, 2 * (1 - row) + core)
    other = 1 - core
    yes = group >= 0

    def block_of(kind):
        side_ = lax.rem(side + kind[0], 2)
        row_ = lax.rem(row + kind[1], 2)
        return side_, slot_of(side_, row_, core)

    def beside(more, kind):
        side_, e = block_of(kind)
        to = group + 2 * side_ - 1
        valid = (to >= 0) & (to < groups) & more
        e_dst = e + (1 - 3 * side_) * views + (1 - side_) * views
        return valid, e, e_dst, 4 + 2 * kind[0] + kind[1], (2 * to + side, view)

    def plan(first, more):
        if first:
            at_once = [(yes, own, own, 0, side_peer), beside(yes, (0, 0)), beside(yes, (0, 1))]
        else:
            at_once = [
                (more, own, own, 0, side_peer),
                (yes, own, own, 1, row_peer),
                (yes, own, own, 2, sibling),
                (more, own, own, 3, far_peer),
                beside(more, (0, 0)),
            ]
        group_steps = []
        for kind in [(1, 0), (1, 1)] if first else [(0, 1), (1, 0), (1, 1)]:
            e = block_of(kind)[1]
            when = yes if kind == (0, 1) else more
            onward = [beside(more, kind), (when, e, e, 8 + 2 * kind[0] + kind[1], sibling)]
            if first and kind == (1, 0):
                onward.append((yes, e, e, 3, row_peer))
            group_steps.append((when, e, onward))
        beside_steps = []
        rest = []
        for row_ in (0, 1):
            for k, base, condition in ((0, 0, has_below), (1, 3 * views, has_above)):
                e = base + 2 * row_ + core
                onward = [(condition & more, e, e, 12 + 2 * row_ + k, sibling)]
                beside_steps.append((condition & more, e, onward))
                rest.append((condition & more, base + 2 * row_ + other))
            if not first:
                rest.append((yes, slot_of(side, row_, other)))
            rest.append((more, slot_of(1 - side, row_, other)))
        return at_once, group_steps, beside_steps, rest

    def start_all(stage, c, sends):
        for condition, *where in sends:
            pl.when(condition)(copy_part(stage, c, *where).start)

    def send_on(stage, c, steps_):
        for condition, e, onward in steps_:
            pl.when(condition)(arrival(stage, c, e).wait_recv)
            start_all(stage, c, onward)

    def spread_done(stage, c, made):
        at_once, group_steps, beside_steps, rest = made
        for condition, e in rest:
            pl.when(condition)(arrival(stage, c, e).wait_recv)
        onwards = [onward for _, _, onward in group_steps + beside_steps]
        for condition, *where in sum(onwards, at_once):
            pl.when(condition)(copy_part(stage, c, *where).wait_send)

    def toeplitz(axis, shape, offset, flip):
        first = lax.broadcasted_iota(jnp.int32, shape, 0)
        second = lax.broadcasted_iota(jnp.int32, shape, 1)
        place = (second - first if flip else first - second) + (rim + offset)

        def add(t, total):
            return jnp.where(place == t, psf_ref[axis * taps + t], total)

        return lax.fori_loop(0, taps, add, jnp.zeros(shape, F32))

    def store_right(ref, matrix):
        high, low = split_bf16(matrix)
        top = jnp.concatenate([high, low], axis=1)
        ref[...] = jnp.concatenate([top, top], axis=0)

    def store_left(ref, matrix):
        high, low = split_bf16(matrix)
        ref[...] = jnp.concatenate(
            [jnp.concatenate([high, high], axis=1), jnp.concatenate([low, low], axis=1)], axis=0
        )

    def prepare():
        store_right(x_fwd, toeplitz(2, (columns, columns), 0, False))
        back_x = toeplitz(2, (columns, columns), 0, True)
        store_right(x_back, back_x)
        store_left(y_fwd, toeplitz(1, (lines, lines), 0, True))
        back_y = toeplitz(1, (lines, lines), 0, False)
        store_left(y_back, back_y)
        store_left(z_fwd, toeplitz(0, (span, 2 * span), -planes, True))
        back_z = toeplitz(0, (span, 2 * span), planes, False)
        store_left(z_back, back_z)
        log_xy[...] = jnp.log(jnp.sum(back_y, axis=1, keepdims=True)) + jnp.log(
            jnp.sum(back_x, axis=0, keepdims=True)
        )
        plane = lax.broadcasted_iota(jnp.int32, (span, 2 * span), 1) + (group * span - planes)
        inside = (plane >= 0) & (plane < owners * planes)
        sums = jnp.sum(jnp.where(inside, back_z, 0.0), axis=1, keepdims=True)
        log_z[...] = jnp.broadcast_to(jnp.log(sums), (span, columns))

    cover_copy = remote(cover.at[side], cover.at[side], cover_sem, 0, device(1 - side, view))
    cover_copy.start()
    axial_target = device(core, view)
    axial_mine = pl.ds(side * planes, planes)
    depth = planes // PARTS
    axial_in = pltpu.make_async_copy(axial_ref, observed.at[axial_mine], local_sem.at[2])

    def axial_copy(q):
        return remote(
            axial_ref.at[pl.ds(q * depth, depth)],
            observed.at[pl.ds(side * planes + q * depth, depth)],
            axial_sem,
            q,
            axial_target,
        )

    def axial_arrival(q):
        theirs = observed.at[pl.ds((1 - side) * planes + q * depth, depth)]
        return remote(theirs, theirs, axial_sem, q, sibling)

    def lateral_copy(to, q, half):
        plane = half * planes + q * depth
        return pltpu.make_async_remote_copy(
            src_ref=turned.at[pl.ds(to * span + plane, depth)],
            dst_ref=observed.at[pl.ds(plane, depth), pl.ds(me * slab, slab), :],
            send_sem=lateral_sem.at[0, to, q, half],
            recv_sem=lateral_sem.at[1, me, q, half],
            device_id=(2 * to + 1 - core, view),
            device_id_type=MESH,
        )

    def lateral_arrival(source, q, half):
        there = observed.at[pl.ds(half * planes + q * depth, depth), pl.ds(source * slab, slab), :]
        return pltpu.make_async_remote_copy(
            src_ref=there,
            dst_ref=there,
            send_sem=lateral_sem.at[0, 0, q, half],
            recv_sem=lateral_sem.at[1, source, q, half],
            device_id=sibling,
            device_id_type=MESH,
        )

    def turn():
        lateral_in.wait()
        for x in range(slab):
            turned[:, x, :] = lateral[x].T

    def each_lateral(act):
        def one(i, carry):
            q, to = i // groups, lax.rem(i, groups)

            @pl.when((takes_lateral == 0) | (to != group))
            def _():
                act(lateral_copy(to, q, 0))
                act(lateral_copy(to, q, 1))

            return carry

        lax.fori_loop(0, PARTS * groups, one, 0)

    def start_axial():
        @pl.when(takes_lateral == 1)
        def _():
            for q in range(PARTS):
                axial_copy(q).start()

        @pl.when(takes_lateral == 0)
        def _():
            axial_in.start()

    def start_lateral():
        each_lateral(lambda copy: copy.start())

        @pl.when(takes_lateral == 1)
        def _():
            observed[:, pl.ds(pl.multiple_of(me * slab, slab), slab), :] = turned[
                pl.ds(group * span, span)
            ]

    def views_arrived(q):
        @pl.when(takes_lateral == 1)
        def _():
            def from_owner(step, carry):
                source = lax.rem(me + step, owners)
                lateral_arrival(source, q, 0).wait_recv()
                lateral_arrival(source, q, 1).wait_recv()
                return carry

            lax.fori_loop(1, owners, from_owner, 0)

            def flip(k, carry):
                z = q * depth + k
                observed[z] = observed[z].T
                observed[planes + z] = observed[planes + z].T
                return carry

            lax.fori_loop(0, depth, flip, 0)

        @pl.when(takes_lateral == 0)
        def _():
            pl.when(q == 0)(axial_in.wait)
            axial_arrival(q).wait_recv()

    def views_sent():
        each_lateral(lambda copy: copy.wait_send())

        @pl.when(takes_lateral == 1)
        def _():
            for q in range(PARTS):
                axial_copy(q).wait_send()

    def along_z(source, matrix, y, first_row=0):
        both = jnp.concatenate(
            [
                source[pl.ds(first_row + y, 2 * span, stride=lines), :],
                source[pl.ds(first_row + y + 1, 2 * span, stride=lines), :],
            ],
            axis=1,
        )
        high, low = split_bf16(both)
        result = dot32(matrix[...], jnp.concatenate([high, low], axis=0))
        result = result[:span] + result[span:]
        return result[:, :columns], result[:, columns:]

    def along_x(planes_two, matrix):
        high, low = split_bf16(planes_two)
        result = dot32(jnp.concatenate([high, low], axis=1), matrix[...])
        return result[:, :columns] + result[:, columns:]

    def along_y(planes_two, matrix):
        high, low = split_bf16(planes_two)
        result = dot32(matrix[...], jnp.concatenate([high, low], axis=0))
        return result[:lines] + result[lines:]

    window_lines = window.reshape(2 * span * lines, columns)
    mid_lines = mid.reshape(span * lines, columns)
    logs_lines = logs.reshape(span * lines, columns)
    quot_lines = quot.reshape(ITERS * 2 * span * lines, columns)

    def z_then_x(source, z_matrix, x_matrix, y, first_row=0):
        results = []
        for step in range(0, GROUP, 2):
            results.extend(along_z(source, z_matrix, y + step, first_row))
        return along_x(jnp.concatenate(results, axis=0), x_matrix)

    def forward_z(c):
        def lines_of(i, carry):
            y = c * chunk_lines + i * GROUP
            result = z_then_x(window_lines, z_fwd, x_fwd, y)
            for step in range(GROUP):
                mid_lines[pl.ds(y + step, span, stride=lines), :] = result[
                    step * span : (step + 1) * span
                ]
            return carry

        lax.fori_loop(0, chunk_lines // GROUP, lines_of, 0)

    def plane_pair(iteration, z):
        blurred = along_y(jnp.concatenate([mid[z], mid[z + 1]], axis=1), y_fwd)
        seen = jnp.concatenate([observed[z], observed[z + 1]], axis=1)
        back = along_y(seen / blurred, y_back)
        first = iteration * 2 * span + planes + z
        quot[first] = back[:, :columns]
        quot[first + 1] = back[:, columns:]

    early = CHUNKS // 2
    steps = planes // EDGE

    def edge(iteration, index, up, plane, count, lines_at):
        start_plane = (2 * planes if up else planes) + plane
        end_plane = (0 if up else 3 * planes) + plane
        way = 1 if up else 0
        return pltpu.make_async_remote_copy(
            src_ref=quot.at[pl.ds(iteration * 2 * span + start_plane, count), lines_at],
            dst_ref=quot.at[pl.ds(iteration * 2 * span + end_plane, count), lines_at],
            send_sem=edge_sem.at[0, iteration, way, index],
            recv_sem=edge_sem.at[1, iteration, way, index],
            device_id=(me + 2 if up else me - 2, view),
            device_id_type=MESH,
        )

    def early_edge(iteration, s, up):
        return edge(iteration, s, up, EDGE * s, EDGE, pl.ds(0, early * chunk_lines))

    def late_edge(iteration, c, up):
        return edge(iteration, steps + c - early, up, 0, planes, chunk(c))

    def middle(iteration):
        def step(s, carry):
            for k in range(0, EDGE, 2):
                plane_pair(iteration, EDGE * s + k)
                plane_pair(iteration, planes + EDGE * s + k)
            pl.when(has_below)(early_edge(iteration, s, False).start)
            pl.when(has_above)(early_edge(iteration, s, True).start)
            return carry

        def part_of(q, carry):
            pl.when(iteration == 0)(lambda: views_arrived(q))
            return lax.fori_loop(q * (steps // PARTS), (q + 1) * (steps // PARTS), step, carry)

        lax.fori_loop(0, PARTS, part_of, 0)
        for c in range(early, CHUNKS):
            pl.when(has_below)(late_edge(iteration, c, False).start)
            pl.when(has_above)(late_edge(iteration, c, True).start)

    def run(body):
        lax.fori_loop(0, steps, body, 0)

    def edges_arrived(iteration, c):
        def finish(s, carry):
            pl.when(has_above)(early_edge(iteration, s, False).wait_recv)
            pl.when(has_below)(early_edge(iteration, s, True).wait_recv)
            return carry

        pl.when(c == 0)(lambda: run(finish))
        pl.when((c >= early) & has_above)(lambda: late_edge(iteration, c, False).wait_recv())
        pl.when((c >= early) & has_below)(lambda: late_edge(iteration, c, True).wait_recv())

    def edges_sent(iteration):
        def finish(s, carry):
            pl.when(has_below)(early_edge(iteration, s, False).wait_send)
            pl.when(has_above)(early_edge(iteration, s, True).wait_send)
            return carry

        lax.fori_loop(0, steps, finish, 0)
        for c in range(early, CHUNKS):
            pl.when(has_below)(late_edge(iteration, c, False).wait_send)
            pl.when(has_above)(late_edge(iteration, c, True).wait_send)

    def backward_z(iteration, c):
        first_row = iteration * 2 * span * lines

        def lines_of(i, carry):
            y = c * chunk_lines + i * GROUP
            back = jnp.log(z_then_x(quot_lines, z_back, x_back, y, first_row))
            for step in range(GROUP):
                value = back[step * span : (step + 1) * span]
                value = value - (log_z[...] + log_xy[pl.ds(y + step, 1), :])
                logs_lines[pl.ds(y + step, span, stride=lines), :] = weight[...] * value
            return carry

        lax.fori_loop(0, chunk_lines // GROUP, lines_of, 0)

    kinds = [(1, 1), (1, 0), (0, 1), (0, 0)]

    def log_block(kind, core_):
        side_ = lax.rem(side + kind[0], 2)
        row_ = lax.rem(row + kind[1], 2)
        return pl.ds((views * side_ + 2 * row_ + core_) * block, block)

    def to_sibling(iteration, c, k):
        return pltpu.make_async_remote_copy(
            src_ref=logs.at[log_block(kinds[k], 1 - core), chunk(c)],
            dst_ref=pair_sum.at[iteration, k, :, chunk(c)],
            send_sem=pair_sem.at[0, iteration, c, k],
            recv_sem=pair_sem.at[1, iteration, c, k],
            device_id=sibling,
            device_id_type=MESH,
        )

    def to_peer(iteration, c, k):
        side_ = lax.rem(side + kinds[k][0], 2)
        row_ = lax.rem(row + kinds[k][1], 2)
        return pltpu.make_async_remote_copy(
            src_ref=logs.at[log_block(kinds[k], core), chunk(c)],
            dst_ref=peer_sum.at[iteration, k, :, chunk(c)],
            send_sem=peer_sem.at[0, iteration, c, k],
            recv_sem=peer_sem.at[1, iteration, c, k],
            device_id=device(side_, 2 * row_ + core),
            device_id_type=MESH,
        )

    def correct(iteration, c):
        edges_arrived(iteration, c)
        backward_z(iteration, c)
        for k in range(4):
            to_sibling(iteration, c, k).start()

    def reduce_pair(iteration, c):
        for k in range(4):
            to_sibling(iteration, c, k).wait_recv()
            mine = log_block(kinds[k], core)
            logs[mine, chunk(c)] = logs[mine, chunk(c)] + pair_sum[iteration, k, :, chunk(c)]
            if k < 3:
                to_peer(iteration, c, k).start()

    def update(iteration, made, c):
        for k in (1, 2, 0):
            to_peer(iteration, c, k).wait_recv()
        count = jnp.sum(cover_ref[...], axis=0, keepdims=True)
        total = logs[log_block((0, 0), core), chunk(c)]
        for k in range(3):
            total = total + peer_sum[iteration, k, :, chunk(c)]
        here = pl.ds(own * block, block)
        window[here, chunk(c)] = window[here, chunk(c)] * jnp.exp(total / count[None])
        start_all(iteration + 1, c, made[0])

    def sums_sent(iteration, c):
        for k in range(4):
            to_sibling(iteration, c, k).wait_send()
        for k in range(3):
            to_peer(iteration, c, k).wait_send()

    def pipeline(stages):
        def turn_of(t, carry):
            for lag, stage in enumerate(stages):
                c = t - lag
                pl.when((c >= 0) & (c < CHUNKS))(functools.partial(stage, c))
            return carry

        lax.fori_loop(0, CHUNKS + len(stages) - 1, turn_of, 0)

    def initial():
        made = plan(True, yes)

        def begin(c, carry):
            start_all(0, c, made[0])
            return carry

        lax.fori_loop(0, CHUNKS, begin, 0)
        start_axial()
        turn()
        start_lateral()
        prepare()

        def settle(c):
            spread_done(0, c, made)
            forward_z(c)

        pipeline(
            [lambda c: send_on(0, c, made[1]), lambda c: send_on(0, c, made[2]), settle]
        )

    def one_pass(iteration, carry):
        more = iteration < ITERS - 1
        made = plan(False, more)
        stage = iteration + 1
        middle(iteration)

        def settle(c):
            spread_done(stage, c, made)

            @pl.when(more)
            def _():
                forward_z(c)

            @pl.when(iteration == ITERS - 1)
            def _():
                out_ref[:, chunk(c)] = window[own_planes, chunk(c)]

        pipeline(
            [
                lambda c: correct(iteration, c),
                lambda c: reduce_pair(iteration, c),
                lambda c: update(iteration, made, c),
                lambda c: send_on(stage, c, made[1]),
                lambda c: send_on(stage, c, made[2]),
                settle,
            ]
        )
        edges_sent(iteration)

        def finish(c, carry_):
            sums_sent(iteration, c)
            return carry_

        return lax.fori_loop(0, CHUNKS, finish, carry)

    initial()
    cover_copy.wait_send()
    remote(cover.at[1 - side], cover.at[1 - side], cover_sem, 0, sibling).wait_recv()
    which = takes_lateral * views + view
    weight[:planes, :] = jnp.broadcast_to(cover[0, pl.ds(which, 1), :], (planes, columns))
    weight[planes:, :] = jnp.broadcast_to(cover[1, pl.ds(which, 1), :], (planes, columns))
    lax.fori_loop(0, ITERS, one_pass, 0)
    views_sent()


def joint(estimate, axial_views, lateral_views, psf_axial, psf_lateral, coverage):
    planes, lines, columns = estimate.shape
    owners = lax.axis_size("owner")
    views = lax.axis_size("view")
    slab = columns // owners
    span = 2 * planes
    depth = owners * planes
    block = planes // views
    takes_lateral = (lax.axis_index("owner") + lax.axis_index("view")) % 2 == 1
    psf = jnp.where(takes_lateral, psf_lateral[0], psf_axial[0])
    psf = psf / jnp.sum(psf, axis=-1, keepdims=True)
    cover = jnp.repeat(coverage[0].astype(F32).T, columns // coverage.shape[1], axis=1)
    vmem = pl.BlockSpec(memory_space=pltpu.VMEM)
    hbm = pl.BlockSpec(memory_space=pl.ANY)
    dma = pltpu.SemaphoreType.DMA
    result = pl.pallas_call(
        functools.partial(joint_kernel, owners, views, planes, lines, columns),
        out_shape=jax.ShapeDtypeStruct((planes, lines, columns), F32),
        in_specs=[pl.BlockSpec(memory_space=pltpu.SMEM)] + [hbm] * 3 + [vmem],
        out_specs=vmem,
        scratch_shapes=[
            pltpu.VMEM((2 * span, lines, columns), F32),
            pltpu.VMEM((span, lines, columns), F32),
            pltpu.VMEM((slab, lines, depth), F32),
            pltpu.VMEM((depth, slab, lines), F32),
            pltpu.VMEM((span, lines, columns), F32),
            pltpu.VMEM((ITERS * 2 * span, lines, columns), F32),
            pltpu.VMEM((span, lines, columns), F32),
            pltpu.VMEM((ITERS, 4, block, lines, columns), F32),
            pltpu.VMEM((ITERS, 3, block, lines, columns), F32),
            pltpu.VMEM((2,) + cover.shape, F32),
            pltpu.VMEM((2 * columns, 2 * columns), BF16),
            pltpu.VMEM((2 * columns, 2 * columns), BF16),
            pltpu.VMEM((2 * lines, 2 * lines), BF16),
            pltpu.VMEM((2 * lines, 2 * lines), BF16),
            pltpu.VMEM((2 * span, 4 * span), BF16),
            pltpu.VMEM((2 * span, 4 * span), BF16),
            pltpu.VMEM((lines, columns), F32),
            pltpu.VMEM((span, columns), F32),
            pltpu.VMEM((span, columns), F32),
            dma((2, 1)),
            dma((2, PARTS)),
            dma((2, owners, PARTS, 2)),
            dma((2, ITERS, 2, planes // EDGE + CHUNKS)),
            dma((2, ITERS + 1, CHUNKS, 4 * views)),
            dma((2, ITERS, CHUNKS, 4)),
            dma((2, ITERS, CHUNKS, 4)),
            dma((3,)),
        ],
        compiler_params=pltpu.CompilerParams(
            collective_id=0, has_side_effects=True, vmem_limit_bytes=48 * 1024 * 1024
        ),
    )(
        psf.reshape(-1),
        estimate,
        axial_views[0],
        lateral_views[0],
        cover,
    )
    return result


def chosen(estimate, axial_views, lateral_views, psf_axial, psf_lateral, coverage):
    planes, lines, columns = estimate.shape
    owners = lax.axis_size("owner")
    views = lax.axis_size("view")
    rim = (psf_axial.shape[-1] - 1) // 2
    fits = (
        lines == columns
        and columns % 128 == 0
        and planes * lines * columns * 4 <= 1024 * 1024
        and planes * owners == columns
        and axial_views.shape[0] == 1
        and lateral_views.shape[0] == 1
        and views == 4
        and owners % 2 == 0
        and planes % views == 0
        and planes % (EDGE * PARTS) == 0
        and rim <= planes
        and columns // owners % 8 == 0
        and lines % (GROUP * CHUNKS) == 0
    )
    body = joint if fits else local
    return body(estimate, axial_views, lateral_views, psf_axial, psf_lateral, coverage)


def solution(mesh):
    in_specs = (
        P("owner", None, None),
        P("view", "owner", None, None),
        P("view", "owner", None, None),
        P("view", None, None),
        P("view", None, None),
        P("owner", None, None),
    )
    out_specs = P("owner", None, None)
    return jax.shard_map(chosen, mesh=mesh, in_specs=in_specs, out_specs=out_specs, check_vma=False)
```

```python
import functools

import jax
import jax.numpy as jnp
from jax import lax
from jax.experimental import pallas as pl
from jax.experimental.pallas import tpu as pltpu
from jax.sharding import PartitionSpec as P

VA = 4
ITERS = 2


PRECISE = lax.Precision.HIGHEST


def extended(shard, sides, width):
    for axis, dim in sides:
        peers, length = (lax.axis_size(axis), shard.shape[dim])
        up = [(i, (i + 1) % peers) for i in range(peers - 1)]
        down = [(j, i) for i, j in up]
        last = lax.slice_in_dim(shard, length - width, length, axis=dim)
        leading = lax.slice_in_dim(shard, 0, width, axis=dim)
        before = lax.ppermute(last, axis, up)
        after = lax.ppermute(leading, axis, down)
        shard = jnp.concatenate([before, shard, after], axis=dim)
    return shard


def band_matrix(kernel, block_width):
    rim_width = (kernel.shape[-1] - 1) // 2
    row_index = jnp.arange(block_width + 2 * rim_width)[:, None]
    col_index = jnp.arange(block_width)[None, :]
    matches = (row_index - col_index)[:, :, None] == jnp.arange(kernel.shape[-1])[None, None, :]
    return jnp.sum(jnp.where(matches[None], kernel[:, None, None, :], 0.0), axis=-1)


def middle_matrix(kernel, length):
    rim_width = (kernel.shape[-1] - 1) // 2
    row_index = jnp.arange(length)[:, None]
    col_index = jnp.arange(length)[None, :]
    matches = (row_index - col_index + rim_width)[:, :, None] == jnp.arange(kernel.shape[-1])[
        None, None, :
    ]
    return jnp.sum(jnp.where(matches[None], kernel[:, None, None, :], 0.0), axis=-1)


def along_last(volume, kernel):
    rim_width = (kernel.shape[-1] - 1) // 2
    length = volume.shape[-1]
    block_width = min(128, length)
    blocks = volume.reshape(volume.shape[:-1] + (length // block_width, block_width))
    zero_rim = jnp.zeros(blocks.shape[:-2] + (1, rim_width), volume.dtype)
    left_rim = jnp.concatenate([zero_rim, blocks[..., :-1, block_width - rim_width :]], axis=-2)
    right_rim = jnp.concatenate([blocks[..., 1:, :rim_width], zero_rim], axis=-2)
    windows = jnp.concatenate([left_rim, blocks, right_rim], axis=-1)
    result = jnp.einsum(
        "vabns,vsi->vabni", windows, band_matrix(kernel, block_width), precision=PRECISE
    )
    return result.reshape(volume.shape)


def forward(padded, kernel_first, kernel_mid, kernel_last):
    plane_count = padded.shape[0] - (kernel_first.shape[-1] - 1)
    result = jnp.einsum(
        "syl,vsi->viyl", padded, band_matrix(kernel_first, plane_count), precision=PRECISE
    )
    result = jnp.einsum(
        "viyl,vyk->vikl", result, middle_matrix(kernel_mid, result.shape[2]), precision=PRECISE
    )
    return along_last(result, kernel_last)


def backward(padded, kernel_first, kernel_mid, kernel_last):
    plane_count = padded.shape[1] - (kernel_first.shape[-1] - 1)
    result = jnp.einsum(
        "vsyl,vsi->viyl", padded, band_matrix(kernel_first, plane_count), precision=PRECISE
    )
    result = jnp.einsum(
        "viyl,vyk->vikl", result, middle_matrix(kernel_mid, result.shape[2]), precision=PRECISE
    )
    return along_last(result, kernel_last)


def edge_weights(kernel, positions, length):
    rim_width = (kernel.shape[-1] - 1) // 2
    source = positions[:, None] + jnp.arange(kernel.shape[-1])[None, :] - rim_width
    inside = (source >= 0) & (source < length)
    return jnp.sum(jnp.where(inside[None], kernel[:, None, :], 0.0), axis=-1)


def log_correction(padded, kernel_first, kernel_mid, kernel_last, first_start, first_total):
    back_sum = backward(padded, kernel_first, kernel_mid, kernel_last)
    plane_count, line_count, column_count = back_sum.shape[1:]
    first_weights = edge_weights(kernel_first, first_start + jnp.arange(plane_count), first_total)
    mid_weights = edge_weights(kernel_mid, jnp.arange(line_count), line_count)
    last_weights = edge_weights(kernel_last, jnp.arange(column_count), column_count)
    scale_sum = (
        first_weights[:, :, None, None]
        * mid_weights[:, None, :, None]
        * last_weights[:, None, None, :]
    )
    return jnp.log(back_sum / scale_sum)


def select_views(covered, view_ids):
    picked = (jnp.arange(covered.shape[-1])[None, :] == view_ids[:, None]).astype(jnp.float32)
    return jnp.einsum("vw,xw->vx", picked, covered, precision=PRECISE)


def slab_logs(padded_estimate, view_data, kernel, flipped, weights, first_start, first_total):
    blurred = forward(padded_estimate, kernel[:, 0], kernel[:, 1], kernel[:, 2])
    quotient = view_data / blurred
    rim_width = (kernel.shape[-1] - 1) // 2
    quotient_padded = extended(quotient, (("owner", 1),), rim_width)
    log_terms = log_correction(
        quotient_padded, flipped[:, 0], flipped[:, 1], flipped[:, 2], first_start, first_total
    )
    return jnp.sum(weights[:, None, None, :] * log_terms, axis=0)


def local(estimate, axial_views, lateral_views, psf_axial, psf_lateral, coverage):
    plane_count, line_count, column_count = estimate.shape
    owners = lax.axis_size("owner")
    slab_index = lax.axis_index("owner")
    view_index = lax.axis_index("view")
    slab_width = column_count // owners
    rim_width = (psf_axial.shape[-1] - 1) // 2
    kernel_axial = psf_axial / jnp.sum(psf_axial, axis=-1, keepdims=True)
    kernel_lateral = psf_lateral / jnp.sum(psf_lateral, axis=-1, keepdims=True)
    flipped_axial = kernel_axial[..., ::-1]
    flipped_lateral = kernel_lateral[..., ::-1]
    block_width = column_count // coverage.shape[1]
    covered = jnp.repeat(coverage[0].astype(jnp.float32), block_width, axis=0)
    cover_count = jnp.sum(covered, axis=-1)
    axial_count = psf_axial.shape[0]
    lateral_count = psf_lateral.shape[0]
    weights_axial = select_views(covered, view_index * axial_count + jnp.arange(axial_count))
    weights_lateral = select_views(
        covered, VA + view_index * lateral_count + jnp.arange(lateral_count)
    )
    plane_start = slab_index * plane_count
    plane_total = plane_count * owners
    moved_views = lateral_views.reshape(
        lateral_count, slab_width, line_count, owners, plane_count
    ).transpose(0, 4, 2, 3, 1)
    lateral_slabs = lax.all_to_all(moved_views, "owner", split_axis=3, concat_axis=4, tiled=True)
    lateral_slabs = lateral_slabs.reshape(lateral_count, plane_count, line_count, column_count)
    view_all = jnp.concatenate([axial_views, lateral_slabs], axis=0)
    kernel_all = jnp.concatenate([kernel_axial, kernel_lateral], axis=0)
    flipped_all = jnp.concatenate([flipped_axial, flipped_lateral], axis=0)
    weights_all = jnp.concatenate([weights_axial, weights_lateral], axis=0)
    for iteration in range(ITERS):
        padded_estimate = extended(estimate, (("owner", 0),), rim_width)
        log_total = slab_logs(
            padded_estimate,
            view_all,
            kernel_all,
            flipped_all,
            weights_all,
            plane_start,
            plane_total,
        )
        log_total = lax.psum(log_total, "view")
        estimate = estimate * jnp.exp(log_total / cover_count[None, None, :])
    return estimate


F32 = jnp.float32
BF16 = jnp.bfloat16
MESH = pl.DeviceIdType.MESH
CHUNKS = 4
PARTS = 2
EDGE = 4
GROUP = 8


def split_bf16(values):
    high = values.astype(BF16)
    low = (values - high.astype(F32)).astype(BF16)
    return high, low


def dot32(left, right):
    return jnp.dot(left, right, preferred_element_type=F32)


def joint_kernel(
    owners,
    views,
    planes,
    lines,
    columns,
    psf_ref,
    estimate_ref,
    axial_ref,
    lateral_ref,
    cover_ref,
    out_ref,
    window,
    observed,
    lateral,
    turned,
    mid,
    quot,
    logs,
    pair_sum,
    peer_sum,
    cover,
    x_fwd,
    x_back,
    y_fwd,
    y_back,
    z_fwd,
    z_back,
    log_xy,
    log_z,
    weight,
    cover_sem,
    axial_sem,
    lateral_sem,
    edge_sem,
    share_sem,
    pair_sem,
    peer_sem,
    local_sem,
):
    taps = psf_ref.shape[0] // 3
    rim = (taps - 1) // 2
    groups = owners // 2
    span = 2 * planes
    block = planes // views
    chunk_lines = lines // CHUNKS
    slab = columns // owners

    me = lax.axis_index("owner")
    view = lax.axis_index("view")
    group = me // 2
    side = lax.rem(me, 2)
    core = lax.rem(view, 2)
    row = view // 2
    takes_lateral = lax.rem(side + core, 2)
    has_below = group > 0
    has_above = group < groups - 1

    def device(side_, view_):
        return (2 * group + side_, view_)

    sibling = device(side, 2 * row + 1 - core)

    barrier = pltpu.get_barrier_semaphore()
    for step in range(1, owners):
        pl.semaphore_signal(
            barrier, inc=1, device_id=(lax.rem(me + step, owners), view), device_id_type=MESH
        )
    for side_ in (side, 1 - side):
        for step in range(1, views):
            pl.semaphore_signal(
                barrier,
                inc=1,
                device_id=device(side_, lax.rem(view + step, views)),
                device_id_type=MESH,
            )
    mine = window.at[pl.ds(2 + 2 * side, 2)]
    estimate_in = pltpu.make_async_copy(estimate_ref, mine, local_sem.at[0])
    lateral_in = pltpu.make_async_copy(lateral_ref, lateral, local_sem.at[1])
    window_planes = window.reshape(2 * span, lines, columns)
    estimate_in.start()
    lateral_in.start()
    cover[pl.ds(side, 1)] = cover_ref[...][None]

    def clear(slab_):
        def plane(z, carry):
            zero = jnp.zeros((lines, columns), F32)
            window_planes[slab_ * planes + z] = zero
            for iteration in range(ITERS):
                quot[iteration * 2 * span + slab_ * planes + z] = zero
            return carry

        lax.fori_loop(0, planes, plane, 0)

    pl.when(group == 0)(lambda: clear(0))
    pl.when(group == groups - 1)(lambda: clear(3))

    estimate_in.wait()
    pl.semaphore_wait(barrier, owners - 1 + 2 * (views - 1))

    def remote(src, dst, sems, index, target):
        return pltpu.make_async_remote_copy(
            src_ref=src,
            dst_ref=dst,
            send_sem=sems.at[0, index],
            recv_sem=sems.at[1, index],
            device_id=target,
            device_id_type=MESH,
        )

    def chunk(c):
        return pl.ds(pl.multiple_of(c * chunk_lines, chunk_lines), chunk_lines)

    def part(first, count, core_, c):
        return window.at[pl.ds(first, count), core_, :, chunk(c)]

    def copy_part(stage, c, slot, src, dst, count, target):
        return pltpu.make_async_remote_copy(
            src_ref=part(src, count, core, c),
            dst_ref=part(dst, count, core, c),
            send_sem=share_sem.at[0, stage, c, slot],
            recv_sem=share_sem.at[1, stage, c, slot],
            device_id=target,
            device_id_type=MESH,
        )

    own = 2 + 2 * side + row
    own_side = 2 + 2 * side
    other_side = 4 - 2 * side
    row_peer = device(side, 2 * (1 - row) + core)
    side_peer = device(1 - side, view)
    far_peer = device(1 - side, 2 * (1 - row) + core)
    other = 1 - core
    yes = group >= 0

    def up_copy(more):
        return (has_above & more, 3, 4, 0, 2, (me + 2, view))

    def down_copy(more):
        return (has_below & more, 4, 2, 6, 2, (me - 2, view))

    def plan(first, more):
        x_arrival = (more, 0, 2 + 2 * (1 - side) + row, 1, core)
        y_arrival = (yes, 1, 2 + 2 * side + 1 - row, 1, core)
        far_arrival = (more, 2, 2 + 2 * (1 - side) + 1 - row, 1, core)
        if first:
            near = (has_above & (side == 1), 3, 4, 0, 2, (me + 2, view))
            near_down = (has_below & (side == 0), 4, 2, 6, 2, (me - 2, view))
            at_once = [(yes, 0, own, own, 1, side_peer), near, near_down]
            across = x_arrival[2]
            group_steps = [
                ([x_arrival], [(yes, 2, across, across, 1, row_peer)]),
                (
                    [far_arrival],
                    [
                        (yes, 5, other_side, other_side, 2, sibling),
                        (has_above & (side == 0), 3, 4, 0, 2, (me + 2, view)),
                        (has_below & (side == 1), 4, 2, 6, 2, (me - 2, view)),
                    ],
                ),
            ]
            rest = [(yes, 5, other_side, 2, other)]
        else:
            at_once = [
                (more, 0, own, own, 1, side_peer),
                (yes, 1, own, own, 1, row_peer),
                (more, 2, own, own, 1, far_peer),
            ]
            group_steps = [
                (
                    [y_arrival, x_arrival, far_arrival],
                    [
                        up_copy(more),
                        down_copy(more),
                        (more, 5, 2, 2, 4, sibling),
                        (jnp.logical_not(more), 8, own_side, own_side, 2, sibling),
                    ],
                )
            ]
            rest = [(more, 5, 2, 4, other), (jnp.logical_not(more), 8, own_side, 2, other)]
        beside_steps = [
            ([(has_below & more, 3, 0, 2, core)], [(has_below & more, 6, 0, 0, 2, sibling)]),
            ([(has_above & more, 4, 6, 2, core)], [(has_above & more, 7, 6, 6, 2, sibling)]),
        ]
        rest = rest + [(has_below & more, 6, 0, 2, other), (has_above & more, 7, 6, 2, other)]
        return at_once, group_steps, beside_steps, rest

    def start_all(stage, c, sends):
        for condition, *where in sends:
            pl.when(condition)(copy_part(stage, c, *where).start)

    def await_all(stage, c, arrivals):
        for condition, slot, first, count, core_ in arrivals:
            there = part(first, count, core_, c)
            made = pltpu.make_async_remote_copy(
                src_ref=there,
                dst_ref=there,
                send_sem=share_sem.at[0, stage, c, slot],
                recv_sem=share_sem.at[1, stage, c, slot],
                device_id=sibling,
                device_id_type=MESH,
            )
            pl.when(condition)(made.wait_recv)

    def send_on(stage, c, steps_):
        for arrivals, onward in steps_:
            await_all(stage, c, arrivals)
            start_all(stage, c, onward)

    def spread_done(stage, c, made):
        at_once, group_steps, beside_steps, rest = made
        await_all(stage, c, rest)
        onwards = [onward for _, onward in group_steps + beside_steps]
        for condition, *where in sum(onwards, at_once):
            pl.when(condition)(copy_part(stage, c, *where).wait_send)

    def toeplitz(axis, shape, offset, flip):
        first = lax.broadcasted_iota(jnp.int32, shape, 0)
        second = lax.broadcasted_iota(jnp.int32, shape, 1)
        place = (second - first if flip else first - second) + (rim + offset)

        def add(t, total):
            return jnp.where(place == t, psf_ref[axis * taps + t], total)

        return lax.fori_loop(0, taps, add, jnp.zeros(shape, F32))

    def store_right(ref, matrix):
        high, low = split_bf16(matrix)
        top = jnp.concatenate([high, low], axis=1)
        ref[...] = jnp.concatenate([top, top], axis=0)

    def store_left(ref, matrix):
        high, low = split_bf16(matrix)
        ref[...] = jnp.concatenate(
            [jnp.concatenate([high, high], axis=1), jnp.concatenate([low, low], axis=1)], axis=0
        )

    def prepare():
        store_right(x_fwd, toeplitz(2, (columns, columns), 0, False))
        back_x = toeplitz(2, (columns, columns), 0, True)
        store_right(x_back, back_x)
        store_left(y_fwd, toeplitz(1, (lines, lines), 0, True))
        back_y = toeplitz(1, (lines, lines), 0, False)
        store_left(y_back, back_y)
        store_left(z_fwd, toeplitz(0, (span, 2 * span), -planes, True))
        back_z = toeplitz(0, (span, 2 * span), planes, False)
        store_left(z_back, back_z)
        log_xy[...] = jnp.log(jnp.sum(back_y, axis=1, keepdims=True)) + jnp.log(
            jnp.sum(back_x, axis=0, keepdims=True)
        )
        plane = lax.broadcasted_iota(jnp.int32, (span, 2 * span), 1) + (group * span - planes)
        inside = (plane >= 0) & (plane < owners * planes)
        sums = jnp.sum(jnp.where(inside, back_z, 0.0), axis=1, keepdims=True)
        log_z[...] = jnp.broadcast_to(jnp.log(sums), (span, columns))

    cover_copy = remote(cover.at[side], cover.at[side], cover_sem, 0, device(1 - side, view))
    cover_copy.start()
    axial_target = device(core, view)
    axial_mine = pl.ds(side * planes, planes)
    depth = planes // PARTS
    axial_in = pltpu.make_async_copy(axial_ref, observed.at[axial_mine], local_sem.at[2])

    def axial_copy(q):
        return remote(
            axial_ref.at[pl.ds(q * depth, depth)],
            observed.at[pl.ds(side * planes + q * depth, depth)],
            axial_sem,
            q,
            axial_target,
        )

    def axial_arrival(q):
        theirs = observed.at[pl.ds((1 - side) * planes + q * depth, depth)]
        return remote(theirs, theirs, axial_sem, q, sibling)

    def lateral_copy(to, q, half):
        plane = half * planes + q * depth
        return pltpu.make_async_remote_copy(
            src_ref=turned.at[pl.ds(to * span + plane, depth)],
            dst_ref=observed.at[pl.ds(plane, depth), pl.ds(me * slab, slab), :],
            send_sem=lateral_sem.at[0, to, q, half],
            recv_sem=lateral_sem.at[1, me, q, half],
            device_id=(2 * to + 1 - core, view),
            device_id_type=MESH,
        )

    def lateral_arrival(source, q, half):
        there = observed.at[pl.ds(half * planes + q * depth, depth), pl.ds(source * slab, slab), :]
        return pltpu.make_async_remote_copy(
            src_ref=there,
            dst_ref=there,
            send_sem=lateral_sem.at[0, 0, q, half],
            recv_sem=lateral_sem.at[1, source, q, half],
            device_id=sibling,
            device_id_type=MESH,
        )

    def turn():
        lateral_in.wait()
        for x in range(slab):
            turned[:, x, :] = lateral[x].T

    def each_lateral(act):
        def one(i, carry):
            q, to = i // groups, lax.rem(i, groups)

            @pl.when((takes_lateral == 0) | (to != group))
            def _():
                act(lateral_copy(to, q, 0))
                act(lateral_copy(to, q, 1))

            return carry

        lax.fori_loop(0, PARTS * groups, one, 0)

    def start_axial():
        @pl.when(takes_lateral == 1)
        def _():
            for q in range(PARTS):
                axial_copy(q).start()

        @pl.when(takes_lateral == 0)
        def _():
            axial_in.start()

    def start_lateral():
        each_lateral(lambda copy: copy.start())

        @pl.when(takes_lateral == 1)
        def _():
            observed[:, pl.ds(pl.multiple_of(me * slab, slab), slab), :] = turned[
                pl.ds(group * span, span)
            ]

    def views_arrived(q):
        @pl.when(takes_lateral == 1)
        def _():
            def from_owner(step, carry):
                source = lax.rem(me + step, owners)
                lateral_arrival(source, q, 0).wait_recv()
                lateral_arrival(source, q, 1).wait_recv()
                return carry

            lax.fori_loop(1, owners, from_owner, 0)

            def flip(k, carry):
                z = q * depth + k
                observed[z] = observed[z].T
                observed[planes + z] = observed[planes + z].T
                return carry

            lax.fori_loop(0, depth, flip, 0)

        @pl.when(takes_lateral == 0)
        def _():
            pl.when(q == 0)(axial_in.wait)
            axial_arrival(q).wait_recv()

    def views_sent():
        each_lateral(lambda copy: copy.wait_send())

        @pl.when(takes_lateral == 1)
        def _():
            for q in range(PARTS):
                axial_copy(q).wait_send()

    def along_z(source, matrix, y, first_row=0):
        both = jnp.concatenate(
            [
                source[pl.ds(first_row + y, 2 * span, stride=lines), :],
                source[pl.ds(first_row + y + 1, 2 * span, stride=lines), :],
            ],
            axis=1,
        )
        high, low = split_bf16(both)
        result = dot32(matrix[...], jnp.concatenate([high, low], axis=0))
        result = result[:span] + result[span:]
        return result[:, :columns], result[:, columns:]

    def along_x(planes_two, matrix):
        high, low = split_bf16(planes_two)
        result = dot32(jnp.concatenate([high, low], axis=1), matrix[...])
        return result[:, :columns] + result[:, columns:]

    def along_y(planes_two, matrix):
        high, low = split_bf16(planes_two)
        result = dot32(matrix[...], jnp.concatenate([high, low], axis=0))
        return result[:lines] + result[lines:]

    window_lines = window.reshape(2 * span * lines, columns)
    mid_lines = mid.reshape(span * lines, columns)
    logs_lines = logs.reshape(span * lines, columns)
    quot_lines = quot.reshape(ITERS * 2 * span * lines, columns)

    def z_then_x(source, z_matrix, x_matrix, y, first_row=0):
        results = []
        for step in range(0, GROUP, 2):
            results.extend(along_z(source, z_matrix, y + step, first_row))
        return along_x(jnp.concatenate(results, axis=0), x_matrix)

    def forward_z(c):
        def lines_of(i, carry):
            y = c * chunk_lines + i * GROUP
            result = z_then_x(window_lines, z_fwd, x_fwd, y)
            for step in range(GROUP):
                mid_lines[pl.ds(y + step, span, stride=lines), :] = result[
                    step * span : (step + 1) * span
                ]
            return carry

        lax.fori_loop(0, chunk_lines // GROUP, lines_of, 0)

    def plane_pair(iteration, z):
        blurred = along_y(jnp.concatenate([mid[z], mid[z + 1]], axis=1), y_fwd)
        seen = jnp.concatenate([observed[z], observed[z + 1]], axis=1)
        back = along_y(seen / blurred, y_back)
        first = iteration * 2 * span + planes + z
        quot[first] = back[:, :columns]
        quot[first + 1] = back[:, columns:]

    early = CHUNKS // 2
    steps = planes // EDGE

    def edge(iteration, index, up, plane, count, lines_at):
        start_plane = (2 * planes if up else planes) + plane
        end_plane = (0 if up else 3 * planes) + plane
        way = 1 if up else 0
        return pltpu.make_async_remote_copy(
            src_ref=quot.at[pl.ds(iteration * 2 * span + start_plane, count), lines_at],
            dst_ref=quot.at[pl.ds(iteration * 2 * span + end_plane, count), lines_at],
            send_sem=edge_sem.at[0, iteration, way, index],
            recv_sem=edge_sem.at[1, iteration, way, index],
            device_id=(me + 2 if up else me - 2, view),
            device_id_type=MESH,
        )

    def early_edge(iteration, s, up):
        return edge(iteration, s, up, EDGE * s, EDGE, pl.ds(0, early * chunk_lines))

    def late_edge(iteration, c, up):
        return edge(iteration, steps + c - early, up, 0, planes, chunk(c))

    def middle(iteration):
        def step(s, carry):
            for k in range(0, EDGE, 2):
                plane_pair(iteration, EDGE * s + k)
                plane_pair(iteration, planes + EDGE * s + k)
            pl.when(has_below)(early_edge(iteration, s, False).start)
            pl.when(has_above)(early_edge(iteration, s, True).start)
            return carry

        def part_of(q, carry):
            pl.when(iteration == 0)(lambda: views_arrived(q))
            return lax.fori_loop(q * (steps // PARTS), (q + 1) * (steps // PARTS), step, carry)

        lax.fori_loop(0, PARTS, part_of, 0)
        for c in range(early, CHUNKS):
            pl.when(has_below)(late_edge(iteration, c, False).start)
            pl.when(has_above)(late_edge(iteration, c, True).start)

    def run(body):
        lax.fori_loop(0, steps, body, 0)

    def edges_arrived(iteration, c):
        def finish(s, carry):
            pl.when(has_above)(early_edge(iteration, s, False).wait_recv)
            pl.when(has_below)(early_edge(iteration, s, True).wait_recv)
            return carry

        pl.when(c == 0)(lambda: run(finish))
        pl.when((c >= early) & has_above)(lambda: late_edge(iteration, c, False).wait_recv())
        pl.when((c >= early) & has_below)(lambda: late_edge(iteration, c, True).wait_recv())

    def edges_sent(iteration):
        def finish(s, carry):
            pl.when(has_below)(early_edge(iteration, s, False).wait_send)
            pl.when(has_above)(early_edge(iteration, s, True).wait_send)
            return carry

        lax.fori_loop(0, steps, finish, 0)
        for c in range(early, CHUNKS):
            pl.when(has_below)(late_edge(iteration, c, False).wait_send)
            pl.when(has_above)(late_edge(iteration, c, True).wait_send)

    def backward_z(iteration, c):
        first_row = iteration * 2 * span * lines

        def lines_of(i, carry):
            y = c * chunk_lines + i * GROUP
            back = jnp.log(z_then_x(quot_lines, z_back, x_back, y, first_row))
            for step in range(GROUP):
                value = back[step * span : (step + 1) * span]
                value = value - (log_z[...] + log_xy[pl.ds(y + step, 1), :])
                logs_lines[pl.ds(y + step, span, stride=lines), :] = weight[...] * value
            return carry

        lax.fori_loop(0, chunk_lines // GROUP, lines_of, 0)

    kinds = [(1, 1), (1, 0), (0, 1)]

    def to_sibling(iteration, c):
        return pltpu.make_async_remote_copy(
            src_ref=logs.at[:, other, :, chunk(c)],
            dst_ref=pair_sum.at[iteration, :, :, chunk(c)],
            send_sem=pair_sem.at[0, iteration, c],
            recv_sem=pair_sem.at[1, iteration, c],
            device_id=sibling,
            device_id_type=MESH,
        )

    def to_peer(iteration, c, k):
        side_ = lax.rem(side + kinds[k][0], 2)
        row_ = lax.rem(row + kinds[k][1], 2)
        return pltpu.make_async_remote_copy(
            src_ref=logs.at[2 * side_ + row_, core, :, chunk(c)],
            dst_ref=peer_sum.at[iteration, k, :, chunk(c)],
            send_sem=peer_sem.at[0, iteration, c, k],
            recv_sem=peer_sem.at[1, iteration, c, k],
            device_id=device(side_, 2 * row_ + core),
            device_id_type=MESH,
        )

    def correct(iteration, c):
        edges_arrived(iteration, c)
        backward_z(iteration, c)
        to_sibling(iteration, c).start()

    def reduce_pair(iteration, c):
        to_sibling(iteration, c).wait_recv()
        for k in range(4):
            logs[k, core, :, chunk(c)] = (
                logs[k, core, :, chunk(c)] + pair_sum[iteration, k, :, chunk(c)]
            )
        for k in range(3):
            to_peer(iteration, c, k).start()

    def update(iteration, made, c):
        for k in (1, 2, 0):
            to_peer(iteration, c, k).wait_recv()
        count = jnp.sum(cover_ref[...], axis=0, keepdims=True)
        total = logs[2 * side + row, core, :, chunk(c)]
        for k in range(3):
            total = total + peer_sum[iteration, k, :, chunk(c)]
        factor = jnp.exp(total / count[None])
        window[own, core, :, chunk(c)] = window[own, core, :, chunk(c)] * factor
        start_all(iteration + 1, c, made[0])

    def sums_sent(iteration, c):
        to_sibling(iteration, c).wait_send()
        for k in range(3):
            to_peer(iteration, c, k).wait_send()

    def pipeline(stages):
        def turn_of(t, carry):
            for lag, stage in enumerate(stages):
                c = t - lag
                pl.when((c >= 0) & (c < CHUNKS))(functools.partial(stage, c))
            return carry

        lax.fori_loop(0, CHUNKS + len(stages) - 1, turn_of, 0)

    def initial():
        made = plan(True, yes)

        def begin(c, carry):
            start_all(0, c, made[0])
            return carry

        lax.fori_loop(0, CHUNKS, begin, 0)
        start_axial()
        turn()
        start_lateral()
        prepare()

        def settle(c):
            spread_done(0, c, made)
            forward_z(c)

        pipeline(
            [lambda c: send_on(0, c, made[1]), lambda c: send_on(0, c, made[2]), settle]
        )

    def one_pass(iteration, carry):
        more = iteration < ITERS - 1
        made = plan(False, more)
        stage = iteration + 1
        middle(iteration)

        def settle(c):
            spread_done(stage, c, made)

            @pl.when(more)
            def _():
                forward_z(c)

            @pl.when(iteration == ITERS - 1)
            def _():
                out_ref[:, :, :, chunk(c)] = window[pl.ds(own_side, 2), :, :, chunk(c)]

        pipeline(
            [
                lambda c: correct(iteration, c),
                lambda c: reduce_pair(iteration, c),
                lambda c: update(iteration, made, c),
                lambda c: send_on(stage, c, made[1]),
                lambda c: send_on(stage, c, made[2]),
                settle,
            ]
        )
        edges_sent(iteration)

        def finish(c, carry_):
            sums_sent(iteration, c)
            return carry_

        return lax.fori_loop(0, CHUNKS, finish, carry)

    initial()
    cover_copy.wait_send()
    remote(cover.at[1 - side], cover.at[1 - side], cover_sem, 0, sibling).wait_recv()
    which = takes_lateral * views + view
    weight[:planes, :] = jnp.broadcast_to(cover[0, pl.ds(which, 1), :], (planes, columns))
    weight[planes:, :] = jnp.broadcast_to(cover[1, pl.ds(which, 1), :], (planes, columns))
    lax.fori_loop(0, ITERS, one_pass, 0)
    views_sent()


def joint(estimate, axial_views, lateral_views, psf_axial, psf_lateral, coverage):
    planes, lines, columns = estimate.shape
    owners = lax.axis_size("owner")
    views = lax.axis_size("view")
    slab = columns // owners
    span = 2 * planes
    depth = owners * planes
    block = planes // views
    takes_lateral = (lax.axis_index("owner") + lax.axis_index("view")) % 2 == 1
    psf = jnp.where(takes_lateral, psf_lateral[0], psf_axial[0])
    psf = psf / jnp.sum(psf, axis=-1, keepdims=True)
    cover = jnp.repeat(coverage[0].astype(F32).T, columns // coverage.shape[1], axis=1)
    vmem = pl.BlockSpec(memory_space=pltpu.VMEM)
    hbm = pl.BlockSpec(memory_space=pl.ANY)
    dma = pltpu.SemaphoreType.DMA
    result = pl.pallas_call(
        functools.partial(joint_kernel, owners, views, planes, lines, columns),
        out_shape=jax.ShapeDtypeStruct((2, 2, block, lines, columns), F32),
        in_specs=[pl.BlockSpec(memory_space=pltpu.SMEM)] + [hbm] * 3 + [vmem],
        out_specs=vmem,
        scratch_shapes=[
            pltpu.VMEM((8, 2, block, lines, columns), F32),
            pltpu.VMEM((span, lines, columns), F32),
            pltpu.VMEM((slab, lines, depth), F32),
            pltpu.VMEM((depth, slab, lines), F32),
            pltpu.VMEM((span, lines, columns), F32),
            pltpu.VMEM((ITERS * 2 * span, lines, columns), F32),
            pltpu.VMEM((4, 2, block, lines, columns), F32),
            pltpu.VMEM((ITERS, 4, block, lines, columns), F32),
            pltpu.VMEM((ITERS, 3, block, lines, columns), F32),
            pltpu.VMEM((2,) + cover.shape, F32),
            pltpu.VMEM((2 * columns, 2 * columns), BF16),
            pltpu.VMEM((2 * columns, 2 * columns), BF16),
            pltpu.VMEM((2 * lines, 2 * lines), BF16),
            pltpu.VMEM((2 * lines, 2 * lines), BF16),
            pltpu.VMEM((2 * span, 4 * span), BF16),
            pltpu.VMEM((2 * span, 4 * span), BF16),
            pltpu.VMEM((lines, columns), F32),
            pltpu.VMEM((span, columns), F32),
            pltpu.VMEM((span, columns), F32),
            dma((2, 1)),
            dma((2, PARTS)),
            dma((2, owners, PARTS, 2)),
            dma((2, ITERS, 2, planes // EDGE + CHUNKS)),
            dma((2, ITERS + 1, CHUNKS, 9)),
            dma((2, ITERS, CHUNKS)),
            dma((2, ITERS, CHUNKS, 3)),
            dma((3,)),
        ],
        compiler_params=pltpu.CompilerParams(
            collective_id=0, has_side_effects=True, vmem_limit_bytes=48 * 1024 * 1024
        ),
    )(
        psf.reshape(-1),
        estimate.reshape(2, 2, block, lines, columns),
        axial_views[0],
        lateral_views[0],
        cover,
    )
    return result.reshape(planes, lines, columns)


def chosen(estimate, axial_views, lateral_views, psf_axial, psf_lateral, coverage):
    planes, lines, columns = estimate.shape
    owners = lax.axis_size("owner")
    views = lax.axis_size("view")
    rim = (psf_axial.shape[-1] - 1) // 2
    fits = (
        lines == columns
        and columns % 128 == 0
        and planes * lines * columns * 4 <= 1024 * 1024
        and planes * owners == columns
        and axial_views.shape[0] == 1
        and lateral_views.shape[0] == 1
        and views == 4
        and owners % 2 == 0
        and planes % views == 0
        and planes % (EDGE * PARTS) == 0
        and rim <= planes
        and columns // owners % 8 == 0
        and lines % (GROUP * CHUNKS) == 0
    )
    body = joint if fits else local
    return body(estimate, axial_views, lateral_views, psf_axial, psf_lateral, coverage)


def solution(mesh):
    in_specs = (
        P("owner", None, None),
        P("view", "owner", None, None),
        P("view", "owner", None, None),
        P("view", None, None),
        P("view", None, None),
        P("owner", None, None),
    )
    out_specs = P("owner", None, None)
    return jax.shard_map(chosen, mesh=mesh, in_specs=in_specs, out_specs=out_specs, check_vma=False)
```

```python
import functools

import jax
import jax.numpy as jnp
from jax import lax
from jax.experimental import pallas as pl
from jax.experimental.pallas import tpu as pltpu
from jax.sharding import PartitionSpec as P

VA = 4
ITERS = 2


PRECISE = lax.Precision.HIGHEST


def extended(shard, sides, width):
    for axis, dim in sides:
        peers, length = (lax.axis_size(axis), shard.shape[dim])
        up = [(i, (i + 1) % peers) for i in range(peers - 1)]
        down = [(j, i) for i, j in up]
        last = lax.slice_in_dim(shard, length - width, length, axis=dim)
        leading = lax.slice_in_dim(shard, 0, width, axis=dim)
        before = lax.ppermute(last, axis, up)
        after = lax.ppermute(leading, axis, down)
        shard = jnp.concatenate([before, shard, after], axis=dim)
    return shard


def band_matrix(kernel, block_width):
    rim_width = (kernel.shape[-1] - 1) // 2
    row_index = jnp.arange(block_width + 2 * rim_width)[:, None]
    col_index = jnp.arange(block_width)[None, :]
    matches = (row_index - col_index)[:, :, None] == jnp.arange(kernel.shape[-1])[None, None, :]
    return jnp.sum(jnp.where(matches[None], kernel[:, None, None, :], 0.0), axis=-1)


def middle_matrix(kernel, length):
    rim_width = (kernel.shape[-1] - 1) // 2
    row_index = jnp.arange(length)[:, None]
    col_index = jnp.arange(length)[None, :]
    matches = (row_index - col_index + rim_width)[:, :, None] == jnp.arange(kernel.shape[-1])[
        None, None, :
    ]
    return jnp.sum(jnp.where(matches[None], kernel[:, None, None, :], 0.0), axis=-1)


def along_last(volume, kernel):
    rim_width = (kernel.shape[-1] - 1) // 2
    length = volume.shape[-1]
    block_width = min(128, length)
    blocks = volume.reshape(volume.shape[:-1] + (length // block_width, block_width))
    zero_rim = jnp.zeros(blocks.shape[:-2] + (1, rim_width), volume.dtype)
    left_rim = jnp.concatenate([zero_rim, blocks[..., :-1, block_width - rim_width :]], axis=-2)
    right_rim = jnp.concatenate([blocks[..., 1:, :rim_width], zero_rim], axis=-2)
    windows = jnp.concatenate([left_rim, blocks, right_rim], axis=-1)
    result = jnp.einsum(
        "vabns,vsi->vabni", windows, band_matrix(kernel, block_width), precision=PRECISE
    )
    return result.reshape(volume.shape)


def forward(padded, kernel_first, kernel_mid, kernel_last):
    plane_count = padded.shape[0] - (kernel_first.shape[-1] - 1)
    result = jnp.einsum(
        "syl,vsi->viyl", padded, band_matrix(kernel_first, plane_count), precision=PRECISE
    )
    result = jnp.einsum(
        "viyl,vyk->vikl", result, middle_matrix(kernel_mid, result.shape[2]), precision=PRECISE
    )
    return along_last(result, kernel_last)


def backward(padded, kernel_first, kernel_mid, kernel_last):
    plane_count = padded.shape[1] - (kernel_first.shape[-1] - 1)
    result = jnp.einsum(
        "vsyl,vsi->viyl", padded, band_matrix(kernel_first, plane_count), precision=PRECISE
    )
    result = jnp.einsum(
        "viyl,vyk->vikl", result, middle_matrix(kernel_mid, result.shape[2]), precision=PRECISE
    )
    return along_last(result, kernel_last)


def edge_weights(kernel, positions, length):
    rim_width = (kernel.shape[-1] - 1) // 2
    source = positions[:, None] + jnp.arange(kernel.shape[-1])[None, :] - rim_width
    inside = (source >= 0) & (source < length)
    return jnp.sum(jnp.where(inside[None], kernel[:, None, :], 0.0), axis=-1)


def log_correction(padded, kernel_first, kernel_mid, kernel_last, first_start, first_total):
    back_sum = backward(padded, kernel_first, kernel_mid, kernel_last)
    plane_count, line_count, column_count = back_sum.shape[1:]
    first_weights = edge_weights(kernel_first, first_start + jnp.arange(plane_count), first_total)
    mid_weights = edge_weights(kernel_mid, jnp.arange(line_count), line_count)
    last_weights = edge_weights(kernel_last, jnp.arange(column_count), column_count)
    scale_sum = (
        first_weights[:, :, None, None]
        * mid_weights[:, None, :, None]
        * last_weights[:, None, None, :]
    )
    return jnp.log(back_sum / scale_sum)


def select_views(covered, view_ids):
    picked = (jnp.arange(covered.shape[-1])[None, :] == view_ids[:, None]).astype(jnp.float32)
    return jnp.einsum("vw,xw->vx", picked, covered, precision=PRECISE)


def slab_logs(padded_estimate, view_data, kernel, flipped, weights, first_start, first_total):
    blurred = forward(padded_estimate, kernel[:, 0], kernel[:, 1], kernel[:, 2])
    quotient = view_data / blurred
    rim_width = (kernel.shape[-1] - 1) // 2
    quotient_padded = extended(quotient, (("owner", 1),), rim_width)
    log_terms = log_correction(
        quotient_padded, flipped[:, 0], flipped[:, 1], flipped[:, 2], first_start, first_total
    )
    return jnp.sum(weights[:, None, None, :] * log_terms, axis=0)


def local(estimate, axial_views, lateral_views, psf_axial, psf_lateral, coverage):
    plane_count, line_count, column_count = estimate.shape
    owners = lax.axis_size("owner")
    slab_index = lax.axis_index("owner")
    view_index = lax.axis_index("view")
    slab_width = column_count // owners
    rim_width = (psf_axial.shape[-1] - 1) // 2
    kernel_axial = psf_axial / jnp.sum(psf_axial, axis=-1, keepdims=True)
    kernel_lateral = psf_lateral / jnp.sum(psf_lateral, axis=-1, keepdims=True)
    flipped_axial = kernel_axial[..., ::-1]
    flipped_lateral = kernel_lateral[..., ::-1]
    block_width = column_count // coverage.shape[1]
    covered = jnp.repeat(coverage[0].astype(jnp.float32), block_width, axis=0)
    cover_count = jnp.sum(covered, axis=-1)
    axial_count = psf_axial.shape[0]
    lateral_count = psf_lateral.shape[0]
    weights_axial = select_views(covered, view_index * axial_count + jnp.arange(axial_count))
    weights_lateral = select_views(
        covered, VA + view_index * lateral_count + jnp.arange(lateral_count)
    )
    plane_start = slab_index * plane_count
    plane_total = plane_count * owners
    moved_views = lateral_views.reshape(
        lateral_count, slab_width, line_count, owners, plane_count
    ).transpose(0, 4, 2, 3, 1)
    lateral_slabs = lax.all_to_all(moved_views, "owner", split_axis=3, concat_axis=4, tiled=True)
    lateral_slabs = lateral_slabs.reshape(lateral_count, plane_count, line_count, column_count)
    view_all = jnp.concatenate([axial_views, lateral_slabs], axis=0)
    kernel_all = jnp.concatenate([kernel_axial, kernel_lateral], axis=0)
    flipped_all = jnp.concatenate([flipped_axial, flipped_lateral], axis=0)
    weights_all = jnp.concatenate([weights_axial, weights_lateral], axis=0)
    for iteration in range(ITERS):
        padded_estimate = extended(estimate, (("owner", 0),), rim_width)
        log_total = slab_logs(
            padded_estimate,
            view_all,
            kernel_all,
            flipped_all,
            weights_all,
            plane_start,
            plane_total,
        )
        log_total = lax.psum(log_total, "view")
        estimate = estimate * jnp.exp(log_total / cover_count[None, None, :])
    return estimate


F32 = jnp.float32
BF16 = jnp.bfloat16
MESH = pl.DeviceIdType.MESH
CHUNKS = 2
PARTS = 2
EDGE = 4
GROUP = 8


def split_bf16(values):
    high = values.astype(BF16)
    low = (values - high.astype(F32)).astype(BF16)
    return high, low


def dot32(left, right):
    return jnp.dot(left, right, preferred_element_type=F32)


def joint_kernel(
    owners,
    views,
    planes,
    lines,
    columns,
    psf_ref,
    estimate_ref,
    axial_ref,
    lateral_ref,
    cover_ref,
    out_ref,
    window,
    observed,
    lateral,
    turned,
    mid,
    quot,
    logs,
    pair_sum,
    peer_sum,
    cover,
    x_fwd,
    x_back,
    y_fwd,
    y_back,
    z_fwd,
    z_back,
    log_xy,
    log_z,
    weight,
    cover_sem,
    axial_sem,
    lateral_sem,
    edge_sem,
    share_sem,
    pair_sem,
    peer_sem,
    local_sem,
):
    taps = psf_ref.shape[0] // 3
    rim = (taps - 1) // 2
    groups = owners // 2
    span = 2 * planes
    block = planes // views
    chunk_lines = lines // CHUNKS
    slab = columns // owners

    me = lax.axis_index("owner")
    view = lax.axis_index("view")
    group = me // 2
    side = lax.rem(me, 2)
    core = lax.rem(view, 2)
    row = view // 2
    takes_lateral = lax.rem(side + core, 2)
    has_below = group > 0
    has_above = group < groups - 1

    def device(side_, view_):
        return (2 * group + side_, view_)

    sibling = device(side, 2 * row + 1 - core)

    barrier = pltpu.get_barrier_semaphore()
    for step in range(1, owners):
        pl.semaphore_signal(
            barrier, inc=1, device_id=(lax.rem(me + step, owners), view), device_id_type=MESH
        )
    for side_ in (side, 1 - side):
        for step in range(1, views):
            pl.semaphore_signal(
                barrier,
                inc=1,
                device_id=device(side_, lax.rem(view + step, views)),
                device_id_type=MESH,
            )
    mine = window.at[pl.ds(2 + 2 * side, 2)]
    estimate_in = pltpu.make_async_copy(estimate_ref, mine, local_sem.at[0])
    lateral_in = pltpu.make_async_copy(lateral_ref, lateral, local_sem.at[1])
    window_planes = window.reshape(2 * span, lines, columns)
    estimate_in.start()
    lateral_in.start()
    cover[pl.ds(side, 1)] = cover_ref[...][None]

    def clear(slab_):
        def plane(z, carry):
            zero = jnp.zeros((lines, columns), F32)
            window_planes[slab_ * planes + z] = zero
            for iteration in range(ITERS):
                quot[iteration * 2 * span + slab_ * planes + z] = zero
            return carry

        lax.fori_loop(0, planes, plane, 0)

    pl.when(group == 0)(lambda: clear(0))
    pl.when(group == groups - 1)(lambda: clear(3))

    estimate_in.wait()
    pl.semaphore_wait(barrier, owners - 1 + 2 * (views - 1))

    def remote(src, dst, sems, index, target):
        return pltpu.make_async_remote_copy(
            src_ref=src,
            dst_ref=dst,
            send_sem=sems.at[0, index],
            recv_sem=sems.at[1, index],
            device_id=target,
            device_id_type=MESH,
        )

    def chunk(c):
        return pl.ds(pl.multiple_of(c * chunk_lines, chunk_lines), chunk_lines)

    def part(first, count, core_, c):
        return window.at[pl.ds(first, count), core_, :, chunk(c)]

    def copy_part(stage, c, slot, src, dst, count, target):
        return pltpu.make_async_remote_copy(
            src_ref=part(src, count, core, c),
            dst_ref=part(dst, count, core, c),
            send_sem=share_sem.at[0, stage, c, slot],
            recv_sem=share_sem.at[1, stage, c, slot],
            device_id=target,
            device_id_type=MESH,
        )

    own = 2 + 2 * side + row
    own_side = 2 + 2 * side
    other_side = 4 - 2 * side
    row_peer = device(side, 2 * (1 - row) + core)
    side_peer = device(1 - side, view)
    far_peer = device(1 - side, 2 * (1 - row) + core)
    other = 1 - core
    yes = group >= 0

    def up_copy(more):
        return (has_above & more, 3, 4, 0, 2, (me + 2, view))

    def down_copy(more):
        return (has_below & more, 4, 2, 6, 2, (me - 2, view))

    def plan(first, more):
        x_arrival = (more, 0, 2 + 2 * (1 - side) + row, 1, core)
        y_arrival = (yes, 1, 2 + 2 * side + 1 - row, 1, core)
        far_arrival = (more, 2, 2 + 2 * (1 - side) + 1 - row, 1, core)
        if first:
            near = (has_above & (side == 1), 3, 4 + row, row, 1, (me + 2, view))
            near_down = (has_below & (side == 0), 4, 2 + row, 6 + row, 1, (me - 2, view))
            at_once = [(yes, 0, own, own, 1, side_peer), near, near_down]
            across = x_arrival[2]
            group_steps = [
                (
                    [x_arrival],
                    [
                        (yes, 2, across, across, 1, row_peer),
                        (has_above & (side == 0), 3, 4 + row, row, 1, (me + 2, view)),
                        (has_below & (side == 1), 4, 2 + row, 6 + row, 1, (me - 2, view)),
                    ],
                ),
                ([far_arrival], [(yes, 5, other_side, other_side, 2, sibling)]),
            ]
            beside_steps = [
                ([(has_below, 3, row, 1, core)], [(has_below, 9, row, row, 1, row_peer)]),
                (
                    [(has_above, 4, 6 + row, 1, core)],
                    [(has_above, 10, 6 + row, 6 + row, 1, row_peer)],
                ),
                ([(has_below, 9, 1 - row, 1, core)], [(has_below, 6, 0, 0, 2, sibling)]),
                ([(has_above, 10, 7 - row, 1, core)], [(has_above, 7, 6, 6, 2, sibling)]),
            ]
            rest = [(yes, 5, other_side, 2, other)]
        else:
            at_once = [
                (more, 0, own, own, 1, side_peer),
                (yes, 1, own, own, 1, row_peer),
                (more, 2, own, own, 1, far_peer),
            ]
            group_steps = [
                (
                    [y_arrival, x_arrival, far_arrival],
                    [
                        up_copy(more),
                        down_copy(more),
                        (more, 5, 2, 2, 4, sibling),
                        (jnp.logical_not(more), 8, own_side, own_side, 2, sibling),
                    ],
                )
            ]
            beside_steps = [
                ([(has_below & more, 3, 0, 2, core)], [(has_below & more, 6, 0, 0, 2, sibling)]),
                ([(has_above & more, 4, 6, 2, core)], [(has_above & more, 7, 6, 6, 2, sibling)]),
            ]
            rest = [(more, 5, 2, 4, other), (jnp.logical_not(more), 8, own_side, 2, other)]
        rest = rest + [(has_below & more, 6, 0, 2, other), (has_above & more, 7, 6, 2, other)]
        return at_once, group_steps, beside_steps, rest

    def start_all(stage, c, sends):
        for condition, *where in sends:
            pl.when(condition)(copy_part(stage, c, *where).start)

    def await_all(stage, c, arrivals):
        for condition, slot, first, count, core_ in arrivals:
            there = part(first, count, core_, c)
            made = pltpu.make_async_remote_copy(
                src_ref=there,
                dst_ref=there,
                send_sem=share_sem.at[0, stage, c, slot],
                recv_sem=share_sem.at[1, stage, c, slot],
                device_id=sibling,
                device_id_type=MESH,
            )
            pl.when(condition)(made.wait_recv)

    def send_on(stage, c, steps_):
        for arrivals, onward in steps_:
            await_all(stage, c, arrivals)
            start_all(stage, c, onward)

    def spread_done(stage, c, made):
        at_once, group_steps, beside_steps, rest = made
        await_all(stage, c, rest)
        onwards = [onward for _, onward in group_steps + beside_steps]
        for condition, *where in sum(onwards, at_once):
            pl.when(condition)(copy_part(stage, c, *where).wait_send)

    def toeplitz(axis, shape, offset, flip):
        first = lax.broadcasted_iota(jnp.int32, shape, 0)
        second = lax.broadcasted_iota(jnp.int32, shape, 1)
        place = (second - first if flip else first - second) + (rim + offset)

        def add(t, total):
            return jnp.where(place == t, psf_ref[axis * taps + t], total)

        return lax.fori_loop(0, taps, add, jnp.zeros(shape, F32))

    def store_right(ref, matrix):
        high, low = split_bf16(matrix)
        top = jnp.concatenate([high, low], axis=1)
        ref[...] = jnp.concatenate([top, top], axis=0)

    def store_left(ref, matrix):
        high, low = split_bf16(matrix)
        ref[...] = jnp.concatenate(
            [jnp.concatenate([high, high], axis=1), jnp.concatenate([low, low], axis=1)], axis=0
        )

    def prepare():
        store_right(x_fwd, toeplitz(2, (columns, columns), 0, False))
        back_x = toeplitz(2, (columns, columns), 0, True)
        store_right(x_back, back_x)
        store_left(y_fwd, toeplitz(1, (lines, lines), 0, True))
        back_y = toeplitz(1, (lines, lines), 0, False)
        store_left(y_back, back_y)
        store_left(z_fwd, toeplitz(0, (span, 2 * span), -planes, True))
        back_z = toeplitz(0, (span, 2 * span), planes, False)
        store_left(z_back, back_z)
        log_xy[...] = jnp.log(jnp.sum(back_y, axis=1, keepdims=True)) + jnp.log(
            jnp.sum(back_x, axis=0, keepdims=True)
        )
        plane = lax.broadcasted_iota(jnp.int32, (span, 2 * span), 1) + (group * span - planes)
        inside = (plane >= 0) & (plane < owners * planes)
        sums = jnp.sum(jnp.where(inside, back_z, 0.0), axis=1, keepdims=True)
        log_z[...] = jnp.broadcast_to(jnp.log(sums), (span, columns))

    cover_copy = remote(cover.at[side], cover.at[side], cover_sem, 0, device(1 - side, view))
    cover_copy.start()
    axial_target = device(core, view)
    axial_mine = pl.ds(side * planes, planes)
    depth = planes // PARTS
    axial_in = pltpu.make_async_copy(axial_ref, observed.at[axial_mine], local_sem.at[2])

    def axial_copy(q):
        return remote(
            axial_ref.at[pl.ds(q * depth, depth)],
            observed.at[pl.ds(side * planes + q * depth, depth)],
            axial_sem,
            q,
            axial_target,
        )

    def axial_arrival(q):
        theirs = observed.at[pl.ds((1 - side) * planes + q * depth, depth)]
        return remote(theirs, theirs, axial_sem, q, sibling)

    def lateral_copy(to, q, half):
        plane = half * planes + q * depth
        return pltpu.make_async_remote_copy(
            src_ref=turned.at[pl.ds(to * span + plane, depth)],
            dst_ref=observed.at[pl.ds(plane, depth), pl.ds(me * slab, slab), :],
            send_sem=lateral_sem.at[0, to, q, half],
            recv_sem=lateral_sem.at[1, me, q, half],
            device_id=(2 * to + 1 - core, view),
            device_id_type=MESH,
        )

    def lateral_arrival(source, q, half):
        there = observed.at[pl.ds(half * planes + q * depth, depth), pl.ds(source * slab, slab), :]
        return pltpu.make_async_remote_copy(
            src_ref=there,
            dst_ref=there,
            send_sem=lateral_sem.at[0, 0, q, half],
            recv_sem=lateral_sem.at[1, source, q, half],
            device_id=sibling,
            device_id_type=MESH,
        )

    def turn():
        lateral_in.wait()
        for x in range(slab):
            turned[:, x, :] = lateral[x].T

    def each_lateral(act):
        def one(i, carry):
            q, to = i // groups, lax.rem(i, groups)

            @pl.when((takes_lateral == 0) | (to != group))
            def _():
                act(lateral_copy(to, q, 0))
                act(lateral_copy(to, q, 1))

            return carry

        lax.fori_loop(0, PARTS * groups, one, 0)

    def start_axial():
        @pl.when(takes_lateral == 1)
        def _():
            for q in range(PARTS):
                axial_copy(q).start()

        @pl.when(takes_lateral == 0)
        def _():
            axial_in.start()

    def start_lateral():
        each_lateral(lambda copy: copy.start())

        @pl.when(takes_lateral == 1)
        def _():
            observed[:, pl.ds(pl.multiple_of(me * slab, slab), slab), :] = turned[
                pl.ds(group * span, span)
            ]

    def views_arrived(q):
        @pl.when(takes_lateral == 1)
        def _():
            def from_owner(step, carry):
                source = lax.rem(me + step, owners)
                lateral_arrival(source, q, 0).wait_recv()
                lateral_arrival(source, q, 1).wait_recv()
                return carry

            lax.fori_loop(1, owners, from_owner, 0)

            def flip(k, carry):
                z = q * depth + k
                observed[z] = observed[z].T
                observed[planes + z] = observed[planes + z].T
                return carry

            lax.fori_loop(0, depth, flip, 0)

        @pl.when(takes_lateral == 0)
        def _():
            pl.when(q == 0)(axial_in.wait)
            axial_arrival(q).wait_recv()

    def views_sent():
        each_lateral(lambda copy: copy.wait_send())

        @pl.when(takes_lateral == 1)
        def _():
            for q in range(PARTS):
                axial_copy(q).wait_send()

    def along_z(source, matrix, y, first_row=0):
        both = jnp.concatenate(
            [
                source[pl.ds(first_row + y, 2 * span, stride=lines), :],
                source[pl.ds(first_row + y + 1, 2 * span, stride=lines), :],
            ],
            axis=1,
        )
        high, low = split_bf16(both)
        result = dot32(matrix[...], jnp.concatenate([high, low], axis=0))
        result = result[:span] + result[span:]
        return result[:, :columns], result[:, columns:]

    def along_x(planes_two, matrix):
        high, low = split_bf16(planes_two)
        result = dot32(jnp.concatenate([high, low], axis=1), matrix[...])
        return result[:, :columns] + result[:, columns:]

    def along_y(planes_two, matrix):
        high, low = split_bf16(planes_two)
        result = dot32(matrix[...], jnp.concatenate([high, low], axis=0))
        return result[:lines] + result[lines:]

    window_lines = window.reshape(2 * span * lines, columns)
    mid_lines = mid.reshape(span * lines, columns)
    logs_lines = logs.reshape(span * lines, columns)
    quot_lines = quot.reshape(ITERS * 2 * span * lines, columns)

    def z_then_x(source, z_matrix, x_matrix, y, first_row=0):
        results = []
        for step in range(0, GROUP, 2):
            results.extend(along_z(source, z_matrix, y + step, first_row))
        return along_x(jnp.concatenate(results, axis=0), x_matrix)

    def forward_z(c):
        def lines_of(i, carry):
            y = c * chunk_lines + i * GROUP
            result = z_then_x(window_lines, z_fwd, x_fwd, y)
            for step in range(GROUP):
                mid_lines[pl.ds(y + step, span, stride=lines), :] = result[
                    step * span : (step + 1) * span
                ]
            return carry

        lax.fori_loop(0, chunk_lines // GROUP, lines_of, 0)

    def plane_pair(iteration, z):
        blurred = along_y(jnp.concatenate([mid[z], mid[z + 1]], axis=1), y_fwd)
        seen = jnp.concatenate([observed[z], observed[z + 1]], axis=1)
        back = along_y(seen / blurred, y_back)
        first = iteration * 2 * span + planes + z
        quot[first] = back[:, :columns]
        quot[first + 1] = back[:, columns:]

    early = CHUNKS // 2
    steps = planes // EDGE

    def edge(iteration, index, up, plane, count, lines_at):
        start_plane = (2 * planes if up else planes) + plane
        end_plane = (0 if up else 3 * planes) + plane
        way = 1 if up else 0
        return pltpu.make_async_remote_copy(
            src_ref=quot.at[pl.ds(iteration * 2 * span + start_plane, count), lines_at],
            dst_ref=quot.at[pl.ds(iteration * 2 * span + end_plane, count), lines_at],
            send_sem=edge_sem.at[0, iteration, way, index],
            recv_sem=edge_sem.at[1, iteration, way, index],
            device_id=(me + 2 if up else me - 2, view),
            device_id_type=MESH,
        )

    def early_edge(iteration, s, up):
        return edge(iteration, s, up, EDGE * s, EDGE, pl.ds(0, early * chunk_lines))

    def late_edge(iteration, c, up):
        return edge(iteration, steps + c - early, up, 0, planes, chunk(c))

    def middle(iteration):
        def step(s, carry):
            for k in range(0, EDGE, 2):
                plane_pair(iteration, EDGE * s + k)
                plane_pair(iteration, planes + EDGE * s + k)
            pl.when(has_below)(early_edge(iteration, s, False).start)
            pl.when(has_above)(early_edge(iteration, s, True).start)
            return carry

        def part_of(q, carry):
            pl.when(iteration == 0)(lambda: views_arrived(q))
            return lax.fori_loop(q * (steps // PARTS), (q + 1) * (steps // PARTS), step, carry)

        lax.fori_loop(0, PARTS, part_of, 0)
        for c in range(early, CHUNKS):
            pl.when(has_below)(late_edge(iteration, c, False).start)
            pl.when(has_above)(late_edge(iteration, c, True).start)

    def run(body):
        lax.fori_loop(0, steps, body, 0)

    def edges_arrived(iteration, c):
        def finish(s, carry):
            pl.when(has_above)(early_edge(iteration, s, False).wait_recv)
            pl.when(has_below)(early_edge(iteration, s, True).wait_recv)
            return carry

        pl.when(c == 0)(lambda: run(finish))
        pl.when((c >= early) & has_above)(lambda: late_edge(iteration, c, False).wait_recv())
        pl.when((c >= early) & has_below)(lambda: late_edge(iteration, c, True).wait_recv())

    def edges_sent(iteration):
        def finish(s, carry):
            pl.when(has_below)(early_edge(iteration, s, False).wait_send)
            pl.when(has_above)(early_edge(iteration, s, True).wait_send)
            return carry

        lax.fori_loop(0, steps, finish, 0)
        for c in range(early, CHUNKS):
            pl.when(has_below)(late_edge(iteration, c, False).wait_send)
            pl.when(has_above)(late_edge(iteration, c, True).wait_send)

    def backward_z(iteration, c):
        first_row = iteration * 2 * span * lines

        def lines_of(i, carry):
            y = c * chunk_lines + i * GROUP
            back = jnp.log(z_then_x(quot_lines, z_back, x_back, y, first_row))
            for step in range(GROUP):
                value = back[step * span : (step + 1) * span]
                value = value - (log_z[...] + log_xy[pl.ds(y + step, 1), :])
                logs_lines[pl.ds(y + step, span, stride=lines), :] = weight[...] * value
            return carry

        lax.fori_loop(0, chunk_lines // GROUP, lines_of, 0)

    kinds = [(1, 1), (1, 0), (0, 1)]

    def to_sibling(iteration, c):
        return pltpu.make_async_remote_copy(
            src_ref=logs.at[:, other, :, chunk(c)],
            dst_ref=pair_sum.at[iteration, :, :, chunk(c)],
            send_sem=pair_sem.at[0, iteration, c],
            recv_sem=pair_sem.at[1, iteration, c],
            device_id=sibling,
            device_id_type=MESH,
        )

    def to_peer(iteration, c, k):
        side_ = lax.rem(side + kinds[k][0], 2)
        row_ = lax.rem(row + kinds[k][1], 2)
        return pltpu.make_async_remote_copy(
            src_ref=logs.at[2 * side_ + row_, core, :, chunk(c)],
            dst_ref=peer_sum.at[iteration, k, :, chunk(c)],
            send_sem=peer_sem.at[0, iteration, c, k],
            recv_sem=peer_sem.at[1, iteration, c, k],
            device_id=device(side_, 2 * row_ + core),
            device_id_type=MESH,
        )

    def correct(iteration, c):
        edges_arrived(iteration, c)
        backward_z(iteration, c)
        to_sibling(iteration, c).start()

    def reduce_pair(iteration, c):
        to_sibling(iteration, c).wait_recv()
        for k in range(4):
            logs[k, core, :, chunk(c)] = (
                logs[k, core, :, chunk(c)] + pair_sum[iteration, k, :, chunk(c)]
            )
        for k in range(3):
            to_peer(iteration, c, k).start()

    def update(iteration, made, c):
        for k in (1, 2, 0):
            to_peer(iteration, c, k).wait_recv()
        count = jnp.sum(cover_ref[...], axis=0, keepdims=True)
        total = logs[2 * side + row, core, :, chunk(c)]
        for k in range(3):
            total = total + peer_sum[iteration, k, :, chunk(c)]
        factor = jnp.exp(total / count[None])
        window[own, core, :, chunk(c)] = window[own, core, :, chunk(c)] * factor
        start_all(iteration + 1, c, made[0])

    def sums_sent(iteration, c):
        to_sibling(iteration, c).wait_send()
        for k in range(3):
            to_peer(iteration, c, k).wait_send()

    def pipeline(stages):
        def turn_of(t, carry):
            for lag, stage in enumerate(stages):
                c = t - lag
                pl.when((c >= 0) & (c < CHUNKS))(functools.partial(stage, c))
            return carry

        lax.fori_loop(0, CHUNKS + len(stages) - 1, turn_of, 0)

    def initial():
        made = plan(True, yes)

        def begin(c, carry):
            start_all(0, c, made[0])
            return carry

        lax.fori_loop(0, CHUNKS, begin, 0)
        start_axial()
        turn()
        start_lateral()
        prepare()

        def settle(c):
            spread_done(0, c, made)
            forward_z(c)

        pipeline(
            [lambda c: send_on(0, c, made[1]), lambda c: send_on(0, c, made[2]), settle]
        )

    def one_pass(iteration, carry):
        more = iteration < ITERS - 1
        made = plan(False, more)
        stage = iteration + 1
        middle(iteration)

        def settle(c):
            spread_done(stage, c, made)

            @pl.when(more)
            def _():
                forward_z(c)

            @pl.when(iteration == ITERS - 1)
            def _():
                out_ref[:, :, :, chunk(c)] = window[pl.ds(own_side, 2), :, :, chunk(c)]

        pipeline(
            [
                lambda c: correct(iteration, c),
                lambda c: reduce_pair(iteration, c),
                lambda c: update(iteration, made, c),
                lambda c: send_on(stage, c, made[1]),
                lambda c: send_on(stage, c, made[2]),
                settle,
            ]
        )
        edges_sent(iteration)

        def finish(c, carry_):
            sums_sent(iteration, c)
            return carry_

        return lax.fori_loop(0, CHUNKS, finish, carry)

    initial()
    cover_copy.wait_send()
    remote(cover.at[1 - side], cover.at[1 - side], cover_sem, 0, sibling).wait_recv()
    which = takes_lateral * views + view
    weight[:planes, :] = jnp.broadcast_to(cover[0, pl.ds(which, 1), :], (planes, columns))
    weight[planes:, :] = jnp.broadcast_to(cover[1, pl.ds(which, 1), :], (planes, columns))
    lax.fori_loop(0, ITERS, one_pass, 0)
    views_sent()


def joint(estimate, axial_views, lateral_views, psf_axial, psf_lateral, coverage):
    planes, lines, columns = estimate.shape
    owners = lax.axis_size("owner")
    views = lax.axis_size("view")
    slab = columns // owners
    span = 2 * planes
    depth = owners * planes
    block = planes // views
    takes_lateral = (lax.axis_index("owner") + lax.axis_index("view")) % 2 == 1
    psf = jnp.where(takes_lateral, psf_lateral[0], psf_axial[0])
    psf = psf / jnp.sum(psf, axis=-1, keepdims=True)
    cover = jnp.repeat(coverage[0].astype(F32).T, columns // coverage.shape[1], axis=1)
    vmem = pl.BlockSpec(memory_space=pltpu.VMEM)
    hbm = pl.BlockSpec(memory_space=pl.ANY)
    dma = pltpu.SemaphoreType.DMA
    result = pl.pallas_call(
        functools.partial(joint_kernel, owners, views, planes, lines, columns),
        out_shape=jax.ShapeDtypeStruct((2, 2, block, lines, columns), F32),
        in_specs=[pl.BlockSpec(memory_space=pltpu.SMEM)] + [hbm] * 3 + [vmem],
        out_specs=vmem,
        scratch_shapes=[
            pltpu.VMEM((8, 2, block, lines, columns), F32),
            pltpu.VMEM((span, lines, columns), F32),
            pltpu.VMEM((slab, lines, depth), F32),
            pltpu.VMEM((depth, slab, lines), F32),
            pltpu.VMEM((span, lines, columns), F32),
            pltpu.VMEM((ITERS * 2 * span, lines, columns), F32),
            pltpu.VMEM((4, 2, block, lines, columns), F32),
            pltpu.VMEM((ITERS, 4, block, lines, columns), F32),
            pltpu.VMEM((ITERS, 3, block, lines, columns), F32),
            pltpu.VMEM((2,) + cover.shape, F32),
            pltpu.VMEM((2 * columns, 2 * columns), BF16),
            pltpu.VMEM((2 * columns, 2 * columns), BF16),
            pltpu.VMEM((2 * lines, 2 * lines), BF16),
            pltpu.VMEM((2 * lines, 2 * lines), BF16),
            pltpu.VMEM((2 * span, 4 * span), BF16),
            pltpu.VMEM((2 * span, 4 * span), BF16),
            pltpu.VMEM((lines, columns), F32),
            pltpu.VMEM((span, columns), F32),
            pltpu.VMEM((span, columns), F32),
            dma((2, 1)),
            dma((2, PARTS)),
            dma((2, owners, PARTS, 2)),
            dma((2, ITERS, 2, planes // EDGE + CHUNKS)),
            dma((2, ITERS + 1, CHUNKS, 11)),
            dma((2, ITERS, CHUNKS)),
            dma((2, ITERS, CHUNKS, 3)),
            dma((3,)),
        ],
        compiler_params=pltpu.CompilerParams(
            collective_id=0, has_side_effects=True, vmem_limit_bytes=48 * 1024 * 1024
        ),
    )(
        psf.reshape(-1),
        estimate.reshape(2, 2, block, lines, columns),
        axial_views[0],
        lateral_views[0],
        cover,
    )
    return result.reshape(planes, lines, columns)


def chosen(estimate, axial_views, lateral_views, psf_axial, psf_lateral, coverage):
    planes, lines, columns = estimate.shape
    owners = lax.axis_size("owner")
    views = lax.axis_size("view")
    rim = (psf_axial.shape[-1] - 1) // 2
    fits = (
        lines == columns
        and columns % 128 == 0
        and planes * lines * columns * 4 <= 1024 * 1024
        and planes * owners == columns
        and axial_views.shape[0] == 1
        and lateral_views.shape[0] == 1
        and views == 4
        and owners % 2 == 0
        and planes % views == 0
        and planes % (EDGE * PARTS) == 0
        and rim <= planes
        and columns // owners % 8 == 0
        and lines % (GROUP * CHUNKS) == 0
    )
    body = joint if fits else local
    return body(estimate, axial_views, lateral_views, psf_axial, psf_lateral, coverage)


def solution(mesh):
    in_specs = (
        P("owner", None, None),
        P("view", "owner", None, None),
        P("view", "owner", None, None),
        P("view", None, None),
        P("view", None, None),
        P("owner", None, None),
    )
    out_specs = P("owner", None, None)
    return jax.shard_map(chosen, mesh=mesh, in_specs=in_specs, out_specs=out_specs, check_vma=False)
```

```python
import functools

import jax
import jax.numpy as jnp
from jax import lax
from jax.experimental import pallas as pl
from jax.experimental.pallas import tpu as pltpu
from jax.sharding import PartitionSpec as P

VA = 4
ITERS = 2


PRECISE = lax.Precision.HIGHEST


def extended(shard, sides, width):
    for axis, dim in sides:
        peers, length = (lax.axis_size(axis), shard.shape[dim])
        up = [(i, (i + 1) % peers) for i in range(peers - 1)]
        down = [(j, i) for i, j in up]
        last = lax.slice_in_dim(shard, length - width, length, axis=dim)
        leading = lax.slice_in_dim(shard, 0, width, axis=dim)
        before = lax.ppermute(last, axis, up)
        after = lax.ppermute(leading, axis, down)
        shard = jnp.concatenate([before, shard, after], axis=dim)
    return shard


def band_matrix(kernel, block_width):
    rim_width = (kernel.shape[-1] - 1) // 2
    row_index = jnp.arange(block_width + 2 * rim_width)[:, None]
    col_index = jnp.arange(block_width)[None, :]
    matches = (row_index - col_index)[:, :, None] == jnp.arange(kernel.shape[-1])[None, None, :]
    return jnp.sum(jnp.where(matches[None], kernel[:, None, None, :], 0.0), axis=-1)


def middle_matrix(kernel, length):
    rim_width = (kernel.shape[-1] - 1) // 2
    row_index = jnp.arange(length)[:, None]
    col_index = jnp.arange(length)[None, :]
    matches = (row_index - col_index + rim_width)[:, :, None] == jnp.arange(kernel.shape[-1])[
        None, None, :
    ]
    return jnp.sum(jnp.where(matches[None], kernel[:, None, None, :], 0.0), axis=-1)


def along_last(volume, kernel):
    rim_width = (kernel.shape[-1] - 1) // 2
    length = volume.shape[-1]
    block_width = min(128, length)
    blocks = volume.reshape(volume.shape[:-1] + (length // block_width, block_width))
    zero_rim = jnp.zeros(blocks.shape[:-2] + (1, rim_width), volume.dtype)
    left_rim = jnp.concatenate([zero_rim, blocks[..., :-1, block_width - rim_width :]], axis=-2)
    right_rim = jnp.concatenate([blocks[..., 1:, :rim_width], zero_rim], axis=-2)
    windows = jnp.concatenate([left_rim, blocks, right_rim], axis=-1)
    result = jnp.einsum(
        "vabns,vsi->vabni", windows, band_matrix(kernel, block_width), precision=PRECISE
    )
    return result.reshape(volume.shape)


def forward(padded, kernel_first, kernel_mid, kernel_last):
    plane_count = padded.shape[0] - (kernel_first.shape[-1] - 1)
    result = jnp.einsum(
        "syl,vsi->viyl", padded, band_matrix(kernel_first, plane_count), precision=PRECISE
    )
    result = jnp.einsum(
        "viyl,vyk->vikl", result, middle_matrix(kernel_mid, result.shape[2]), precision=PRECISE
    )
    return along_last(result, kernel_last)


def backward(padded, kernel_first, kernel_mid, kernel_last):
    plane_count = padded.shape[1] - (kernel_first.shape[-1] - 1)
    result = jnp.einsum(
        "vsyl,vsi->viyl", padded, band_matrix(kernel_first, plane_count), precision=PRECISE
    )
    result = jnp.einsum(
        "viyl,vyk->vikl", result, middle_matrix(kernel_mid, result.shape[2]), precision=PRECISE
    )
    return along_last(result, kernel_last)


def edge_weights(kernel, positions, length):
    rim_width = (kernel.shape[-1] - 1) // 2
    source = positions[:, None] + jnp.arange(kernel.shape[-1])[None, :] - rim_width
    inside = (source >= 0) & (source < length)
    return jnp.sum(jnp.where(inside[None], kernel[:, None, :], 0.0), axis=-1)


def log_correction(padded, kernel_first, kernel_mid, kernel_last, first_start, first_total):
    back_sum = backward(padded, kernel_first, kernel_mid, kernel_last)
    plane_count, line_count, column_count = back_sum.shape[1:]
    first_weights = edge_weights(kernel_first, first_start + jnp.arange(plane_count), first_total)
    mid_weights = edge_weights(kernel_mid, jnp.arange(line_count), line_count)
    last_weights = edge_weights(kernel_last, jnp.arange(column_count), column_count)
    scale_sum = (
        first_weights[:, :, None, None]
        * mid_weights[:, None, :, None]
        * last_weights[:, None, None, :]
    )
    return jnp.log(back_sum / scale_sum)


def select_views(covered, view_ids):
    picked = (jnp.arange(covered.shape[-1])[None, :] == view_ids[:, None]).astype(jnp.float32)
    return jnp.einsum("vw,xw->vx", picked, covered, precision=PRECISE)


def slab_logs(padded_estimate, view_data, kernel, flipped, weights, first_start, first_total):
    blurred = forward(padded_estimate, kernel[:, 0], kernel[:, 1], kernel[:, 2])
    quotient = view_data / blurred
    rim_width = (kernel.shape[-1] - 1) // 2
    quotient_padded = extended(quotient, (("owner", 1),), rim_width)
    log_terms = log_correction(
        quotient_padded, flipped[:, 0], flipped[:, 1], flipped[:, 2], first_start, first_total
    )
    return jnp.sum(weights[:, None, None, :] * log_terms, axis=0)


def local(estimate, axial_views, lateral_views, psf_axial, psf_lateral, coverage):
    plane_count, line_count, column_count = estimate.shape
    owners = lax.axis_size("owner")
    slab_index = lax.axis_index("owner")
    view_index = lax.axis_index("view")
    slab_width = column_count // owners
    rim_width = (psf_axial.shape[-1] - 1) // 2
    kernel_axial = psf_axial / jnp.sum(psf_axial, axis=-1, keepdims=True)
    kernel_lateral = psf_lateral / jnp.sum(psf_lateral, axis=-1, keepdims=True)
    flipped_axial = kernel_axial[..., ::-1]
    flipped_lateral = kernel_lateral[..., ::-1]
    block_width = column_count // coverage.shape[1]
    covered = jnp.repeat(coverage[0].astype(jnp.float32), block_width, axis=0)
    cover_count = jnp.sum(covered, axis=-1)
    axial_count = psf_axial.shape[0]
    lateral_count = psf_lateral.shape[0]
    weights_axial = select_views(covered, view_index * axial_count + jnp.arange(axial_count))
    weights_lateral = select_views(
        covered, VA + view_index * lateral_count + jnp.arange(lateral_count)
    )
    plane_start = slab_index * plane_count
    plane_total = plane_count * owners
    moved_views = lateral_views.reshape(
        lateral_count, slab_width, line_count, owners, plane_count
    ).transpose(0, 4, 2, 3, 1)
    lateral_slabs = lax.all_to_all(moved_views, "owner", split_axis=3, concat_axis=4, tiled=True)
    lateral_slabs = lateral_slabs.reshape(lateral_count, plane_count, line_count, column_count)
    view_all = jnp.concatenate([axial_views, lateral_slabs], axis=0)
    kernel_all = jnp.concatenate([kernel_axial, kernel_lateral], axis=0)
    flipped_all = jnp.concatenate([flipped_axial, flipped_lateral], axis=0)
    weights_all = jnp.concatenate([weights_axial, weights_lateral], axis=0)
    for iteration in range(ITERS):
        padded_estimate = extended(estimate, (("owner", 0),), rim_width)
        log_total = slab_logs(
            padded_estimate,
            view_all,
            kernel_all,
            flipped_all,
            weights_all,
            plane_start,
            plane_total,
        )
        log_total = lax.psum(log_total, "view")
        estimate = estimate * jnp.exp(log_total / cover_count[None, None, :])
    return estimate


F32 = jnp.float32
BF16 = jnp.bfloat16
MESH = pl.DeviceIdType.MESH
CHUNKS = 4
PARTS = 2


def split_bf16(values):
    high = values.astype(BF16)
    low = (values - high.astype(F32)).astype(BF16)
    return high, low


def dot32(left, right):
    return jnp.dot(left, right, preferred_element_type=F32)


def joint_kernel(
    owners,
    views,
    planes,
    lines,
    columns,
    psf_ref,
    estimate_ref,
    axial_ref,
    lateral_ref,
    cover_ref,
    out_ref,
    window,
    observed,
    lateral,
    turned,
    mid,
    quot,
    logs,
    pair_sum,
    peer_sum,
    cover,
    x_fwd,
    x_back,
    y_fwd,
    y_back,
    z_fwd,
    z_back,
    log_xy,
    log_z,
    weight,
    cover_sem,
    axial_sem,
    lateral_sem,
    edge_sem,
    share_sem,
    pair_sem,
    peer_sem,
    local_sem,
):
    taps = psf_ref.shape[0] // 3
    rim = (taps - 1) // 2
    groups = owners // 2
    span = 2 * planes
    block = planes // views
    chunk_lines = lines // CHUNKS
    slab = columns // owners

    me = lax.axis_index("owner")
    view = lax.axis_index("view")
    group = me // 2
    side = lax.rem(me, 2)
    core = lax.rem(view, 2)
    row = view // 2
    takes_lateral = lax.rem(side + core, 2)
    has_below = group > 0
    has_above = group < groups - 1

    def device(side_, view_):
        return (2 * group + side_, view_)

    sibling = device(side, 2 * row + 1 - core)

    barrier = pltpu.get_barrier_semaphore()
    for step in range(1, owners):
        pl.semaphore_signal(
            barrier, inc=1, device_id=(lax.rem(me + step, owners), view), device_id_type=MESH
        )
    for side_ in (side, 1 - side):
        for step in range(1, views):
            pl.semaphore_signal(
                barrier,
                inc=1,
                device_id=device(side_, lax.rem(view + step, views)),
                device_id_type=MESH,
            )
    mine = window.at[pl.ds(2 + 2 * side, 2)]
    estimate_in = pltpu.make_async_copy(estimate_ref, mine, local_sem.at[0])
    lateral_in = pltpu.make_async_copy(lateral_ref, lateral, local_sem.at[1])
    window_planes = window.reshape(2 * span, lines, columns)
    estimate_in.start()
    lateral_in.start()
    cover[pl.ds(side, 1)] = cover_ref[...][None]

    def clear(slab_):
        def plane(z, carry):
            zero = jnp.zeros((lines, columns), F32)
            window_planes[slab_ * planes + z] = zero
            for iteration in range(ITERS):
                quot[iteration * 2 * span + slab_ * planes + z] = zero
            return carry

        lax.fori_loop(0, planes, plane, 0)

    pl.when(group == 0)(lambda: clear(0))
    pl.when(group == groups - 1)(lambda: clear(3))

    estimate_in.wait()
    pl.semaphore_wait(barrier, owners - 1 + 2 * (views - 1))

    def remote(src, dst, sems, index, target):
        return pltpu.make_async_remote_copy(
            src_ref=src,
            dst_ref=dst,
            send_sem=sems.at[0, index],
            recv_sem=sems.at[1, index],
            device_id=target,
            device_id_type=MESH,
        )

    def chunk(c):
        return pl.ds(pl.multiple_of(c * chunk_lines, chunk_lines), chunk_lines)

    def part(first, count, core_, c):
        return window.at[pl.ds(first, count), core_, :, chunk(c)]

    def copy_part(stage, c, slot, src, dst, count, target):
        return pltpu.make_async_remote_copy(
            src_ref=part(src, count, core, c),
            dst_ref=part(dst, count, core, c),
            send_sem=share_sem.at[0, stage, c, slot],
            recv_sem=share_sem.at[1, stage, c, slot],
            device_id=target,
            device_id_type=MESH,
        )

    own = 2 + 2 * side + row
    own_side = 2 + 2 * side
    other_side = 4 - 2 * side
    row_peer = device(side, 2 * (1 - row) + core)
    side_peer = device(1 - side, view)
    far_peer = device(1 - side, 2 * (1 - row) + core)
    other = 1 - core
    yes = group >= 0

    def up_copy(more):
        return (has_above & more, 3, 4, 0, 2, (me + 2, view))

    def down_copy(more):
        return (has_below & more, 4, 2, 6, 2, (me - 2, view))

    def plan(first, more):
        x_arrival = (more, 0, 2 + 2 * (1 - side) + row, 1, core)
        y_arrival = (yes, 1, 2 + 2 * side + 1 - row, 1, core)
        far_arrival = (more, 2, 2 + 2 * (1 - side) + 1 - row, 1, core)
        if first:
            near = (has_above & (side == 1), 3, 4, 0, 2, (me + 2, view))
            near_down = (has_below & (side == 0), 4, 2, 6, 2, (me - 2, view))
            at_once = [(yes, 0, own, own, 1, side_peer), near, near_down]
            across = x_arrival[2]
            group_steps = [
                ([x_arrival], [(yes, 2, across, across, 1, row_peer)]),
                (
                    [far_arrival],
                    [
                        (yes, 5, other_side, other_side, 2, sibling),
                        (has_above & (side == 0), 3, 4, 0, 2, (me + 2, view)),
                        (has_below & (side == 1), 4, 2, 6, 2, (me - 2, view)),
                    ],
                ),
            ]
            rest = [(yes, 5, other_side, 2, other)]
        else:
            at_once = [
                (more, 0, own, own, 1, side_peer),
                (yes, 1, own, own, 1, row_peer),
                (more, 2, own, own, 1, far_peer),
            ]
            group_steps = [
                (
                    [y_arrival, x_arrival, far_arrival],
                    [
                        up_copy(more),
                        down_copy(more),
                        (more, 5, 2, 2, 4, sibling),
                        (jnp.logical_not(more), 8, own_side, own_side, 2, sibling),
                    ],
                )
            ]
            rest = [(more, 5, 2, 4, other), (jnp.logical_not(more), 8, own_side, 2, other)]
        beside_steps = [
            ([(has_below & more, 3, 0, 2, core)], [(has_below & more, 6, 0, 0, 2, sibling)]),
            ([(has_above & more, 4, 6, 2, core)], [(has_above & more, 7, 6, 6, 2, sibling)]),
        ]
        rest = rest + [(has_below & more, 6, 0, 2, other), (has_above & more, 7, 6, 2, other)]
        return at_once, group_steps, beside_steps, rest

    def start_all(stage, c, sends):
        for condition, *where in sends:
            pl.when(condition)(copy_part(stage, c, *where).start)

    def await_all(stage, c, arrivals):
        for condition, slot, first, count, core_ in arrivals:
            there = part(first, count, core_, c)
            made = pltpu.make_async_remote_copy(
                src_ref=there,
                dst_ref=there,
                send_sem=share_sem.at[0, stage, c, slot],
                recv_sem=share_sem.at[1, stage, c, slot],
                device_id=sibling,
                device_id_type=MESH,
            )
            pl.when(condition)(made.wait_recv)

    def send_on(stage, c, steps_):
        for arrivals, onward in steps_:
            await_all(stage, c, arrivals)
            start_all(stage, c, onward)

    def spread_done(stage, c, made):
        at_once, group_steps, beside_steps, rest = made
        await_all(stage, c, rest)
        onwards = [onward for _, onward in group_steps + beside_steps]
        for condition, *where in sum(onwards, at_once):
            pl.when(condition)(copy_part(stage, c, *where).wait_send)

    def toeplitz(axis, shape, offset, flip):
        first = lax.broadcasted_iota(jnp.int32, shape, 0)
        second = lax.broadcasted_iota(jnp.int32, shape, 1)
        place = (second - first if flip else first - second) + (rim + offset)

        def add(t, total):
            return jnp.where(place == t, psf_ref[axis * taps + t], total)

        return lax.fori_loop(0, taps, add, jnp.zeros(shape, F32))

    def store_right(ref, matrix):
        high, low = split_bf16(matrix)
        top = jnp.concatenate([high, low], axis=1)
        ref[...] = jnp.concatenate([top, top], axis=0)

    def store_left(ref, matrix):
        high, low = split_bf16(matrix)
        ref[...] = jnp.concatenate(
            [jnp.concatenate([high, high], axis=1), jnp.concatenate([low, low], axis=1)], axis=0
        )

    def prepare():
        store_right(x_fwd, toeplitz(2, (columns, columns), 0, False))
        back_x = toeplitz(2, (columns, columns), 0, True)
        store_right(x_back, back_x)
        store_left(y_fwd, toeplitz(1, (lines, lines), 0, True))
        back_y = toeplitz(1, (lines, lines), 0, False)
        store_left(y_back, back_y)
        store_left(z_fwd, toeplitz(0, (span, 2 * span), -planes, True))
        back_z = toeplitz(0, (span, 2 * span), planes, False)
        store_left(z_back, back_z)
        log_xy[...] = jnp.log(jnp.sum(back_y, axis=1, keepdims=True)) + jnp.log(
            jnp.sum(back_x, axis=0, keepdims=True)
        )
        plane = lax.broadcasted_iota(jnp.int32, (span, 2 * span), 1) + (group * span - planes)
        inside = (plane >= 0) & (plane < owners * planes)
        sums = jnp.sum(jnp.where(inside, back_z, 0.0), axis=1, keepdims=True)
        log_z[...] = jnp.broadcast_to(jnp.log(sums), (span, columns))

    cover_copy = remote(cover.at[side], cover.at[side], cover_sem, 0, device(1 - side, view))
    cover_copy.start()
    axial_target = device(core, view)
    axial_mine = pl.ds(side * planes, planes)
    depth = planes // PARTS
    axial_in = pltpu.make_async_copy(axial_ref, observed.at[axial_mine], local_sem.at[2])

    def axial_copy(q):
        return remote(
            axial_ref.at[pl.ds(q * depth, depth)],
            observed.at[pl.ds(side * planes + q * depth, depth)],
            axial_sem,
            q,
            axial_target,
        )

    def axial_arrival(q):
        theirs = observed.at[pl.ds((1 - side) * planes + q * depth, depth)]
        return remote(theirs, theirs, axial_sem, q, sibling)

    def lateral_copy(to, q, half):
        plane = half * planes + q * depth
        return pltpu.make_async_remote_copy(
            src_ref=turned.at[pl.ds(to * span + plane, depth)],
            dst_ref=observed.at[pl.ds(plane, depth), pl.ds(me * slab, slab), :],
            send_sem=lateral_sem.at[0, to, q, half],
            recv_sem=lateral_sem.at[1, me, q, half],
            device_id=(2 * to + 1 - core, view),
            device_id_type=MESH,
        )

    def lateral_arrival(source, q, half):
        there = observed.at[pl.ds(half * planes + q * depth, depth), pl.ds(source * slab, slab), :]
        return pltpu.make_async_remote_copy(
            src_ref=there,
            dst_ref=there,
            send_sem=lateral_sem.at[0, 0, q, half],
            recv_sem=lateral_sem.at[1, source, q, half],
            device_id=sibling,
            device_id_type=MESH,
        )

    def turn():
        lateral_in.wait()
        for x in range(slab):
            turned[:, x, :] = lateral[x].T

    def each_lateral(act):
        def one(i, carry):
            q, to = i // groups, lax.rem(i, groups)

            @pl.when((takes_lateral == 0) | (to != group))
            def _():
                act(lateral_copy(to, q, 0))
                act(lateral_copy(to, q, 1))

            return carry

        lax.fori_loop(0, PARTS * groups, one, 0)

    def start_axial():
        @pl.when(takes_lateral == 1)
        def _():
            for q in range(PARTS):
                axial_copy(q).start()

        @pl.when(takes_lateral == 0)
        def _():
            axial_in.start()

    def start_lateral():
        each_lateral(lambda copy: copy.start())

        @pl.when(takes_lateral == 1)
        def _():
            observed[:, pl.ds(pl.multiple_of(me * slab, slab), slab), :] = turned[
                pl.ds(group * span, span)
            ]

    def views_arrived(q):
        @pl.when(takes_lateral == 1)
        def _():
            def from_owner(step, carry):
                source = lax.rem(me + step, owners)
                lateral_arrival(source, q, 0).wait_recv()
                lateral_arrival(source, q, 1).wait_recv()
                return carry

            lax.fori_loop(1, owners, from_owner, 0)

            def flip(k, carry):
                z = q * depth + k
                observed[z] = observed[z].T
                observed[planes + z] = observed[planes + z].T
                return carry

            lax.fori_loop(0, depth, flip, 0)

        @pl.when(takes_lateral == 0)
        def _():
            pl.when(q == 0)(axial_in.wait)
            axial_arrival(q).wait_recv()

    def views_sent():
        each_lateral(lambda copy: copy.wait_send())

        @pl.when(takes_lateral == 1)
        def _():
            for q in range(PARTS):
                axial_copy(q).wait_send()

    def along_z(source, matrix, y, first_row=0):
        both = jnp.concatenate(
            [
                source[pl.ds(first_row + y, 2 * span, stride=lines), :],
                source[pl.ds(first_row + y + 1, 2 * span, stride=lines), :],
            ],
            axis=1,
        )
        high, low = split_bf16(both)
        result = dot32(matrix[...], jnp.concatenate([high, low], axis=0))
        result = result[:span] + result[span:]
        return result[:, :columns], result[:, columns:]

    def along_x(planes_two, matrix):
        high, low = split_bf16(planes_two)
        result = dot32(jnp.concatenate([high, low], axis=1), matrix[...])
        return result[:, :columns] + result[:, columns:]

    def along_y(planes_two, matrix):
        high, low = split_bf16(planes_two)
        result = dot32(matrix[...], jnp.concatenate([high, low], axis=0))
        return result[:lines] + result[lines:]

    def side_by_side(stacked):
        return jnp.concatenate([stacked[:lines], stacked[lines:]], axis=1)

    def stacked_up(beside):
        return jnp.concatenate([beside[:, :columns], beside[:, columns:]], axis=0)

    window_lines = window.reshape(2 * span * lines, columns)
    mid_lines = mid.reshape(span * lines, columns)
    logs_lines = logs.reshape(span * lines, columns)
    quot_lines = quot.reshape(ITERS * 2 * span * lines, columns)

    def forward_z(c):
        def lines_of(i, carry):
            for step in range(4):
                y = c * chunk_lines + i * 8 + 2 * step
                one, two = along_z(window_lines, z_fwd, y)
                mid_lines[pl.ds(y, span, stride=lines), :] = one
                mid_lines[pl.ds(y + 1, span, stride=lines), :] = two
            return carry

        lax.fori_loop(0, chunk_lines // 8, lines_of, 0)

    def plane_pair(iteration, z):
        blurred = along_x(mid[pl.ds(z, 2)].reshape(2 * lines, columns), x_fwd)
        blurred = along_y(side_by_side(blurred), y_fwd)
        seen = jnp.concatenate([observed[z], observed[z + 1]], axis=1)
        back = along_y(seen / blurred, y_back)
        back = along_x(stacked_up(back), x_back)
        quot[pl.ds(iteration * 2 * span + planes + z, 2)] = back.reshape(2, lines, columns)

    early = CHUNKS // 2
    steps = planes // 2

    def edge(iteration, index, up, plane, count, lines_at):
        start_plane = (2 * planes if up else planes) + plane
        end_plane = (0 if up else 3 * planes) + plane
        way = 1 if up else 0
        return pltpu.make_async_remote_copy(
            src_ref=quot.at[pl.ds(iteration * 2 * span + start_plane, count), lines_at],
            dst_ref=quot.at[pl.ds(iteration * 2 * span + end_plane, count), lines_at],
            send_sem=edge_sem.at[0, iteration, way, index],
            recv_sem=edge_sem.at[1, iteration, way, index],
            device_id=(me + 2 if up else me - 2, view),
            device_id_type=MESH,
        )

    def early_edge(iteration, s, up):
        return edge(iteration, s, up, 2 * s, 2, pl.ds(0, early * chunk_lines))

    def late_edge(iteration, c, up):
        return edge(iteration, steps + c - early, up, 0, planes, chunk(c))

    def middle(iteration):
        def step(s, carry):
            plane_pair(iteration, 2 * s)
            plane_pair(iteration, planes + 2 * s)
            pl.when(has_below)(early_edge(iteration, s, False).start)
            pl.when(has_above)(early_edge(iteration, s, True).start)
            return carry

        def part_of(q, carry):
            pl.when(iteration == 0)(lambda: views_arrived(q))
            return lax.fori_loop(q * (steps // PARTS), (q + 1) * (steps // PARTS), step, carry)

        lax.fori_loop(0, PARTS, part_of, 0)
        for c in range(early, CHUNKS):
            pl.when(has_below)(late_edge(iteration, c, False).start)
            pl.when(has_above)(late_edge(iteration, c, True).start)

    def run(body):
        lax.fori_loop(0, steps, body, 0)

    def edges_arrived(iteration, c):
        def finish(s, carry):
            pl.when(has_above)(early_edge(iteration, s, False).wait_recv)
            pl.when(has_below)(early_edge(iteration, s, True).wait_recv)
            return carry

        pl.when(c == 0)(lambda: run(finish))
        pl.when((c >= early) & has_above)(lambda: late_edge(iteration, c, False).wait_recv())
        pl.when((c >= early) & has_below)(lambda: late_edge(iteration, c, True).wait_recv())

    def edges_sent(iteration):
        def finish(s, carry):
            pl.when(has_below)(early_edge(iteration, s, False).wait_send)
            pl.when(has_above)(early_edge(iteration, s, True).wait_send)
            return carry

        lax.fori_loop(0, steps, finish, 0)
        for c in range(early, CHUNKS):
            pl.when(has_below)(late_edge(iteration, c, False).wait_send)
            pl.when(has_above)(late_edge(iteration, c, True).wait_send)

    def backward_z(iteration, c):
        first_row = iteration * 2 * span * lines

        def lines_of(i, carry):
            for part_ in range(4):
                y = c * chunk_lines + i * 8 + 2 * part_
                for step, back in enumerate(along_z(quot_lines, z_back, y, first_row)):
                    value = jnp.log(back) - (log_z[...] + log_xy[pl.ds(y + step, 1), :])
                    logs_lines[pl.ds(y + step, span, stride=lines), :] = weight[...] * value
            return carry

        lax.fori_loop(0, chunk_lines // 8, lines_of, 0)

    kinds = [(1, 1), (1, 0), (0, 1)]

    def to_sibling(iteration, c):
        return pltpu.make_async_remote_copy(
            src_ref=logs.at[:, other, :, chunk(c)],
            dst_ref=pair_sum.at[iteration, :, :, chunk(c)],
            send_sem=pair_sem.at[0, iteration, c],
            recv_sem=pair_sem.at[1, iteration, c],
            device_id=sibling,
            device_id_type=MESH,
        )

    def to_peer(iteration, c, k):
        side_ = lax.rem(side + kinds[k][0], 2)
        row_ = lax.rem(row + kinds[k][1], 2)
        return pltpu.make_async_remote_copy(
            src_ref=logs.at[2 * side_ + row_, core, :, chunk(c)],
            dst_ref=peer_sum.at[iteration, k, :, chunk(c)],
            send_sem=peer_sem.at[0, iteration, c, k],
            recv_sem=peer_sem.at[1, iteration, c, k],
            device_id=device(side_, 2 * row_ + core),
            device_id_type=MESH,
        )

    def correct(iteration, c):
        edges_arrived(iteration, c)
        backward_z(iteration, c)
        to_sibling(iteration, c).start()

    def reduce_pair(iteration, c):
        to_sibling(iteration, c).wait_recv()
        for k in range(4):
            logs[k, core, :, chunk(c)] = (
                logs[k, core, :, chunk(c)] + pair_sum[iteration, k, :, chunk(c)]
            )
        for k in range(3):
            to_peer(iteration, c, k).start()

    def update(iteration, made, c):
        for k in (1, 2, 0):
            to_peer(iteration, c, k).wait_recv()
        count = jnp.sum(cover_ref[...], axis=0, keepdims=True)
        total = logs[2 * side + row, core, :, chunk(c)]
        for k in range(3):
            total = total + peer_sum[iteration, k, :, chunk(c)]
        factor = jnp.exp(total / count[None])
        window[own, core, :, chunk(c)] = window[own, core, :, chunk(c)] * factor
        start_all(iteration + 1, c, made[0])

    def sums_sent(iteration, c):
        to_sibling(iteration, c).wait_send()
        for k in range(3):
            to_peer(iteration, c, k).wait_send()

    def pipeline(stages):
        def turn_of(t, carry):
            for lag, stage in enumerate(stages):
                c = t - lag
                pl.when((c >= 0) & (c < CHUNKS))(functools.partial(stage, c))
            return carry

        lax.fori_loop(0, CHUNKS + len(stages) - 1, turn_of, 0)

    def initial():
        made = plan(True, yes)

        def begin(c, carry):
            start_all(0, c, made[0])
            return carry

        lax.fori_loop(0, CHUNKS, begin, 0)
        start_axial()
        turn()
        start_lateral()

        def forward_group(c, carry):
            send_on(0, c, made[1])
            return carry

        lax.fori_loop(0, CHUNKS, forward_group, 0)
        prepare()

        def settle(c):
            spread_done(0, c, made)
            forward_z(c)

        pipeline([lambda c: send_on(0, c, made[2]), settle])

    def one_pass(iteration, carry):
        more = iteration < ITERS - 1
        made = plan(False, more)
        stage = iteration + 1
        middle(iteration)

        def settle(c):
            spread_done(stage, c, made)

            @pl.when(more)
            def _():
                forward_z(c)

            @pl.when(iteration == ITERS - 1)
            def _():
                out_ref[:, :, :, chunk(c)] = window[pl.ds(own_side, 2), :, :, chunk(c)]

        pipeline(
            [
                lambda c: correct(iteration, c),
                lambda c: reduce_pair(iteration, c),
                lambda c: update(iteration, made, c),
                lambda c: send_on(stage, c, made[1]),
                lambda c: send_on(stage, c, made[2]),
                settle,
            ]
        )
        edges_sent(iteration)

        def finish(c, carry_):
            sums_sent(iteration, c)
            return carry_

        return lax.fori_loop(0, CHUNKS, finish, carry)

    initial()
    cover_copy.wait_send()
    remote(cover.at[1 - side], cover.at[1 - side], cover_sem, 0, sibling).wait_recv()
    which = takes_lateral * views + view
    weight[:planes, :] = jnp.broadcast_to(cover[0, pl.ds(which, 1), :], (planes, columns))
    weight[planes:, :] = jnp.broadcast_to(cover[1, pl.ds(which, 1), :], (planes, columns))
    lax.fori_loop(0, ITERS, one_pass, 0)
    views_sent()


def joint(estimate, axial_views, lateral_views, psf_axial, psf_lateral, coverage):
    planes, lines, columns = estimate.shape
    owners = lax.axis_size("owner")
    views = lax.axis_size("view")
    slab = columns // owners
    span = 2 * planes
    depth = owners * planes
    block = planes // views
    takes_lateral = (lax.axis_index("owner") + lax.axis_index("view")) % 2 == 1
    psf = jnp.where(takes_lateral, psf_lateral[0], psf_axial[0])
    psf = psf / jnp.sum(psf, axis=-1, keepdims=True)
    cover = jnp.repeat(coverage[0].astype(F32).T, columns // coverage.shape[1], axis=1)
    vmem = pl.BlockSpec(memory_space=pltpu.VMEM)
    hbm = pl.BlockSpec(memory_space=pl.ANY)
    dma = pltpu.SemaphoreType.DMA
    result = pl.pallas_call(
        functools.partial(joint_kernel, owners, views, planes, lines, columns),
        out_shape=jax.ShapeDtypeStruct((2, 2, block, lines, columns), F32),
        in_specs=[pl.BlockSpec(memory_space=pltpu.SMEM)] + [hbm] * 3 + [vmem],
        out_specs=vmem,
        scratch_shapes=[
            pltpu.VMEM((8, 2, block, lines, columns), F32),
            pltpu.VMEM((span, lines, columns), F32),
            pltpu.VMEM((slab, lines, depth), F32),
            pltpu.VMEM((depth, slab, lines), F32),
            pltpu.VMEM((span, lines, columns), F32),
            pltpu.VMEM((ITERS * 2 * span, lines, columns), F32),
            pltpu.VMEM((4, 2, block, lines, columns), F32),
            pltpu.VMEM((ITERS, 4, block, lines, columns), F32),
            pltpu.VMEM((ITERS, 3, block, lines, columns), F32),
            pltpu.VMEM((2,) + cover.shape, F32),
            pltpu.VMEM((2 * columns, 2 * columns), BF16),
            pltpu.VMEM((2 * columns, 2 * columns), BF16),
            pltpu.VMEM((2 * lines, 2 * lines), BF16),
            pltpu.VMEM((2 * lines, 2 * lines), BF16),
            pltpu.VMEM((2 * span, 4 * span), BF16),
            pltpu.VMEM((2 * span, 4 * span), BF16),
            pltpu.VMEM((lines, columns), F32),
            pltpu.VMEM((span, columns), F32),
            pltpu.VMEM((span, columns), F32),
            dma((2, 1)),
            dma((2, PARTS)),
            dma((2, owners, PARTS, 2)),
            dma((2, ITERS, 2, planes // 2 + CHUNKS)),
            dma((2, ITERS + 1, CHUNKS, 9)),
            dma((2, ITERS, CHUNKS)),
            dma((2, ITERS, CHUNKS, 3)),
            dma((3,)),
        ],
        compiler_params=pltpu.CompilerParams(
            collective_id=0, has_side_effects=True, vmem_limit_bytes=48 * 1024 * 1024
        ),
    )(
        psf.reshape(-1),
        estimate.reshape(2, 2, block, lines, columns),
        axial_views[0],
        lateral_views[0],
        cover,
    )
    return result.reshape(planes, lines, columns)


def chosen(estimate, axial_views, lateral_views, psf_axial, psf_lateral, coverage):
    planes, lines, columns = estimate.shape
    owners = lax.axis_size("owner")
    views = lax.axis_size("view")
    rim = (psf_axial.shape[-1] - 1) // 2
    fits = (
        lines == columns
        and columns % 128 == 0
        and planes * lines * columns * 4 <= 1024 * 1024
        and planes * owners == columns
        and axial_views.shape[0] == 1
        and lateral_views.shape[0] == 1
        and views == 4
        and owners % 2 == 0
        and planes % views == 0
        and planes % (2 * PARTS) == 0
        and rim <= planes
        and columns // owners % 8 == 0
        and lines % (8 * CHUNKS) == 0
    )
    body = joint if fits else local
    return body(estimate, axial_views, lateral_views, psf_axial, psf_lateral, coverage)


def solution(mesh):
    in_specs = (
        P("owner", None, None),
        P("view", "owner", None, None),
        P("view", "owner", None, None),
        P("view", None, None),
        P("view", None, None),
        P("owner", None, None),
    )
    out_specs = P("owner", None, None)
    return jax.shard_map(chosen, mesh=mesh, in_specs=in_specs, out_specs=out_specs, check_vma=False)
```
